32 devices in a mesh: ctx: 2 (over y), exp: 16 (over z, x, core).
Axes of the slice: x: 2, y: 2, z: 4, core: 2. Of those that a mesh axis runs over, the one named last changes fastest.
Arguments:
- block_input: bfloat16 [16, 1024, 2560], P('exp', 'ctx'), may hold values from -6 to 6
- attn_gain: float32 [2560], replicated, may hold values from 0.25 to 1.75
- query_weight: bfloat16 [2560, 2560], P(('ctx', 'exp')), may hold values from -0.125 to 0.125
- key_matrix: bfloat16 [2560, 512], P(('ctx', 'exp')), may hold values from -0.125 to 0.125
- value_matrix: bfloat16 [2560, 512], P(('ctx', 'exp')), may hold values from -0.125 to 0.125
- output_weight: bfloat16 [2560, 2560], P(('ctx', 'exp')), may hold values from -0.5 to 0.5
- ffn_gain: float32 [2560], replicated, may hold values from 0.25 to 1.75
- shared_gate: bfloat16 [2560, 3072], P(('ctx', 'exp')), may hold values from -0.125 to 0.125
- shared_up: bfloat16 [2560, 3072], P(('ctx', 'exp')), may hold values from -0.125 to 0.125
- shared_down: bfloat16 [3072, 2560], P(('ctx', 'exp')), may hold values from -0.21875 to 0.21875
- expert_gate: bfloat16 [16, 2560, 1536], P('exp', 'ctx'), may hold values from -0.125 to 0.125
- expert_up: bfloat16 [16, 2560, 1536], P('exp', 'ctx'), may hold values from -0.125 to 0.125
- expert_down: bfloat16 [16, 1536, 2560], P('exp', None, 'ctx'), may hold values from -0.625 to 0.625
- routes: int32 [16, 1024, 6], P('exp', 'ctx'), may hold values from 0 to 15, all different within a row; in each aligned block of 512 rows (0 to 511, 512 to 1023, ..., all dimensions but the last counted through in order) at most 256 rows name the same one
- route_weights: float32 [16, 1024, 6], P('exp', 'ctx'), may hold values from 0.05 to 0.3
- cotangent: bfloat16 [16, 1024, 2560], P('exp', 'ctx'), may hold values from -6 to 6
Outputs:
- block_output: bfloat16 [16, 1024, 2560], P('exp', 'ctx')
- input_grad: float32 [16, 1024, 2560], P('exp', 'ctx')
- attn_gain_grad: float32 [2560], P(('ctx', 'exp'))
- query_grad: float32 [2560, 2560], P(('ctx', 'exp'))
- key_grad: float32 [2560, 512], P(('ctx', 'exp'))
- value_grad: float32 [2560, 512], P(('ctx', 'exp'))
- output_grad: float32 [2560, 2560], P(None, ('ctx', 'exp'))
- ffn_gain_grad: float32 [2560], P(('ctx', 'exp'))
- shared_gate_grad: float32 [2560, 3072], P(('ctx', 'exp'))
- shared_up_grad: float32 [2560, 3072], P(('ctx', 'exp'))
- shared_down_grad: float32 [3072, 2560], P(('ctx', 'exp'))
- expert_gate_grad: float32 [16, 2560, 1536], P('exp', 'ctx')
- expert_up_grad: float32 [16, 2560, 1536], P('exp', 'ctx')
- expert_down_grad: float32 [16, 1536, 2560], P('exp', None, 'ctx')
The draws below stay inside these ranges and needn't reach their ends.
Inputs may be any that keep to these rules, and one draw needn't show every extreme that they name: `routes`: A token names 6 different experts. Within the rows of one device each expert is named by at most 256 rows, and by exactly 256 in some devices' rows.
All inputs are finite; a program needn't handle non-finite values.
Results may differ from the reference program's by a relative error of at most 0.025.
Values may be sent and summed in bfloat16 or wider, within the bound.
No kernel may reach another device: no remote copies, remote signals or barrier semaphores. Data moves between devices by JAX's collectives and lax.ppermute only.
A program may use at most 576 MiB of HBM per device.

```python
import math
import jax
import jax.numpy as jnp
import numpy as np
from jax import lax

MODEL_WIDTH = 2560
QUERY_HEADS = 20
KEY_VALUE_HEADS = 4
HEAD_SIZE = 128
FF = 1536
SH = 3072
TOP = 6
SEQUENCE_TOKENS = 1024
EXPERTS = 16
SEQS = 16
TOK_DEV = 512
CAP = 256


def raised(values, stream_key, source, target, shards_of, factor):
    def block_of(axis_at):
        return (jnp.arange(values.shape[axis_at]) // (values.shape[axis_at] // shards_of)).reshape((-1,) + (1,) * (values.ndim - 1 - axis_at))

    first = jax.random.permutation(stream_key, shards_of)[block_of(target)]
    second = (block_of(target) + shards_of // 2) % shards_of
    return jnp.where((block_of(source) == first) | (block_of(source) == second), factor * values, values)


def level_of(key, shape, split, smallest, high):
    level, own = 1.0, jax.random.fold_in(key, 6)
    for position, blocks in split:
        heights = jnp.exp(jax.random.uniform(jax.random.fold_in(own, position), (blocks,), jnp.float32, smallest / len(split), high / len(split)))
        level = level * jnp.repeat(heights, shape[position] // blocks).reshape([-1 if axis == position else 1 for axis in range(len(shape))])
    return level


def routed_block(key, own, number, rows, number_of, top, most, lean):
    ranking = jax.random.permutation(key, number_of)
    packed, ordinary = portions_of(number_of, rows * top, most, lean, True), portions_of(number_of, rows * top, most, lean, False)
    places = jnp.arange(number_of)

    def named(lengths, turn):
        used = int((lengths > 0).sum())
        fixed = max(1, used // 4)
        passed = fixed + (places - fixed + turn * (used - fixed)) % max(1, number_of - fixed)
        return jnp.zeros((number_of,), jnp.int32).at[ranking[jnp.where(places < fixed, places, passed)]].set(jnp.asarray(lengths, jnp.int32))

    lengths = jnp.where(number % 4 == 0, named(packed, number // 4), named(ordinary, number - number // 4 - 1))
    mixed = jax.random.permutation(jax.random.fold_in(own, 3), number_of)
    source_of, taker = mixed[0:number_of // 2 * 2:2], mixed[1:number_of // 2 * 2:2]
    slack = jnp.minimum(lengths[source_of] - 1, most - lengths[taker]) // 2
    slack = jnp.where((source_of == ranking[0]) | (taker == ranking[0]) | (lengths[taker] == 0), 0, jnp.maximum(slack, 0))
    passed = jax.random.randint(jax.random.fold_in(own, 4), (number_of // 2,), 0, 1 << 20) % (slack + 1)
    lengths = lengths.at[source_of].add(-passed).at[taker].add(passed)
    labels = jnp.searchsorted(jnp.cumsum(lengths), jnp.arange(rows * top), side="right").astype(jnp.int32)
    grid = labels.reshape(top, rows).T
    grid = grid[jax.random.permutation(jax.random.fold_in(own, 1), rows)]
    turn = jax.random.randint(jax.random.fold_in(own, 2), (rows, 1), 0, top)
    return jnp.take_along_axis(grid, (jnp.arange(top)[None, :] + turn) % top, axis=1)


def portions_of(count, total, most, slope, full):
    weights = [(1 << 20) // math.isqrt(rank ** slope) + 1 for rank in range(1, count + 1)]
    largest = most if full else min(most, max(-(-total // count), total * weights[0] // sum(weights)))
    least = 1 if total - largest >= count - 1 else 0
    holding, rest = [largest] + [least] * (count - 1), total - largest - least * (count - 1)
    while rest > 0:
        candidates = [i for i in range(1, count) if holding[i] < largest] or [i for i in range(1, count) if holding[i] < most]
        mass, budget = sum([weights[i] for i in candidates]), rest
        for i in candidates:
            addition = min(most - holding[i], max(1, budget * weights[i] // mass), rest)
            holding[i] = holding[i] + addition
            rest = rest - addition
    return np.array(holding)


def noise(rng, shape, scale, reach, cuts=(), held_as=jnp.bfloat16):
    factor_of = level_of(rng, shape, cuts, -0.22, 0.18) if cuts else 1.0
    array = jax.random.normal(rng, shape, jnp.float32) * scale * factor_of
    return jnp.minimum(jnp.maximum(array, -reach), reach).astype(held_as)


def gaussian_with(rng, extent, spread, limit, cuts, heavy, held_as=jnp.bfloat16):
    values = spread * jax.random.normal(rng, extent, jnp.float32)
    if cuts:
        values = values * level_of(rng, extent, cuts, -0.22, 0.18)
    return jnp.clip(raised(values, jax.random.fold_in(rng, 3), *heavy), -limit, limit).astype(held_as)


def setup_inputs(seed: int = 0) -> dict:
    seeds = jax.random.split(jax.random.key(seed), 17)
    block_input = noise(seeds[0], (SEQS, SEQUENCE_TOKENS, MODEL_WIDTH), 1.0, 6.0, ((0, 16), (1, 2)))
    attn_gain = jnp.clip(1.0 + 0.15 * jax.random.normal(seeds[1], (MODEL_WIDTH,), jnp.float32), 0.25, 1.75)
    query_weight = noise(seeds[2], (MODEL_WIDTH, QUERY_HEADS * HEAD_SIZE), MODEL_WIDTH ** -0.5, 0.125, ((0, 32),))
    key_matrix = noise(seeds[3], (MODEL_WIDTH, KEY_VALUE_HEADS * HEAD_SIZE), MODEL_WIDTH ** -0.5, 0.125, ((0, 32),))
    value_matrix = noise(seeds[4], (MODEL_WIDTH, KEY_VALUE_HEADS * HEAD_SIZE), MODEL_WIDTH ** -0.5, 0.125, ((0, 32),))
    output_weight = noise(seeds[5], (QUERY_HEADS * HEAD_SIZE, MODEL_WIDTH), (QUERY_HEADS * HEAD_SIZE // 16) ** -0.5, 0.5, ((0, 32),))
    ffn_gain = jnp.clip(1.0 + 0.15 * jax.random.normal(seeds[6], (MODEL_WIDTH,), jnp.float32), 0.25, 1.75)
    shared_gate = noise(seeds[7], (MODEL_WIDTH, SH), MODEL_WIDTH ** -0.5, 0.125, ((0, 32),))
    shared_up = noise(seeds[8], (MODEL_WIDTH, SH), MODEL_WIDTH ** -0.5, 0.125, ((0, 32),))
    shared_down = noise(seeds[9], (SH, MODEL_WIDTH), (SH // 4) ** -0.5, 0.21875, ((0, 32),))
    expert_gate = noise(seeds[10], (EXPERTS, MODEL_WIDTH, FF), MODEL_WIDTH ** -0.5, 0.125, ((0, 16), (1, 2)))
    expert_up = noise(seeds[11], (EXPERTS, MODEL_WIDTH, FF), MODEL_WIDTH ** -0.5, 0.125, ((0, 16), (1, 2)))
    expert_down = noise(seeds[12], (EXPERTS, FF, MODEL_WIDTH), (FF // 16) ** -0.5, 0.625, ((0, 16), (2, 2)))
    routes_keys = jax.random.split(jax.random.fold_in(seeds[13], 1), SEQS * SEQUENCE_TOKENS // TOK_DEV)
    routes_turns = jax.random.permutation(jax.random.fold_in(seeds[13], 3), SEQS * SEQUENCE_TOKENS // TOK_DEV)
    routes = jax.vmap(lambda own, number: routed_block(jax.random.fold_in(seeds[13], 2), own, number, TOK_DEV, EXPERTS, TOP, CAP, 1))(routes_keys, routes_turns).reshape((SEQS, SEQUENCE_TOKENS, TOP))
    route_weights = jnp.clip(0.05 + 0.25 * jax.random.uniform(seeds[14], (SEQS, SEQUENCE_TOKENS, TOP), jnp.float32) ** level_of(seeds[14], (SEQS, SEQUENCE_TOKENS, TOP), ((0, 16), (1, 2)), -0.2, 0.2), 0.05, 0.3)
    cotangent = gaussian_with(seeds[15], (SEQS, SEQUENCE_TOKENS, MODEL_WIDTH), 1.0, 6.0, ((0, 16), (1, 2)), (0, 2, 16, 2.0))
    return {"block_input": block_input, "attn_gain": attn_gain, "query_weight": query_weight, "key_matrix": key_matrix, "value_matrix": value_matrix, "output_weight": output_weight, "ffn_gain": ffn_gain, "shared_gate": shared_gate, "shared_up": shared_up, "shared_down": shared_down, "expert_gate": expert_gate, "expert_up": expert_up, "expert_down": expert_down, "routes": routes, "route_weights": route_weights, "cotangent": cotangent}


norm_eps = 1e-05
rope_base = 500000.0
causal_masked_score = -1e+30

@jax.custom_vjp
def reduced_cast(v):
    return lax.optimization_barrier(v.astype(jnp.bfloat16)).astype(jnp.float32)

@jax.custom_vjp
def reduced_cast_backward(v):
    return v

def low_keep(v):
    return (reduced_cast(v), None)

def low_pass(kept, grad):
    return (grad,)

def back_keep(v):
    return (v, None)

def back_low(kept, grad):
    return (reduced_cast(grad),)
reduced_cast.defvjp(low_keep, low_pass)
reduced_cast_backward.defvjp(back_keep, back_low)

def precise_product(left, right):
    return jnp.dot(left, right, precision=lax.Precision.HIGHEST, preferred_element_type=jnp.float32)

def rms_apply(value_rows_all, gain_vector):
    return value_rows_all * lax.rsqrt(lax.optimization_barrier(jnp.mean(value_rows_all * value_rows_all, axis=-1, keepdims=True)) + norm_eps) * gain_vector

def rotary_apply(value_rows_all, token_positions, head_count, direction):
    row_count = value_rows_all.shape[0]
    head_width = value_rows_all.shape[1] // head_count
    half_width = head_width // 2
    shaped = value_rows_all.reshape(row_count, head_count, head_width)
    frequency = rope_base ** (-(jnp.arange(half_width, dtype=jnp.float32) * 2.0 / head_width))
    angles = token_positions[:, None].astype(jnp.float32) * frequency[None, :]
    cosine = jnp.cos(angles)[:, None, :]
    sine_part = direction * jnp.sin(angles)[:, None, :]
    first_half = shaped[:, :, :half_width]
    second = shaped[:, :, half_width:]
    turned = jnp.concatenate([first_half * cosine - second * sine_part, first_half * sine_part + second * cosine], axis=-1)
    return turned.reshape(row_count, head_count * head_width)

def attend_one(normalized_rows, query_projection_weight, key_projection_weight, value_projection_weight, output_projection_weight):
    token_positions = jnp.arange(SEQUENCE_TOKENS, dtype=jnp.int32)
    group_width = QUERY_HEADS // KEY_VALUE_HEADS
    query_rows = reduced_cast(rotary_apply(reduced_cast_backward(precise_product(normalized_rows, query_projection_weight)), token_positions, QUERY_HEADS, 1.0))
    key_value_pairs = reduced_cast(rotary_apply(reduced_cast_backward(precise_product(normalized_rows, key_projection_weight)), token_positions, KEY_VALUE_HEADS, 1.0))
    value_rows_all = reduced_cast(reduced_cast_backward(precise_product(normalized_rows, value_projection_weight)))
    query_head_split = query_rows.reshape(SEQUENCE_TOKENS, KEY_VALUE_HEADS, group_width, HEAD_SIZE)
    key_head_split = key_value_pairs.reshape(SEQUENCE_TOKENS, KEY_VALUE_HEADS, HEAD_SIZE)
    value_head_split = value_rows_all.reshape(SEQUENCE_TOKENS, KEY_VALUE_HEADS, HEAD_SIZE)
    scores = jnp.einsum('qhgd,khd->hgqk', query_head_split, key_head_split, precision=lax.Precision.HIGHEST)
    scores = reduced_cast_backward(scores * HEAD_SIZE ** (-0.5))
    allowed = token_positions[:, None] >= token_positions[None, :]
    scores = jnp.where(allowed, scores, causal_masked_score)
    shifted = jnp.exp(scores - lax.optimization_barrier(jnp.max(scores, axis=-1, keepdims=True)))
    probabilities = shifted / lax.optimization_barrier(jnp.sum(shifted, axis=-1, keepdims=True))
    attended = jnp.einsum('hgqk,khd->qhgd', reduced_cast(probabilities), value_head_split, precision=lax.Precision.HIGHEST)
    attended = reduced_cast(reduced_cast_backward(attended.reshape(SEQUENCE_TOKENS, QUERY_HEADS * HEAD_SIZE)))
    return reduced_cast_backward(precise_product(attended, output_projection_weight))

def single_expert(pieces):
    row_block, gate_w, up_w, down_w = pieces
    gate_val = reduced_cast_backward(precise_product(row_block, gate_w))
    up_val = reduced_cast_backward(precise_product(row_block, up_w))
    activation = reduced_cast(jax.nn.silu(gate_val) * up_val)
    return reduced_cast(reduced_cast_backward(precise_product(activation, down_w)))

def reference(block_input, attn_gain, query_weight, key_matrix, value_matrix, output_weight, ffn_gain, shared_gate, shared_up, shared_down, expert_gate, expert_up, expert_down, routes, route_weights, cotangent):
    blocks = SEQS * SEQUENCE_TOKENS // TOK_DEV
    flat_routes = routes.reshape(blocks, TOK_DEV * TOP).astype(jnp.int32)
    onehot = (flat_routes[:, :, None] == jnp.arange(EXPERTS, dtype=jnp.int32)[None, None, :]).astype(jnp.int32)
    before = jnp.cumsum(onehot, axis=1) - onehot
    slot_in_block = lax.optimization_barrier(jnp.sum(before * onehot, axis=2))
    slot_index = ((flat_routes * blocks + jnp.arange(blocks, dtype=jnp.int32)[:, None]) * CAP + slot_in_block).reshape(-1)
    gate_values = route_weights.reshape(-1, TOP).astype(jnp.float32)

    def forward_pass(input_rows, first_gain, query_projection_weight, key_projection_weight, value_projection_weight, output_projection_weight, second_gain, shared_gate_weight, shared_up_weight, shared_down_weight, expert_gate_weight, expert_up_weight, expert_down_weight):
        normed_one = reduced_cast(rms_apply(input_rows, first_gain))
        attn_out = lax.map(jax.checkpoint(lambda normalized_rows: attend_one(normalized_rows, query_projection_weight, key_projection_weight, value_projection_weight, output_projection_weight)), normed_one)
        middle = (input_rows + attn_out).reshape(-1, MODEL_WIDTH)
        normed_two = reduced_cast(rms_apply(middle, second_gain))
        shared_act = reduced_cast(jax.nn.silu(reduced_cast_backward(precise_product(normed_two, shared_gate_weight))) * reduced_cast_backward(precise_product(normed_two, shared_up_weight)))
        shared_out = precise_product(shared_act, shared_down_weight)
        holding_store = jnp.zeros((EXPERTS * blocks * CAP, MODEL_WIDTH), jnp.float32).at[slot_index].set(jnp.repeat(normed_two, TOP, axis=0))
        holding_store = reduced_cast_backward(holding_store).reshape(EXPERTS, blocks * CAP, MODEL_WIDTH)
        expert_token_rows = lax.map(jax.checkpoint(single_expert), (holding_store, expert_gate_weight, expert_up_weight, expert_down_weight))
        picked = expert_token_rows.reshape(-1, MODEL_WIDTH)[slot_index].reshape(-1, TOP, MODEL_WIDTH)
        routed_out = lax.optimization_barrier(jnp.sum(gate_values[:, :, None] * picked, axis=1))
        return (middle + shared_out + routed_out).reshape(input_rows.shape)
    result, pullback = jax.vjp(forward_pass, block_input.astype(jnp.float32), attn_gain.astype(jnp.float32), query_weight.astype(jnp.float32), key_matrix.astype(jnp.float32), value_matrix.astype(jnp.float32), output_weight.astype(jnp.float32), ffn_gain.astype(jnp.float32), shared_gate.astype(jnp.float32), shared_up.astype(jnp.float32), shared_down.astype(jnp.float32), expert_gate.astype(jnp.float32), expert_up.astype(jnp.float32), expert_down.astype(jnp.float32))
    gradients = pullback(cotangent.astype(jnp.float32))
    return (result.astype(jnp.bfloat16), gradients[0], gradients[1], gradients[2], gradients[3], gradients[4], gradients[5], gradients[6], gradients[7], gradients[8], gradients[9], gradients[10], gradients[11], gradients[12])
```

```python
import functools

import jax
import jax.numpy as jnp
import numpy as np
from jax import lax
from jax.experimental import pallas as pl
from jax.experimental.pallas import tpu as pltpu
from jax.sharding import PartitionSpec as P

MODEL_WIDTH = 2560
QUERY_HEADS = 20
KEY_VALUE_HEADS = 4
HEAD_SIZE = 128
TOP = 6
GROUP = QUERY_HEADS // KEY_VALUE_HEADS
QUERY_WIDTH = QUERY_HEADS * HEAD_SIZE
KEY_WIDTH = KEY_VALUE_HEADS * HEAD_SIZE
KERNEL_VMEM = 56 * 1024 * 1024


norm_eps = 1e-05
rope_base = 500000.0
causal_masked_score = -1e30


def rope_tables(token_positions):
    half_width = HEAD_SIZE // 2
    frequency = rope_base ** (-(jnp.arange(half_width, dtype=jnp.float32) * 2.0 / HEAD_SIZE))
    angles = token_positions[:, None].astype(jnp.float32) * frequency[None, :]
    cosine, sine = jnp.cos(angles), jnp.sin(angles)
    return (
        jnp.concatenate([cosine, cosine], axis=1),
        jnp.concatenate([-sine, sine], axis=1),
    )


def rms_scale(value_rows_all):
    return lax.rsqrt(jnp.mean(value_rows_all * value_rows_all, axis=-1, keepdims=True) + norm_eps)


def norm_back(grad_normed, source, inverse, gain_vector):
    scaled = grad_normed * gain_vector
    return inverse * scaled - source * inverse**3 * jnp.mean(
        scaled * source, axis=-1, keepdims=True
    )


def silu_back(grad_act, gate_val, up_val):
    sigmoid_val = jax.nn.sigmoid(gate_val)
    grad_gate = grad_act * up_val * sigmoid_val * (1.0 + gate_val * (1.0 - sigmoid_val))
    grad_up = grad_act * gate_val * sigmoid_val
    return (grad_gate.astype(jnp.bfloat16), grad_up.astype(jnp.bfloat16))


def dot32(left, right):
    return jnp.dot(left, right, preferred_element_type=jnp.float32)


def dot_t(left, right):
    return lax.dot_general(
        left, right, (((1,), (1,)), ((), ())), preferred_element_type=jnp.float32
    )


def t_dot(left, right):
    return lax.dot_general(
        left, right, (((0,), (0,)), ((), ())), preferred_element_type=jnp.float32
    )


def tie(*values):
    return lax.optimization_barrier(values)


def kernel_params():
    return pltpu.CompilerParams(vmem_limit_bytes=KERNEL_VMEM)


def cost(flops, bytes_accessed, transcendentals=0):
    return pl.CostEstimate(
        flops=int(flops), bytes_accessed=int(bytes_accessed), transcendentals=int(transcendentals)
    )


def turn(values, cosine, sine):
    return values * cosine + pltpu.roll(values, HEAD_SIZE // 2, 1) * sine


def project_kernel(plain_from, rows_ref, weight_ref, cos_ref, sin_ref, out_ref):
    product = dot32(rows_ref[...], weight_ref[...])
    plain = pl.program_id(0) >= plain_from
    cosine = jnp.where(plain, 1.0, cos_ref[...])
    sine = jnp.where(plain, 0.0, sin_ref[...])
    for head in range(product.shape[1] // HEAD_SIZE):
        lanes = slice(head * HEAD_SIZE, (head + 1) * HEAD_SIZE)
        out_ref[:, lanes] = turn(product[:, lanes], cosine, sine).astype(jnp.bfloat16)


def project(rows, weight, tables, first_block, blocks, plain_from):
    count = rows.shape[0]
    return pl.pallas_call(
        functools.partial(project_kernel, plain_from),
        grid=(blocks,),
        in_specs=[
            pl.BlockSpec(rows.shape, lambda j: (0, 0)),
            pl.BlockSpec((weight.shape[0], KEY_WIDTH), lambda j: (0, first_block + j)),
            pl.BlockSpec(tables[0].shape, lambda j: (0, 0)),
            pl.BlockSpec(tables[1].shape, lambda j: (0, 0)),
        ],
        out_specs=pl.BlockSpec((count, KEY_WIDTH), lambda j: (0, j)),
        out_shape=jax.ShapeDtypeStruct((count, blocks * KEY_WIDTH), jnp.bfloat16),
        compiler_params=kernel_params(),
        cost_estimate=cost(
            2 * count * weight.shape[0] * blocks * KEY_WIDTH,
            2 * weight.shape[0] * (blocks * KEY_WIDTH + count),
        ),
        name="project",
    )(rows, weight, *tables)


def attend_probs(offset, first_row, query, keys):
    scores = dot_t(query, keys) * HEAD_SIZE ** (-0.5)
    rows = lax.broadcasted_iota(jnp.int32, scores.shape, 0) + (offset + first_row)
    places = lax.broadcasted_iota(jnp.int32, scores.shape, 1)
    scores = jnp.where(rows >= places, scores, causal_masked_score)
    weights = jnp.exp(scores - jnp.max(scores, axis=1, keepdims=True))
    return weights * (1.0 / jnp.sum(weights, axis=1, keepdims=True))


def attend_kernel(tile, offset_ref, query_ref, key_ref, value_ref, out_ref):
    keys, values = key_ref[...], value_ref[...]
    for head in range(GROUP):
        lanes = slice(head * HEAD_SIZE, (head + 1) * HEAD_SIZE)
        for start in range(0, query_ref.shape[0], tile):
            rows = slice(start, start + tile)
            probs = attend_probs(offset_ref[0], start, query_ref[rows, lanes], keys)
            out_ref[rows, lanes] = dot32(probs.astype(jnp.bfloat16), values).astype(jnp.bfloat16)


def attend(offset, query, key_value):
    count, places = query.shape[0], key_value.shape[0]
    work = count * places * HEAD_SIZE * QUERY_HEADS
    return pl.pallas_call(
        functools.partial(attend_kernel, min(count, 256)),
        grid=(KEY_VALUE_HEADS,),
        in_specs=[
            pl.BlockSpec(memory_space=pltpu.SMEM),
            pl.BlockSpec((count, GROUP * HEAD_SIZE), lambda g: (0, g)),
            pl.BlockSpec((places, HEAD_SIZE), lambda g: (0, g)),
            pl.BlockSpec((places, HEAD_SIZE), lambda g: (0, KEY_VALUE_HEADS + g)),
        ],
        out_specs=pl.BlockSpec((count, GROUP * HEAD_SIZE), lambda g: (0, g)),
        out_shape=jax.ShapeDtypeStruct(query.shape, jnp.bfloat16),
        compiler_params=kernel_params(),
        cost_estimate=cost(4 * work, 4 * query.size + 2 * key_value.size, work // HEAD_SIZE),
        name="attend",
    )(offset, query, key_value, key_value)


def attend_back_kernel(
    tile,
    offset_ref,
    query_ref,
    key_ref,
    value_ref,
    grad_ref,
    cos_ref,
    sin_ref,
    key_cos_ref,
    key_sin_ref,
    query_out,
    key_out,
    value_out,
):
    scale = HEAD_SIZE ** (-0.5)
    keys, values = key_ref[...], value_ref[...]
    key_sum = jnp.zeros(keys.shape, jnp.float32)
    value_sum = jnp.zeros(values.shape, jnp.float32)
    for head in range(GROUP):
        lanes = slice(head * HEAD_SIZE, (head + 1) * HEAD_SIZE)
        for start in range(0, query_ref.shape[0], tile):
            rows = slice(start, start + tile)
            query, grad = query_ref[rows, lanes], grad_ref[rows, lanes]
            probs = attend_probs(offset_ref[0], start, query, keys)
            grad_probs = dot_t(grad, values)
            delta = jnp.sum(probs * grad_probs, axis=1, keepdims=True)
            grad_scores = (probs * (grad_probs - delta)).astype(jnp.bfloat16)
            query_grad = dot32(grad_scores, keys) * scale
            query_out[rows, lanes] = turn(
                query_grad, cos_ref[rows, :], -sin_ref[rows, :]
            ).astype(jnp.bfloat16)
            key_sum = key_sum + t_dot(grad_scores, query)
            value_sum = value_sum + t_dot(probs.astype(jnp.bfloat16), grad)
    key_out[...] = turn(key_sum * scale, key_cos_ref[...], -key_sin_ref[...])
    value_out[...] = value_sum


def attend_back(offset, query, key_value, grad, tables, key_tables):
    count, places = query.shape[0], key_value.shape[0]
    work = count * places * HEAD_SIZE * QUERY_HEADS
    heads = pl.BlockSpec((count, GROUP * HEAD_SIZE), lambda g: (0, g))
    table = pl.BlockSpec((count, HEAD_SIZE), lambda g: (0, 0))
    key_table = pl.BlockSpec((places, HEAD_SIZE), lambda g: (0, 0))
    key_heads = pl.BlockSpec((places, HEAD_SIZE), lambda g: (0, g))
    return pl.pallas_call(
        functools.partial(attend_back_kernel, min(count, 256)),
        grid=(KEY_VALUE_HEADS,),
        in_specs=[
            pl.BlockSpec(memory_space=pltpu.SMEM),
            heads,
            key_heads,
            pl.BlockSpec((places, HEAD_SIZE), lambda g: (0, KEY_VALUE_HEADS + g)),
            heads,
            table,
            table,
            key_table,
            key_table,
        ],
        out_specs=[heads, key_heads, key_heads],
        out_shape=[
            jax.ShapeDtypeStruct(query.shape, jnp.bfloat16),
            jax.ShapeDtypeStruct((places, KEY_WIDTH), jnp.float32),
            jax.ShapeDtypeStruct((places, KEY_WIDTH), jnp.float32),
        ],
        compiler_params=kernel_params(),
        cost_estimate=cost(
            10 * work, 6 * query.size + 6 * key_value.size, work // HEAD_SIZE
        ),
        name="attend_back",
    )(offset, query, key_value, key_value, grad, *tables, *key_tables)


def combine_kernel(scaled, unit_ref, info_ref, rows_ref, act_ref, weight_ref, *rest):
    *added_refs, out_ref = rest
    slot = info_ref[0, :, 0:1]
    capacity = rows_ref.shape[1]
    lanes = lax.broadcasted_iota(jnp.int32, (slot.shape[0], capacity), 1).astype(jnp.float32)
    pick = jnp.where(slot == lanes, 1.0, 0.0).astype(jnp.bfloat16)
    total = dot32(pick, rows_ref[0])
    if scaled:
        total = total * info_ref[0, :, 1:2]
    total = total + dot32(act_ref[0], weight_ref[...])
    for added in added_refs:
        total = total + added[0].astype(jnp.float32)
    out_ref[0] = total.astype(out_ref.dtype)


def combine(units, info, rows, act, weight, scaled, added=(), out_dtype=jnp.bfloat16):
    count = units.shape[0]
    half, width = info.shape[1], rows.shape[2]
    columns = width // 2
    hidden = act.shape[2]
    in_specs = [
        pl.BlockSpec((1, half, info.shape[2]), lambda j, i, u: (u[i], 0, 0)),
        pl.BlockSpec((1, rows.shape[1], columns), lambda j, i, u: (u[i] // 2, 0, j)),
        pl.BlockSpec((1, half, hidden), lambda j, i, u: (u[i], 0, 0)),
        pl.BlockSpec((hidden, columns), lambda j, i, u: (0, j)),
    ]
    for _, at in added:
        in_specs.append(pl.BlockSpec((1, half, columns), lambda j, i, u, at=at: (at + i, 0, j)))
    return pl.pallas_call(
        functools.partial(combine_kernel, scaled),
        grid_spec=pltpu.PrefetchScalarGridSpec(
            num_scalar_prefetch=1,
            grid=(2, count),
            in_specs=in_specs,
            out_specs=pl.BlockSpec((1, half, columns), lambda j, i, u: (i, 0, j)),
        ),
        out_shape=jax.ShapeDtypeStruct((count, half, width), out_dtype),
        compiler_params=kernel_params(),
        cost_estimate=cost(
            2 * count * half * width * (rows.shape[1] + hidden),
            2 * count * width * (rows.shape[1] + half * (1 + len(added))),
        ),
        name="combine",
    )(units, info, rows, act, weight, *[array for array, _ in added])


def exp_ring(chips):
    if chips % 2:
        return list(range(chips))
    return list(range(0, chips, 2)) + list(range(chips - 1, 0, -2))


def exp_sum_scatter(make, final, pieces=()):
    exp_count = lax.axis_size("exp")
    chips = exp_count // 2
    ring = exp_ring(chips)
    place_of = np.argsort(np.array(ring)).astype(np.int32)
    index = lax.axis_index("exp")
    core = index % 2
    place = jnp.asarray(place_of)[index // 2]
    ring_array = jnp.asarray(np.array(ring, np.int32))

    def unit(at, of_core, half):
        return ((ring_array[at % chips] * 2 + of_core) * 2 + half).astype(jnp.int32)

    def both_units(step, of_core):
        return [unit(place - step + chips, of_core, 0), unit(place + step, of_core, 1)]

    swap = [(i, i ^ 1) for i in range(exp_count)]
    onward, backward = [], []
    for at in range(chips):
        for of_core in range(2):
            here, there = ring[at] * 2 + of_core, ring[(at + 1) % chips] * 2 + of_core
            onward.append((here, there))
            backward.append((there, here))
    early = 2
    groups = [range(1, early + 1), range(early + 1, chips + 1)]
    partner = []
    for steps in groups:
        units = jnp.stack([u for step in steps for u in both_units(step, 1 - core)])
        sent = lax.ppermute(make(units, ()), "exp", swap)
        partner += [(sent, 2 * i + half) for i in range(len(steps)) for half in range(2)]
    arrived = [(), ()]
    done = []
    for step in range(1, chips + 1):
        units = both_units(step, core)
        totals = []
        for half in range(2):
            added = arrived[half] + (partner[2 * (step - 1) + half],)
            if step < chips:
                totals.append(make(units[half][None], added))
            else:
                totals.append(final(half, units[half][None], added))
        if step == chips:
            return jnp.concatenate(totals, axis=0), done
        if step <= len(pieces):
            operands, work = pieces[step - 1]
            totals[0], totals[1], operands = tie(totals[0], totals[1], operands(done))
        moved = [lax.ppermute(totals[0], "exp", onward), lax.ppermute(totals[1], "exp", backward)]
        if step <= len(pieces):
            moved[0], moved[1], result = tie(moved[0], moved[1], work(*operands))
            done.append(result)
        arrived = [((moved[0], 0),), ((moved[1], 0),)]


def ctx_gather(part, axis):
    if lax.axis_size("ctx") != 2:
        return lax.all_gather(part, "ctx", axis=axis, tiled=True)
    other = lax.ppermute(part, "ctx", [(0, 1), (1, 0)])
    first = lax.axis_index("ctx") == 0
    return jnp.concatenate(
        [jnp.where(first, part, other), jnp.where(first, other, part)], axis=axis
    )


def ctx_cut(left, right, axis, part):
    if lax.axis_size("ctx") == 2:
        size = (left, right)[axis].shape[1] // 2
        if axis == 0:
            left = lax.dynamic_slice_in_dim(left, part * size, size, axis=1)
        else:
            right = lax.dynamic_slice_in_dim(right, part * size, size, axis=1)
    return t_dot(left, right)


def ctx_theirs(axis):
    return lambda left, right: ctx_cut(left, right, axis, 1 - lax.axis_index("ctx")).astype(
        jnp.bfloat16
    )


def ctx_send(theirs, axis):
    if lax.axis_size("ctx") == 2:
        return lax.ppermute(theirs, "ctx", [(0, 1), (1, 0)])
    return lax.psum_scatter(theirs, "ctx", scatter_dimension=axis, tiled=True)


def ctx_total(axis):
    def total(left, right, arrived):
        if lax.axis_size("ctx") == 2:
            return ctx_cut(left, right, axis, lax.axis_index("ctx")) + arrived.astype(jnp.float32)
        return arrived.astype(jnp.float32)

    return total


def on_device(
    block_input,
    attn_gain,
    query_weight,
    key_matrix,
    value_matrix,
    output_weight,
    ffn_gain,
    shared_gate,
    shared_up,
    shared_down,
    expert_gate,
    expert_up,
    expert_down,
    routes,
    route_weights,
    cotangent,
):
    input_rows = block_input[0].astype(jnp.float32)
    tokens = input_rows.shape[0]
    ctx_count = lax.axis_size("ctx")
    exp_count = lax.axis_size("exp")
    exp_index = lax.axis_index("exp")
    both = ("ctx", "exp")
    offset = lax.axis_index("ctx") * tokens
    offset_array = jnp.full((1,), offset, jnp.int32)
    tables = rope_tables(offset + jnp.arange(tokens, dtype=jnp.int32))
    key_tables = rope_tables(jnp.arange(ctx_count * tokens, dtype=jnp.int32))

    attn_in = jnp.concatenate([query_weight, key_matrix, value_matrix], axis=1)
    full_in = lax.all_gather(attn_in, both, axis=0, tiled=True)
    routing = lax.all_gather(
        jnp.concatenate([routes[0].T.astype(jnp.float32), route_weights[0].T], axis=0),
        "exp",
        axis=0,
    )
    grad_low = cotangent[0]

    own_rows = shared_gate.shape[0]
    own_hidden = shared_down.shape[0]
    shared_columns = ctx_count * own_hidden
    shared_in = jnp.stack([shared_gate, shared_up]).reshape(
        2, own_rows, ctx_count, exp_count, own_hidden
    )
    shared_in = jnp.transpose(shared_in, (3, 1, 0, 2, 4)).reshape(
        exp_count, own_rows, 2 * shared_columns
    )
    shared_in = lax.all_to_all(shared_in, "exp", split_axis=0, concat_axis=0, tiled=True)
    shared_in = ctx_gather(shared_in.reshape(exp_count * own_rows, 2 * shared_columns), 0)
    shared_in_t = shared_in.T
    shared_out_w = ctx_gather(shared_down, 0)

    gate_w = ctx_gather(expert_gate[0], 0)
    gate_w, up_part = tie(gate_w, expert_up[0])
    up_w = ctx_gather(up_part, 0)
    up_w, down_part = tie(up_w, expert_down[0])
    down_w = ctx_gather(down_part, 1)

    capacity = tokens * TOP * 4 // (3 * exp_count)
    named = routing[:, :TOP] == exp_index.astype(jnp.float32)
    chosen = jnp.any(named, axis=1)
    token_weight = jnp.sum(jnp.where(named, routing[:, TOP:], 0.0), axis=1)
    upto = (jnp.arange(tokens)[:, None] <= jnp.arange(tokens)[None, :]).astype(jnp.bfloat16)
    slot = dot32(chosen.astype(jnp.bfloat16), upto).astype(jnp.int32) - 1
    slot = jnp.where(chosen, slot, -1)
    match = slot[:, None, :] == jnp.arange(capacity, dtype=jnp.int32)[None, :, None]
    pick = match.astype(jnp.bfloat16)
    slot_weight = jnp.sum(jnp.where(match, token_weight[:, None, :], 0.0), axis=2)
    token_info = jnp.pad(
        jnp.stack([slot.astype(jnp.float32), token_weight], axis=2), ((0, 0), (0, 0), (0, 126))
    ).reshape(2 * exp_count, tokens // 2, 128)

    inverse_one = rms_scale(input_rows)
    normed_one = (input_rows * inverse_one * attn_gain).astype(jnp.bfloat16)
    full_in, normed_one, pick, slot_weight, token_info, shared_in, shared_in_t, shared_out_w, gate_w = tie(
        full_in,
        normed_one,
        pick,
        slot_weight,
        token_info,
        shared_in,
        shared_in_t,
        shared_out_w,
        gate_w,
    )
    output_weight, full_in = tie(output_weight, full_in)
    full_output = lax.all_gather(output_weight, both, axis=0, tiled=True)
    key_value = ctx_gather(
        project(normed_one, full_in, tables, QUERY_HEADS // KEY_VALUE_HEADS, 2, 1), 0
    )
    query = project(normed_one, full_in, tables, 0, QUERY_HEADS // KEY_VALUE_HEADS, QUERY_HEADS)
    attended_low = attend(offset_array, query, key_value)
    full_output, up_w = tie(full_output, up_w)
    middle = input_rows + dot32(attended_low, full_output)
    inverse_two = rms_scale(middle)
    normed_two = (middle * inverse_two * ffn_gain).astype(jnp.bfloat16)

    rows_all = lax.all_gather(normed_two, "exp", axis=0, tiled=True)
    rows_all, down_w, grad_low = tie(rows_all, down_w, grad_low)
    grad_all = lax.all_gather(grad_low, "exp", axis=0, tiled=True)

    def to_slots(rows):
        return jnp.einsum(
            "sct,std->scd",
            pick,
            rows.reshape(exp_count, tokens, MODEL_WIDTH),
            preferred_element_type=jnp.float32,
        )

    received = to_slots(rows_all).astype(jnp.bfloat16).reshape(exp_count * capacity, MODEL_WIDTH)

    expert_g = dot32(received, gate_w)
    expert_u = dot32(received, up_w)
    expert_act = (jax.nn.silu(expert_g) * expert_u).astype(jnp.bfloat16)
    shared_gu = dot32(rows_all, shared_in)
    shared_g = shared_gu[:, :shared_columns]
    shared_u = shared_gu[:, shared_columns:]
    shared_act = (jax.nn.silu(shared_g) * shared_u).astype(jnp.bfloat16)
    expert_rows = dot32(expert_act, down_w).astype(jnp.bfloat16)

    units_all = 2 * exp_count
    half_tokens = tokens // 2

    def slots(rows):
        return rows.reshape(exp_count, capacity, MODEL_WIDTH)

    def halves(rows):
        return rows.reshape(units_all, half_tokens, rows.shape[1])

    pair = exp_count >= 4 and exp_count % 4 == 0 and ctx_count == 2

    def sum_over_exp(part, pieces, out_dtype, own=None):
        if pair:
            return exp_sum_scatter(
                lambda units, added: part(units, added=added),
                lambda half, units, added: part(
                    units,
                    added=added + (() if own is None else ((own, half),)),
                    out_dtype=out_dtype,
                ),
                pieces,
            )
        everything = part(jnp.arange(units_all, dtype=jnp.int32))
        summed = lax.psum_scatter(
            everything.reshape(exp_count * tokens, MODEL_WIDTH),
            "exp",
            scatter_dimension=0,
            tiled=True,
        ).astype(jnp.float32)
        if own is not None:
            summed = summed + own.reshape(tokens, MODEL_WIDTH)
        done = []
        for operands, work in pieces:
            done.append(work(*operands(done)))
        return summed.astype(out_dtype), done

    def back_rows(rows, weight):
        return (
            (to_slots(rows) * weight[:, :, None])
            .astype(jnp.bfloat16)
            .reshape(exp_count * capacity, MODEL_WIDTH)
        )

    def back_act(rows, weight):
        return silu_back(dot_t(rows, weight), expert_g, expert_u)

    def back_shared(rows, weight):
        return jnp.concatenate(silu_back(dot_t(rows, weight), shared_g, shared_u), axis=1)

    def back_up(earlier, rows, weight):
        return (earlier + dot_t(rows, weight)).astype(jnp.bfloat16)

    out_part = functools.partial(
        combine,
        info=token_info,
        rows=slots(expert_rows),
        act=halves(shared_act),
        weight=shared_out_w,
        scaled=True,
    )
    output, done = sum_over_exp(
        out_part,
        [
            (lambda done: (grad_all, slot_weight), back_rows),
            (lambda done: (done[0], down_w), back_act),
            (lambda done: (grad_all, shared_out_w), back_shared),
            (lambda done: (done[1][0], gate_w), dot_t),
            (lambda done: (done[3], done[1][1], up_w), back_up),
        ],
        jnp.bfloat16,
        middle.reshape(2, half_tokens, MODEL_WIDTH),
    )
    output = output.reshape(tokens, MODEL_WIDTH)
    grad_expert, (grad_eg, grad_eu), shared_back, _, grad_rows = done

    grad_part = functools.partial(
        combine,
        info=token_info,
        rows=slots(grad_rows),
        act=halves(shared_back),
        weight=shared_in_t,
        scaled=False,
    )
    sent = {}

    def arrival(name, theirs, axis):
        if name not in sent:
            sent[name] = ctx_send(theirs, axis)
        return sent[name]

    grad_two, done = sum_over_exp(
        grad_part,
        [
            (lambda done: (received, grad_eg), ctx_theirs(0)),
            (lambda done: (received, grad_eu), ctx_theirs(0)),
            (lambda done: (expert_act, grad_expert), ctx_theirs(1)),
            (
                lambda done: (rows_all, shared_back, shared_act, grad_all),
                lambda a, b, c, d: (ctx_theirs(0)(a, b), ctx_theirs(0)(c, d)),
            ),
            (
                lambda done: (received, grad_eg, arrival("gate", done[0], 0)),
                ctx_total(0),
            ),
            (lambda done: (), lambda: ()),
            (
                lambda done: (received, grad_eu, arrival("up", done[1], 0)),
                ctx_total(0),
            ),
        ],
        jnp.float32,
    )
    grad_two = grad_two.reshape(tokens, MODEL_WIDTH)
    expert_gate_grad = done[4][None]
    expert_up_grad = done[6][None]

    ffn_gain_term = jnp.sum(grad_two * middle * inverse_two, axis=0)
    gain_term = jnp.pad(ffn_gain_term[:, None], ((0, 0), (0, 127))).astype(jnp.bfloat16)
    grad_middle = grad_low.astype(jnp.float32) + norm_back(grad_two, middle, inverse_two, ffn_gain)
    grad_middle_low = grad_middle.astype(jnp.bfloat16)
    attended_gradient = dot_t(grad_middle_low, full_output).astype(jnp.bfloat16)
    output_term = t_dot(grad_middle_low, attended_low).astype(jnp.bfloat16)
    sum_o = lax.psum_scatter(output_term, both, scatter_dimension=0, tiled=True)

    grad_query_raw, key_terms, value_terms = attend_back(
        offset_array, query, key_value, attended_gradient, tables, key_tables
    )
    key_value_grad = jnp.concatenate([key_terms, value_terms], axis=1)
    if ctx_count == 2:
        own = lax.dynamic_slice_in_dim(key_value_grad, offset, tokens, axis=0)
        other = lax.dynamic_slice_in_dim(key_value_grad, tokens - offset, tokens, axis=0)
        key_value_raw = own + ctx_send(other.astype(jnp.bfloat16), 0).astype(jnp.float32)
    else:
        key_value_raw = ctx_send(key_value_grad.astype(jnp.bfloat16), 0)
    key_value_raw = key_value_raw.astype(jnp.bfloat16)
    grad_raw = jnp.concatenate([grad_query_raw, key_value_raw], axis=1)
    in_term = t_dot(normed_one, grad_raw).astype(jnp.bfloat16)
    grad_one = dot_t(grad_raw, full_in)
    input_grad = grad_middle + norm_back(grad_one, input_rows, inverse_one, attn_gain)
    edge = QUERY_WIDTH + 2 * KEY_WIDTH
    sum_in = lax.psum_scatter(
        jnp.concatenate([in_term, gain_term], axis=1), both, scatter_dimension=0, tiled=True
    ).astype(jnp.float32)
    own_gain = lax.dynamic_slice_in_dim(
        attn_gain, (lax.axis_index("ctx") * exp_count + exp_index) * own_rows, own_rows
    )
    attn_gain_grad = jnp.sum(sum_in[:, :edge] * attn_in.astype(jnp.float32), axis=1) / own_gain

    expert_down_grad = ctx_total(1)(expert_act, grad_expert, arrival("down", done[2], 1))[None]
    sum_sd = ctx_total(0)(shared_act, grad_all, arrival("shared_down", done[3][1], 0))
    shared_in_grad = ctx_total(0)(
        rows_all, shared_back, arrival("shared_in", done[3][0], 0)
    ).astype(jnp.bfloat16)
    shared_in_grad = lax.all_to_all(
        shared_in_grad.reshape(exp_count, own_rows, 2 * shared_columns),
        "exp",
        split_axis=0,
        concat_axis=0,
        tiled=True,
    ).reshape(exp_count, own_rows, 2, ctx_count, own_hidden)
    shared_in_grad = (
        jnp.transpose(shared_in_grad, (2, 1, 3, 0, 4))
        .reshape(2, own_rows, exp_count * shared_columns)
        .astype(jnp.float32)
    )
    return (
        output[None],
        input_grad[None],
        attn_gain_grad,
        sum_in[:, :QUERY_WIDTH],
        sum_in[:, QUERY_WIDTH : QUERY_WIDTH + KEY_WIDTH],
        sum_in[:, QUERY_WIDTH + KEY_WIDTH : edge],
        sum_o.astype(jnp.float32).T,
        sum_in[:, edge],
        shared_in_grad[0],
        shared_in_grad[1],
        sum_sd,
        expert_gate_grad,
        expert_up_grad,
        expert_down_grad,
    )


def solution(mesh):
    return jax.shard_map(
        on_device,
        mesh=mesh,
        in_specs=(
            P("exp", "ctx", None),
            P(),
            P(("ctx", "exp"), None),
            P(("ctx", "exp"), None),
            P(("ctx", "exp"), None),
            P(("ctx", "exp"), None),
            P(),
            P(("ctx", "exp"), None),
            P(("ctx", "exp"), None),
            P(("ctx", "exp"), None),
            P("exp", "ctx", None),
            P("exp", "ctx", None),
            P("exp", None, "ctx"),
            P("exp", "ctx", None),
            P("exp", "ctx", None),
            P("exp", "ctx", None),
        ),
        out_specs=(
            P("exp", "ctx", None),
            P("exp", "ctx", None),
            P(("ctx", "exp")),
            P(("ctx", "exp"), None),
            P(("ctx", "exp"), None),
            P(("ctx", "exp"), None),
            P(None, ("ctx", "exp")),
            P(("ctx", "exp")),
            P(("ctx", "exp"), None),
            P(("ctx", "exp"), None),
            P(("ctx", "exp"), None),
            P("exp", "ctx", None),
            P("exp", "ctx", None),
            P("exp", None, "ctx"),
        ),
        check_vma=False,
    )
```

```python
import functools

import jax
import jax.numpy as jnp
import numpy as np
from jax import lax
from jax.experimental import pallas as pl
from jax.experimental.pallas import tpu as pltpu
from jax.sharding import PartitionSpec as P

MODEL_WIDTH = 2560
QUERY_HEADS = 20
KEY_VALUE_HEADS = 4
HEAD_SIZE = 128
TOP = 6
GROUP = QUERY_HEADS // KEY_VALUE_HEADS
QUERY_WIDTH = QUERY_HEADS * HEAD_SIZE
KEY_WIDTH = KEY_VALUE_HEADS * HEAD_SIZE
KERNEL_VMEM = 56 * 1024 * 1024
COMBINE_VMEM = 36 * 1024 * 1024


norm_eps = 1e-05
rope_base = 500000.0
causal_masked_score = -1e30


def rope_tables(token_positions):
    half_width = HEAD_SIZE // 2
    frequency = rope_base ** (-(jnp.arange(half_width, dtype=jnp.float32) * 2.0 / HEAD_SIZE))
    angles = token_positions[:, None].astype(jnp.float32) * frequency[None, :]
    cosine, sine = jnp.cos(angles), jnp.sin(angles)
    return (
        jnp.concatenate([cosine, cosine], axis=1),
        jnp.concatenate([-sine, sine], axis=1),
    )


def rms_scale(value_rows_all):
    return lax.rsqrt(jnp.mean(value_rows_all * value_rows_all, axis=-1, keepdims=True) + norm_eps)


def norm_back(grad_normed, source, inverse, gain_vector):
    scaled = grad_normed * gain_vector
    return inverse * scaled - source * inverse**3 * jnp.mean(
        scaled * source, axis=-1, keepdims=True
    )


def dot32(left, right):
    return jnp.dot(left, right, preferred_element_type=jnp.float32)


def dot_t(left, right):
    return lax.dot_general(
        left, right, (((1,), (1,)), ((), ())), preferred_element_type=jnp.float32
    )


def t_dot(left, right):
    return lax.dot_general(
        left, right, (((0,), (0,)), ((), ())), preferred_element_type=jnp.float32
    )


def tie(*values):
    return lax.optimization_barrier(values)


def kernel_params(limit=KERNEL_VMEM):
    return pltpu.CompilerParams(vmem_limit_bytes=limit)


def cost(flops, bytes_accessed, transcendentals=0):
    return pl.CostEstimate(
        flops=int(flops), bytes_accessed=int(bytes_accessed), transcendentals=int(transcendentals)
    )


def turn(values, cosine, sine):
    return values * cosine + pltpu.roll(values, HEAD_SIZE // 2, 1) * sine


def project_kernel(plain_from, rows_ref, weight_ref, cos_ref, sin_ref, out_ref):
    product = dot32(rows_ref[...], weight_ref[...])
    plain = pl.program_id(0) >= plain_from
    cosine = jnp.where(plain, 1.0, cos_ref[...])
    sine = jnp.where(plain, 0.0, sin_ref[...])
    for head in range(product.shape[1] // HEAD_SIZE):
        lanes = slice(head * HEAD_SIZE, (head + 1) * HEAD_SIZE)
        out_ref[:, lanes] = turn(product[:, lanes], cosine, sine).astype(jnp.bfloat16)


def project(rows, weight, tables, first_block, blocks, plain_from):
    count = rows.shape[0]
    return pl.pallas_call(
        functools.partial(project_kernel, plain_from),
        grid=(blocks,),
        in_specs=[
            pl.BlockSpec(rows.shape, lambda j: (0, 0)),
            pl.BlockSpec((weight.shape[0], KEY_WIDTH), lambda j: (0, first_block + j)),
            pl.BlockSpec(tables[0].shape, lambda j: (0, 0)),
            pl.BlockSpec(tables[1].shape, lambda j: (0, 0)),
        ],
        out_specs=pl.BlockSpec((count, KEY_WIDTH), lambda j: (0, j)),
        out_shape=jax.ShapeDtypeStruct((count, blocks * KEY_WIDTH), jnp.bfloat16),
        compiler_params=kernel_params(),
        cost_estimate=cost(
            2 * count * weight.shape[0] * blocks * KEY_WIDTH,
            2 * weight.shape[0] * (blocks * KEY_WIDTH + count),
        ),
        name="project",
    )(rows, weight, *tables)


def attend_probs(offset, first_row, query, keys):
    scores = dot_t(query, keys) * HEAD_SIZE ** (-0.5)
    rows = lax.broadcasted_iota(jnp.int32, scores.shape, 0) + (offset + first_row)
    places = lax.broadcasted_iota(jnp.int32, scores.shape, 1)
    scores = jnp.where(rows >= places, scores, causal_masked_score)
    weights = jnp.exp(scores - jnp.max(scores, axis=1, keepdims=True))
    return weights * (1.0 / jnp.sum(weights, axis=1, keepdims=True))


def attend_kernel(tile, offset_ref, query_ref, key_ref, value_ref, out_ref):
    keys, values = key_ref[...], value_ref[...]
    for head in range(GROUP):
        lanes = slice(head * HEAD_SIZE, (head + 1) * HEAD_SIZE)
        for start in range(0, query_ref.shape[0], tile):
            rows = slice(start, start + tile)
            probs = attend_probs(offset_ref[0], start, query_ref[rows, lanes], keys)
            out_ref[rows, lanes] = dot32(probs.astype(jnp.bfloat16), values).astype(jnp.bfloat16)


def attend(offset, query, key_value):
    count, places = query.shape[0], key_value.shape[0]
    work = count * places * HEAD_SIZE * QUERY_HEADS
    return pl.pallas_call(
        functools.partial(attend_kernel, min(count, 256)),
        grid=(KEY_VALUE_HEADS,),
        in_specs=[
            pl.BlockSpec(memory_space=pltpu.SMEM),
            pl.BlockSpec((count, GROUP * HEAD_SIZE), lambda g: (0, g)),
            pl.BlockSpec((places, HEAD_SIZE), lambda g: (0, g)),
            pl.BlockSpec((places, HEAD_SIZE), lambda g: (0, KEY_VALUE_HEADS + g)),
        ],
        out_specs=pl.BlockSpec((count, GROUP * HEAD_SIZE), lambda g: (0, g)),
        out_shape=jax.ShapeDtypeStruct(query.shape, jnp.bfloat16),
        compiler_params=kernel_params(),
        cost_estimate=cost(4 * work, 4 * query.size + 2 * key_value.size, work // HEAD_SIZE),
        name="attend",
    )(offset, query, key_value, key_value)


def attend_back_kernel(
    tile,
    offset_ref,
    query_ref,
    key_ref,
    value_ref,
    grad_ref,
    cos_ref,
    sin_ref,
    key_cos_ref,
    key_sin_ref,
    query_out,
    key_out,
    value_out,
):
    scale = HEAD_SIZE ** (-0.5)
    keys, values = key_ref[...], value_ref[...]
    key_sum = jnp.zeros(keys.shape, jnp.float32)
    value_sum = jnp.zeros(values.shape, jnp.float32)
    for head in range(GROUP):
        lanes = slice(head * HEAD_SIZE, (head + 1) * HEAD_SIZE)
        for start in range(0, query_ref.shape[0], tile):
            rows = slice(start, start + tile)
            query, grad = query_ref[rows, lanes], grad_ref[rows, lanes]
            probs = attend_probs(offset_ref[0], start, query, keys)
            grad_probs = dot_t(grad, values)
            delta = jnp.sum(probs * grad_probs, axis=1, keepdims=True)
            grad_scores = (probs * (grad_probs - delta)).astype(jnp.bfloat16)
            query_grad = dot32(grad_scores, keys) * scale
            query_out[rows, lanes] = turn(
                query_grad, cos_ref[rows, :], -sin_ref[rows, :]
            ).astype(jnp.bfloat16)
            key_sum = key_sum + t_dot(grad_scores, query)
            value_sum = value_sum + t_dot(probs.astype(jnp.bfloat16), grad)
    key_out[...] = turn(key_sum * scale, key_cos_ref[...], -key_sin_ref[...])
    value_out[...] = value_sum


def attend_back(offset, query, key_value, grad, tables, key_tables):
    count, places = query.shape[0], key_value.shape[0]
    work = count * places * HEAD_SIZE * QUERY_HEADS
    heads = pl.BlockSpec((count, GROUP * HEAD_SIZE), lambda g: (0, g))
    table = pl.BlockSpec((count, HEAD_SIZE), lambda g: (0, 0))
    key_table = pl.BlockSpec((places, HEAD_SIZE), lambda g: (0, 0))
    key_heads = pl.BlockSpec((places, HEAD_SIZE), lambda g: (0, g))
    return pl.pallas_call(
        functools.partial(attend_back_kernel, min(count, 256)),
        grid=(KEY_VALUE_HEADS,),
        in_specs=[
            pl.BlockSpec(memory_space=pltpu.SMEM),
            heads,
            key_heads,
            pl.BlockSpec((places, HEAD_SIZE), lambda g: (0, KEY_VALUE_HEADS + g)),
            heads,
            table,
            table,
            key_table,
            key_table,
        ],
        out_specs=[heads, key_heads, key_heads],
        out_shape=[
            jax.ShapeDtypeStruct(query.shape, jnp.bfloat16),
            jax.ShapeDtypeStruct((places, KEY_WIDTH), jnp.float32),
            jax.ShapeDtypeStruct((places, KEY_WIDTH), jnp.float32),
        ],
        compiler_params=kernel_params(),
        cost_estimate=cost(
            10 * work, 6 * query.size + 6 * key_value.size, work // HEAD_SIZE
        ),
        name="attend_back",
    )(offset, query, key_value, key_value, grad, *tables, *key_tables)


def silu_parts(gate_val, up_val):
    sigmoid_val = jax.nn.sigmoid(gate_val)
    silu_val = gate_val * sigmoid_val
    slope = up_val * sigmoid_val * (1.0 + gate_val * (1.0 - sigmoid_val))
    return [part.astype(jnp.bfloat16) for part in (silu_val * up_val, slope, silu_val)]


def row_chunks(count):
    return [slice(start, start + min(count, 256)) for start in range(0, count, min(count, 256))]


def slot_match(slots, capacity):
    places = lax.broadcasted_iota(jnp.int32, (capacity, slots.shape[1]), 0).astype(jnp.float32)
    return slots == places


def enter_kernel(slot_ref, rows_ref, weight_ref, picked_ref, act_ref, slope_ref):
    hidden = act_ref.shape[2]
    for chunk in row_chunks(rows_ref.shape[1]):
        product = dot32(rows_ref[0, chunk, :], weight_ref[...])
        act, slope, silu_val = silu_parts(product[:, :hidden], product[:, hidden:])
        act_ref[0, chunk, :] = act
        slope_ref[0, chunk, :hidden] = slope
        slope_ref[0, chunk, hidden:] = silu_val
    pick = jnp.where(slot_match(slot_ref[0, 0:1, :], picked_ref.shape[1]), 1.0, 0.0)
    picked_ref[0] = dot32(pick.astype(jnp.bfloat16), rows_ref[0]).astype(jnp.bfloat16)


def enter(slot_rows, rows, weight, capacity):
    count, tokens, width = rows.shape
    hidden = weight.shape[1] // 2
    block = lambda a, b: pl.BlockSpec((1, a, b), lambda i: (i, 0, 0))
    return pl.pallas_call(
        enter_kernel,
        grid=(count,),
        in_specs=[
            block(2, tokens),
            block(tokens, width),
            pl.BlockSpec(weight.shape, lambda i: (0, 0)),
        ],
        out_specs=[block(capacity, width), block(tokens, hidden), block(tokens, 2 * hidden)],
        out_shape=[
            jax.ShapeDtypeStruct((count, capacity, width), jnp.bfloat16),
            jax.ShapeDtypeStruct((count, tokens, hidden), jnp.bfloat16),
            jax.ShapeDtypeStruct((count, tokens, 2 * hidden), jnp.bfloat16),
        ],
        compiler_params=kernel_params(),
        cost_estimate=cost(
            2 * count * tokens * width * (capacity + 2 * hidden),
            2 * count * width * (tokens + capacity),
        ),
        name="enter",
    )(slot_rows, rows, weight)


def enter_back_kernel(slot_ref, rows_ref, weight_ref, slope_ref, picked_ref, grad_ref):
    rows = rows_ref[0]
    hidden = weight_ref.shape[0]
    for chunk in row_chunks(rows_ref.shape[1]):
        product = dot_t(rows_ref[0, chunk, :], weight_ref[...])
        for lanes in (slice(0, hidden), slice(hidden, 2 * hidden)):
            slope = slope_ref[0, chunk, lanes].astype(jnp.float32)
            grad_ref[0, chunk, lanes] = (product * slope).astype(jnp.bfloat16)
    match = slot_match(slot_ref[0, 0:1, :], picked_ref.shape[1])
    slot_weight = jnp.sum(jnp.where(match, slot_ref[0, 1:2, :], 0.0), axis=1, keepdims=True)
    pick = jnp.where(match, 1.0, 0.0).astype(jnp.bfloat16)
    picked_ref[0] = (dot32(pick, rows) * slot_weight).astype(jnp.bfloat16)


def enter_back(slot_rows, rows, weight, slope, capacity):
    count, tokens, width = rows.shape
    hidden = weight.shape[0]
    block = lambda a, b: pl.BlockSpec((1, a, b), lambda i: (i, 0, 0))
    return pl.pallas_call(
        enter_back_kernel,
        grid=(count,),
        in_specs=[
            block(2, tokens),
            block(tokens, width),
            pl.BlockSpec(weight.shape, lambda i: (0, 0)),
            block(tokens, 2 * hidden),
        ],
        out_specs=[block(capacity, width), block(tokens, 2 * hidden)],
        out_shape=[
            jax.ShapeDtypeStruct((count, capacity, width), jnp.bfloat16),
            jax.ShapeDtypeStruct((count, tokens, 2 * hidden), jnp.bfloat16),
        ],
        compiler_params=kernel_params(),
        cost_estimate=cost(
            2 * count * tokens * width * (capacity + hidden),
            2 * count * width * (tokens + capacity),
        ),
        name="enter_back",
    )(slot_rows, rows, weight, slope)


def expert_in_kernel(rows_ref, gate_ref, up_ref, act_ref, slope_ref, silu_ref):
    for chunk in row_chunks(rows_ref.shape[0]):
        rows = rows_ref[chunk, :]
        parts = silu_parts(dot32(rows, gate_ref[...]), dot32(rows, up_ref[...]))
        act_ref[chunk, :], slope_ref[chunk, :], silu_ref[chunk, :] = parts


def expert_in(rows, gate, up):
    count, width = rows.shape
    hidden = gate.shape[1]
    high, wide = min(count, 1024), 512
    weight = pl.BlockSpec((width, wide), lambda m, n: (0, n))
    out = pl.BlockSpec((high, wide), lambda m, n: (m, n))
    return pl.pallas_call(
        expert_in_kernel,
        grid=(count // high, hidden // wide),
        in_specs=[pl.BlockSpec((high, width), lambda m, n: (m, 0)), weight, weight],
        out_specs=[out] * 3,
        out_shape=[jax.ShapeDtypeStruct((count, hidden), jnp.bfloat16)] * 3,
        compiler_params=kernel_params(),
        cost_estimate=cost(4 * count * width * hidden, 2 * count * (width + 3 * hidden)),
        name="expert_in",
    )(rows, gate, up)


def expert_back_kernel(rows_ref, weight_ref, slope_ref, silu_ref, *rest):
    gate_out, up_out = rest[-2:]
    for chunk in row_chunks(rows_ref.shape[0]):
        product = dot_t(rows_ref[chunk, :], weight_ref[...])
        slope = slope_ref[chunk, :].astype(jnp.float32)
        silu_val = silu_ref[chunk, :].astype(jnp.float32)
        gate_out[chunk, :] = (product * slope).astype(jnp.bfloat16)
        up_out[chunk, :] = (product * silu_val).astype(jnp.bfloat16)


def expert_back(rows, weight, slope, silu_val, half, earlier=()):
    count, width = rows.shape
    hidden = weight.shape[0]
    high, wide = min(count // 2, 1024), 512
    first = half * (count // 2 // high)
    tile = pl.BlockSpec((high, wide), lambda m, n: (first + m, n))
    return pl.pallas_call(
        expert_back_kernel,
        grid=(count // 2 // high, hidden // wide),
        in_specs=[
            pl.BlockSpec((high, width), lambda m, n: (first + m, 0)),
            pl.BlockSpec((wide, width), lambda m, n: (n, 0)),
            tile,
            tile,
        ]
        + [pl.BlockSpec(memory_space=pl.ANY)] * len(earlier),
        out_specs=[tile, tile],
        out_shape=[jax.ShapeDtypeStruct((count, hidden), jnp.bfloat16)] * 2,
        input_output_aliases={4 + i: i for i in range(len(earlier))},
        compiler_params=kernel_params(),
        cost_estimate=cost(count * width * hidden, count * (width + 4 * hidden)),
        name="expert_back",
    )(rows, weight, slope, silu_val, *earlier)


def expert_rows_kernel(gate_grad_ref, up_grad_ref, gate_ref, up_ref, *rest):
    out_ref = rest[-1]
    total = dot_t(gate_grad_ref[...], gate_ref[...]) + dot_t(up_grad_ref[...], up_ref[...])
    out_ref[...] = total.astype(jnp.bfloat16)


def expert_grad_rows(gate_grad, up_grad, gate, up, column_half, half, earlier=()):
    count, hidden = gate_grad.shape
    wide = gate.shape[0] // 2
    high = min(count // 2, 512)
    first = half * (count // 2 // high)
    grad = pl.BlockSpec((high, hidden), lambda m: (first + m, 0))
    weight = pl.BlockSpec((wide, hidden), lambda m: (column_half, 0))
    return pl.pallas_call(
        expert_rows_kernel,
        grid=(count // 2 // high,),
        in_specs=[grad, grad, weight, weight] + [pl.BlockSpec(memory_space=pl.ANY)] * len(earlier),
        out_specs=pl.BlockSpec((high, wide), lambda m: (first + m, 0)),
        out_shape=jax.ShapeDtypeStruct((count, wide), jnp.bfloat16),
        input_output_aliases={4: 0} if earlier else {},
        compiler_params=kernel_params(),
        cost_estimate=cost(
            2 * count * wide * hidden, (2 * count + 4 * wide) * hidden + count * wide
        ),
        name="expert_grad_rows",
    )(gate_grad, up_grad, gate, up, *earlier)


def qkv_grad_kernel(rows_ref, query_ref, key_value_ref, gain_ref, out_ref):
    rows = rows_ref[...]
    edge = query_ref.shape[1]
    end = edge + key_value_ref.shape[1]
    out_ref[:, :edge] = dot32(rows, query_ref[...]).astype(jnp.bfloat16)
    out_ref[:, edge:end] = dot32(rows, key_value_ref[...]).astype(jnp.bfloat16)
    out_ref[:, end:] = gain_ref[...]


def qkv_grad(rows_t, query_grad, key_value_grad, gain_term):
    width, count = rows_t.shape
    high = 256
    columns = query_grad.shape[1] + key_value_grad.shape[1] + gain_term.shape[1]
    whole = lambda array: pl.BlockSpec(array.shape, lambda m: (0, 0))
    return pl.pallas_call(
        qkv_grad_kernel,
        grid=(width // high,),
        in_specs=[
            pl.BlockSpec((high, count), lambda m: (m, 0)),
            whole(query_grad),
            whole(key_value_grad),
            pl.BlockSpec((high, gain_term.shape[1]), lambda m: (m, 0)),
        ],
        out_specs=pl.BlockSpec((high, columns), lambda m: (m, 0)),
        out_shape=jax.ShapeDtypeStruct((width, columns), jnp.bfloat16),
        compiler_params=kernel_params(),
        cost_estimate=cost(2 * width * count * columns, 2 * width * (columns + count)),
        name="qkv_grad",
    )(rows_t, query_grad, key_value_grad, gain_term)


def combine_kernel(scaled, pieces, arrivals, added, unit_ref, info_ref, act_ref, weight_ref, *rest):
    rows_refs, rest = rest[:pieces], rest[pieces:]
    arrived_refs, rest = rest[:arrivals], rest[arrivals:]
    added_refs, out_refs = rest[:added], rest[added:]
    slot = info_ref[0, :, 0:1]
    capacity = rows_refs[0].shape[1]
    lanes = lax.broadcasted_iota(jnp.int32, (slot.shape[0], capacity), 1).astype(jnp.float32)
    pick = jnp.where(slot == lanes, 1.0, 0.0).astype(jnp.bfloat16)

    def store(way):
        total = dot32(pick, rows_refs[way % pieces][0])
        if scaled:
            total = total * info_ref[0, :, 1:2]
        total = total + dot32(act_ref[0], weight_ref[...])
        for added_ref in added_refs:
            total = total + added_ref[0].astype(jnp.float32)
        if arrivals:
            total = total + arrived_refs[way][0].astype(jnp.float32)
        out_ref = out_refs[way % len(out_refs)]
        out_ref[0] = total.astype(out_ref.dtype)

    if pieces == 1 and not arrivals and len(out_refs) == 1:
        store(0)
        return
    for way in range(2):

        @pl.when(pl.program_id(0) % 2 == way)
        def _(way=way):
            store(way)


def combine(
    units, info, rows, act, weight, scaled, arrived=(), partner=(), own=(), kind="units",
    out_dtype=jnp.bfloat16,
):
    count = units.shape[0]
    tokens = info.shape[1]
    width, hidden = weight.shape[1], act.shape[2]
    capacity = rows[0].shape[1]
    columns = width // 2
    unit_block = lambda array: pl.BlockSpec((1,) + array.shape[1:], lambda i, u: (u[i], 0, 0))
    fixed = pl.BlockSpec((1, tokens, columns), lambda i, u: (0, 0, 0))
    half = pl.BlockSpec((1, tokens, columns), lambda i, u: (0, 0, i % 2))
    in_specs = [
        unit_block(info),
        unit_block(act),
        pl.BlockSpec((hidden, columns), lambda i, u: (0, i % 2)),
    ]
    block = (1, capacity, columns)
    if len(rows) == 1:
        in_specs.append(pl.BlockSpec(block, lambda i, u: (u[i], 0, i % 2)))
    else:
        in_specs.append(pl.BlockSpec(block, lambda i, u: (u[i - i % 2], 0, 0)))
        in_specs.append(pl.BlockSpec(block, lambda i, u: (u[i - i % 2 + 1], 0, 0)))
    in_specs += [fixed] * len(arrived)
    added = [array for array, _ in partner] + list(own)
    for _, at in partner:
        in_specs.append(pl.BlockSpec((1, tokens, columns), lambda i, u, at=at: (at + i, 0, 0)))
    in_specs += [half] * len(own)
    out_specs, out_shape = {
        "units": (
            [pl.BlockSpec((1, tokens, columns), lambda i, u: (i, 0, 0))],
            [(count, tokens, columns)],
        ),
        "ways": ([fixed, fixed], [(1, tokens, columns)] * 2),
        "tokens": ([half], [(1, tokens, width)]),
    }[kind]
    return pl.pallas_call(
        functools.partial(combine_kernel, scaled, len(rows), len(arrived), len(added)),
        grid_spec=pltpu.PrefetchScalarGridSpec(
            num_scalar_prefetch=1, grid=(count,), in_specs=in_specs, out_specs=out_specs
        ),
        out_shape=[jax.ShapeDtypeStruct(shape, out_dtype) for shape in out_shape],
        compiler_params=kernel_params(COMBINE_VMEM),
        cost_estimate=cost(
            2 * count * tokens * columns * (capacity + hidden),
            2 * count * columns * (capacity + tokens * (1 + len(added) + len(arrived) // 2)),
        ),
        name="combine",
    )(units, info, act, weight, *rows, *arrived, *added)


def weight_grad_kernel(part_ref, left_ref, right_ref, *rest):
    *arrived_refs, out_ref, sum_ref = rest
    step = pl.program_id(0)
    product = t_dot(left_ref[...], right_ref[...])

    @pl.when(step == 0)
    def _():
        sum_ref[...] = product

    @pl.when(step > 0)
    def _():
        sum_ref[...] += product

    @pl.when(step == pl.num_programs(0) - 1)
    def _():
        total = sum_ref[...]
        for arrived_ref in arrived_refs:
            total = total + arrived_ref[...].astype(jnp.float32)
        out_ref[...] = total.astype(out_ref.dtype)


def weight_grad(left, right, axis, part, out_dtype, arrived=()):
    count = left.shape[0]
    high = min(count, 1024)
    widths = [left.shape[1], right.shape[1]]
    widths[axis] //= 2
    at = (lambda k, p: (k, p[0]), lambda k, p: (k, 0))
    whole = pl.BlockSpec(tuple(widths), lambda k, p: (0, 0))
    return pl.pallas_call(
        weight_grad_kernel,
        grid_spec=pltpu.PrefetchScalarGridSpec(
            num_scalar_prefetch=1,
            grid=(count // high,),
            in_specs=[
                pl.BlockSpec((high, widths[0]), at[axis]),
                pl.BlockSpec((high, widths[1]), at[1 - axis]),
            ]
            + [whole] * len(arrived),
            out_specs=whole,
            scratch_shapes=[pltpu.VMEM(tuple(widths), jnp.float32)],
        ),
        out_shape=jax.ShapeDtypeStruct(tuple(widths), out_dtype),
        compiler_params=kernel_params(),
        cost_estimate=cost(
            2 * count * widths[0] * widths[1], 2 * count * sum(widths) + 4 * widths[0] * widths[1]
        ),
        name="weight_grad",
    )(part, left, right, *arrived)


def exp_ring(chips):
    if chips % 2:
        return list(range(chips))
    return list(range(0, chips, 2)) + list(range(chips - 1, 0, -2))


class ChipRing:
    def __init__(self):
        exp_count = lax.axis_size("exp")
        self.chips = exp_count // 2
        ring = exp_ring(self.chips)
        place_of = np.argsort(np.array(ring)).astype(np.int32)
        index = lax.axis_index("exp")
        self.core = index % 2
        self.place = jnp.asarray(place_of)[index // 2]
        self.ring = jnp.asarray(np.array(ring, np.int32))
        self.swap = [(i, i ^ 1) for i in range(exp_count)]
        self.ways = ([], [])
        for at in range(self.chips):
            for core in range(2):
                here, there = ring[at] * 2 + core, ring[(at + 1) % self.chips] * 2 + core
                self.ways[0].append((here, there))
                self.ways[1].append((there, here))

    def targets(self, step):
        at = jnp.stack([self.place - step + self.chips, self.place + step]) % self.chips
        return self.ring[at]

    def move(self, totals):
        return [lax.ppermute(total, "exp", way) for total, way in zip(totals, self.ways)]

    def swap_cores(self, value):
        return lax.ppermute(value, "exp", self.swap)


class ExpRing:
    def __init__(self, part, out_dtype, own=(), late_from=(4,)):
        self.part, self.out_dtype, self.own = part, out_dtype, own
        self.line = ChipRing()
        self.arrived, self.step = (), 0
        self.swapped, self.partner = [], []
        edges = list(late_from) + [self.line.chips + 1]
        first = part(self.other_units(range(1, 2)))[0]
        first, units = tie(first, self.other_units(range(2, edges[0])))
        self.take(first)
        second = part(units)[0]
        second, self.late_units = tie(
            second, [self.other_units(range(*edge)) for edge in zip(edges, edges[1:])]
        )
        self.take(second)

    def units(self, step, core):
        return (self.line.targets(step) * 2 + core).astype(jnp.int32)

    def other_units(self, steps):
        return jnp.concatenate([self.units(step, 1 - self.line.core) for step in steps])

    def take(self, total):
        self.partner += [(len(self.swapped), 2 * i) for i in range(total.shape[0] // 2)]
        self.swapped.append(self.line.swap_cores(total))

    def from_partner(self, step):
        group, at = self.partner[step - 1]
        return ((self.swapped[group], at),)

    def late(self, units):
        return self.part(units)[0]

    def totals(self):
        self.step += 1
        return self.part(
            self.units(self.step, self.line.core),
            arrived=self.arrived,
            partner=self.from_partner(self.step),
            kind="ways",
        )

    def finish(self):
        return self.part(
            self.units(self.line.chips, self.line.core),
            arrived=self.arrived,
            partner=self.from_partner(self.line.chips),
            own=self.own,
            kind="tokens",
            out_dtype=self.out_dtype,
        )[0][0]


def ring_step(rings, work, *operands):
    totals = [ring.totals() for ring in rings]
    totals, operands = tie(totals, operands)
    moved = [ring.line.move(total) for ring, total in zip(rings, totals)]
    swapped = [ring.swapped for ring in rings]
    moved, swapped, result = tie(moved, swapped, work(*operands))
    for ring, arrived, ring.swapped in zip(rings, moved, swapped):
        ring.arrived = tuple(arrived)
    return result


class SpreadSum:
    def __init__(self, term):
        self.line = ChipRing()
        rows = term.shape[0] // (4 * self.line.chips)
        self.term = term.reshape(2, self.line.chips, 2, rows, term.shape[1])
        self.arrived = self.line.swap_cores(self.pick(self.term, 1 - self.line.core, 2))

    def pick(self, array, index, axis):
        return lax.dynamic_index_in_dim(array, index, axis, keepdims=False)

    def add(self, *values):
        return sum(value.astype(jnp.float32) for value in values)

    def ctx_done(self, arrived):
        value = self.add(self.pick(self.term, self.line.core, 2), arrived).astype(jnp.bfloat16)
        index = lax.axis_index("ctx")
        arrived = ctx_send(self.pick(value, 1 - index, 0), 0)
        return self.add(self.pick(value, index, 0), arrived).astype(jnp.bfloat16)

    def finish(self, value, pieces):
        done = []
        columns = value.shape[2] // 2
        halves = [value[..., :columns], value[..., columns:]]
        arrived = ([], [])
        for step in range(1, self.line.chips + 1):
            targets = self.line.targets(step)
            totals = [
                self.add(self.pick(halves[way], targets[way], 0), *arrived[way]) for way in range(2)
            ]
            if step == self.line.chips:
                return jnp.concatenate(totals, axis=1), done
            totals = [total.astype(jnp.bfloat16) for total in totals]
            if step <= len(pieces):
                operands, work = pieces[step - 1]
                totals, operands = tie(totals, operands)
            moved = self.line.move(totals)
            if step <= len(pieces):
                moved, result = tie(moved, work(*operands))
                done.append(result)
            arrived = tuple([value] for value in moved)


def ctx_fetch(part, axis):
    if lax.axis_size("ctx") != 2:
        return lax.all_gather(part, "ctx", axis=axis, tiled=True)
    return lax.ppermute(part, "ctx", [(0, 1), (1, 0)])


def ctx_join(part, other, axis):
    if lax.axis_size("ctx") != 2:
        return other
    return lax.dynamic_update_slice_in_dim(
        jnp.concatenate([other, other], axis=axis),
        part,
        lax.axis_index("ctx") * part.shape[axis],
        axis,
    )


def ctx_gather(part, axis):
    return ctx_join(part, ctx_fetch(part, axis), axis)


def ctx_pair_part(which):
    return jnp.full((1,), which, jnp.int32)


def ctx_theirs(left, right, axis):
    if lax.axis_size("ctx") == 2:
        part = ctx_pair_part(1 - lax.axis_index("ctx"))
        return weight_grad(left, right, axis, part, jnp.bfloat16)
    return t_dot(left, right).astype(jnp.bfloat16)


def ctx_send(theirs, axis):
    if lax.axis_size("ctx") == 2:
        return lax.ppermute(theirs, "ctx", [(0, 1), (1, 0)])
    return lax.psum_scatter(theirs, "ctx", scatter_dimension=axis, tiled=True)


def ctx_total(left, right, axis, arrived):
    if lax.axis_size("ctx") == 2:
        part = ctx_pair_part(lax.axis_index("ctx"))
        return weight_grad(left, right, axis, part, jnp.float32, (arrived,))
    return arrived.astype(jnp.float32)


def on_device(
    block_input,
    attn_gain,
    query_weight,
    key_matrix,
    value_matrix,
    output_weight,
    ffn_gain,
    shared_gate,
    shared_up,
    shared_down,
    expert_gate,
    expert_up,
    expert_down,
    routes,
    route_weights,
    cotangent,
):
    input_rows = block_input[0].astype(jnp.float32)
    tokens = input_rows.shape[0]
    ctx_count = lax.axis_size("ctx")
    exp_count = lax.axis_size("exp")
    exp_index = lax.axis_index("exp")
    both = ("ctx", "exp")
    offset = lax.axis_index("ctx") * tokens
    offset_array = jnp.full((1,), offset, jnp.int32)
    tables = rope_tables(offset + jnp.arange(tokens, dtype=jnp.int32))
    key_tables = rope_tables(jnp.arange(ctx_count * tokens, dtype=jnp.int32))

    own_rows = shared_gate.shape[0]
    attn_in = jnp.concatenate([query_weight, key_matrix, value_matrix], axis=1)
    edge = attn_in.shape[1]
    own_weights = route_weights[0].T
    (weights_high,) = tie(own_weights.astype(jnp.bfloat16))
    weights_low = (own_weights - weights_high.astype(jnp.float32)).astype(jnp.bfloat16)
    routing = jnp.concatenate(
        [routes[0].T.astype(jnp.bfloat16), weights_high, weights_low], axis=0
    ).reshape(-1)
    routing_columns = -(-routing.shape[0] // (own_rows * 128)) * 128
    routing = jnp.pad(routing, (0, own_rows * routing_columns - routing.shape[0]))
    full_in = lax.all_gather(
        jnp.concatenate([attn_in, routing.reshape(own_rows, routing_columns)], axis=1),
        both,
        axis=0,
        tiled=True,
    )
    routing = lax.dynamic_slice(
        full_in,
        (lax.axis_index("ctx") * exp_count * own_rows, edge),
        (exp_count * own_rows, routing_columns),
    ).reshape(exp_count, own_rows * routing_columns)
    routing = routing[:, : 3 * TOP * tokens].reshape(exp_count, 3 * TOP, tokens)
    routing = routing.astype(jnp.float32)
    grad_low = cotangent[0]

    own_hidden = shared_down.shape[0]
    padded = -(-ctx_count * own_hidden // 256) * 256
    padded_own = padded // ctx_count
    shared_in = jnp.stack([shared_gate, shared_up]).reshape(
        2, own_rows, ctx_count, exp_count, own_hidden
    )
    shared_in = jnp.transpose(shared_in, (3, 1, 0, 2, 4)).reshape(
        exp_count, own_rows, 2 * ctx_count * own_hidden
    )
    shared_in = lax.all_to_all(shared_in, "exp", split_axis=0, concat_axis=0, tiled=True)
    shared_in = jnp.pad(
        shared_in.reshape(exp_count * own_rows, 2 * ctx_count, own_hidden),
        ((0, 0), (0, 0), (0, padded_own - own_hidden)),
    ).reshape(exp_count * own_rows, 2 * padded)
    shared_in = ctx_gather(shared_in, 0)
    shared_in_t = shared_in.T
    shared_out_w = ctx_gather(jnp.pad(shared_down, ((0, padded_own - own_hidden), (0, 0))), 0)

    capacity = tokens * TOP * 4 // (3 * exp_count)
    named = routing[:, :TOP] == exp_index.astype(jnp.float32)
    chosen = jnp.any(named, axis=1)
    token_weight = jnp.sum(
        jnp.where(named, routing[:, TOP : 2 * TOP] + routing[:, 2 * TOP :], 0.0), axis=1
    )
    upto = (jnp.arange(tokens)[:, None] <= jnp.arange(tokens)[None, :]).astype(jnp.bfloat16)
    slot = dot32(chosen.astype(jnp.bfloat16), upto).astype(jnp.int32) - 1
    slot = jnp.where(chosen, slot, -1)
    slot_rows = jnp.stack([slot.astype(jnp.float32), token_weight], axis=1)
    token_info = jnp.pad(
        jnp.stack([slot.astype(jnp.float32), token_weight], axis=2), ((0, 0), (0, 0), (0, 126))
    )

    inverse_one = rms_scale(input_rows)
    normed_one = (input_rows * inverse_one * attn_gain).astype(jnp.bfloat16)
    full_in, normed_one, shared_in, shared_in_t, shared_out_w = tie(
        full_in, normed_one, shared_in, shared_in_t, shared_out_w
    )
    output_weight, full_in = tie(output_weight, full_in)
    full_output = lax.all_gather(output_weight, both, axis=0, tiled=True)
    key_value = ctx_gather(
        project(normed_one, full_in, tables, QUERY_HEADS // KEY_VALUE_HEADS, 2, 1), 0
    )
    normed_one_t = normed_one.T
    query = project(normed_one, full_in, tables, 0, QUERY_HEADS // KEY_VALUE_HEADS, QUERY_HEADS)
    attended_low = attend(offset_array, query, key_value)

    full_output, gate_part, up_part, down_part = tie(
        full_output, expert_gate[0], expert_up[0], expert_down[0]
    )
    gate_w = ctx_gather(gate_part, 0)
    up_w = ctx_gather(up_part, 0)
    down_other = ctx_fetch(down_part, 1)

    middle = input_rows + dot32(attended_low, full_output)
    inverse_two = rms_scale(middle)
    normed_two = (middle * inverse_two * ffn_gain).astype(jnp.bfloat16)

    rows_all = lax.all_gather(normed_two, "exp", axis=0, tiled=True)
    rows_all, gate_w, up_w, grad_low, slot_rows, token_info = tie(
        rows_all, gate_w, up_w, grad_low, slot_rows, token_info
    )
    grad_all = lax.all_gather(grad_low, "exp", axis=0, tiled=True)

    def blocks(rows):
        return rows.reshape(exp_count, tokens, MODEL_WIDTH)

    def flat(rows):
        return rows.reshape(rows.shape[0] * rows.shape[1], rows.shape[2])

    received, shared_act, shared_slope = enter(slot_rows, blocks(rows_all), shared_in, capacity)
    received = flat(received)
    expert_act, expert_slope, expert_silu = expert_in(received, gate_w, up_w)
    expert_act, down_other = tie(expert_act, down_other)
    down_w = ctx_join(down_part, down_other, 1)
    expert_rows = dot32(expert_act, down_w).astype(jnp.bfloat16)

    def slots(rows):
        return rows.reshape(exp_count, capacity, rows.shape[1])

    pair = exp_count >= 4 and exp_count % 4 == 0 and ctx_count == 2

    def sum_over_exp(part):
        units = jnp.repeat(jnp.arange(exp_count, dtype=jnp.int32), 2)
        everything = part(units)[0].reshape(exp_count, 2, tokens, MODEL_WIDTH // 2)
        return lax.psum_scatter(
            jnp.swapaxes(everything, 1, 2).reshape(exp_count * tokens, MODEL_WIDTH),
            "exp",
            scatter_dimension=0,
            tiled=True,
        ).astype(jnp.float32)

    out_part = functools.partial(
        combine,
        info=token_info,
        rows=(slots(expert_rows),),
        act=shared_act,
        weight=shared_out_w,
        scaled=True,
    )
    shared_act = flat(shared_act)
    rings = []
    if pair:
        out_ring = ExpRing(out_part, jnp.bfloat16, (middle[None],))
        rings = [out_ring]
        out_ring.take(ring_step(rings, out_ring.late, out_ring.late_units[0]))
    grad_expert, shared_back = ring_step(
        rings,
        lambda *operands: enter_back(*operands, capacity),
        slot_rows,
        blocks(grad_all),
        shared_out_w,
        shared_slope,
    )
    grad_expert = flat(grad_expert)
    grad_eu = ()
    for half in range(2):
        grad_eu = ring_step(
            rings,
            lambda *operands: expert_back(*operands[:4], half, operands[4:]),
            grad_expert,
            down_w,
            expert_slope,
            expert_silu,
            *grad_eu,
        )
    grad_eg, grad_eu = grad_eu
    pieces = [(), ()]
    for column_half, half in ((0, 0), (0, 1), (1, 0), (1, 1)):
        if (column_half, half) == (1, 1):
            rings = []
        piece = ring_step(
            rings,
            lambda *operands: expert_grad_rows(*operands[:4], column_half, half, operands[4:]),
            grad_eg,
            grad_eu,
            gate_w,
            up_w,
            *pieces[column_half],
        )
        pieces[column_half] = (piece,)
    grad_rows = [slots(piece) for (piece,) in pieces]

    grad_part = functools.partial(
        combine,
        info=token_info,
        rows=tuple(grad_rows),
        act=shared_back,
        weight=shared_in_t,
        scaled=False,
    )
    shared_back = flat(shared_back)
    theirs = lambda axis: lambda left, right: ctx_theirs(left, right, axis)
    total = lambda axis: lambda left, right, arrived: ctx_total(left, right, axis, arrived)
    if pair:
        output = out_ring.finish()
        grad_ring = ExpRing(grad_part, jnp.float32, late_from=(4, 6))
        rings = [grad_ring]
    else:
        output = (middle + sum_over_exp(out_part)).astype(jnp.bfloat16)

    def theirs_and_late(which, *operands):
        if not pair:
            return ring_step(rings, theirs(0), *operands)
        result, late = ring_step(
            rings,
            lambda units, *operands: (theirs(0)(*operands), grad_ring.late(units)),
            grad_ring.late_units[which],
            *operands,
        )
        grad_ring.take(late)
        return result

    gate_theirs = theirs_and_late(0, received, grad_eg)
    gate_arrived = ctx_send(gate_theirs, 0)
    up_theirs = theirs_and_late(1, received, grad_eu)
    up_arrived = ctx_send(up_theirs, 0)
    down_theirs = ring_step(rings, theirs(1), expert_act, grad_expert)
    down_arrived = ctx_send(down_theirs, 1)
    shared_in_theirs, shared_down_theirs = ring_step(
        rings,
        lambda a, b, c, d: (ctx_theirs(a, b, 0), ctx_theirs(c, d, 0)),
        rows_all,
        shared_back,
        shared_act,
        grad_all,
    )
    shared_in_arrived = ctx_send(shared_in_theirs, 0)
    shared_down_arrived = ctx_send(shared_down_theirs, 0)
    expert_gate_grad = ring_step(rings, total(0), received, grad_eg, gate_arrived)[None]
    if pair:
        ring_step(rings, lambda: ())
    expert_up_grad = ring_step(rings, total(0), received, grad_eu, up_arrived)[None]
    if pair:
        grad_two = grad_ring.finish()
    else:
        grad_two = sum_over_exp(grad_part)
    grad_two, down_arrived = tie(grad_two, down_arrived)

    ffn_gain_term = jnp.sum(grad_two * middle * inverse_two, axis=0)
    gain_term = jnp.pad(ffn_gain_term[:, None], ((0, 0), (0, 127))).astype(jnp.bfloat16)
    grad_middle = grad_low.astype(jnp.float32) + norm_back(grad_two, middle, inverse_two, ffn_gain)
    grad_middle_low = grad_middle.astype(jnp.bfloat16)
    output_term = t_dot(grad_middle_low, attended_low).astype(jnp.bfloat16)
    if pair:
        output_sum = SpreadSum(output_term)
        attended_gradient = dot_t(grad_middle_low, full_output).astype(jnp.bfloat16)
    else:
        attended_gradient = dot_t(grad_middle_low, full_output).astype(jnp.bfloat16)
        sum_o = lax.psum_scatter(output_term, both, scatter_dimension=0, tiled=True)

    grad_query_raw, key_terms, value_terms = attend_back(
        offset_array, query, key_value, attended_gradient, tables, key_tables
    )
    key_value_grad = jnp.concatenate([key_terms, value_terms], axis=1)
    if pair:
        own = lax.dynamic_slice_in_dim(key_value_grad, offset, tokens, axis=0)
        other = lax.dynamic_slice_in_dim(key_value_grad, tokens - offset, tokens, axis=0)
        other, swapped = tie(other.astype(jnp.bfloat16), output_sum.arrived)
        key_value_raw = own + ctx_send(other, 0).astype(jnp.float32)
        swapped = output_sum.ctx_done(swapped)
    else:
        key_value_raw = ctx_send(key_value_grad.astype(jnp.bfloat16), 0)
    key_value_raw = key_value_raw.astype(jnp.bfloat16)
    in_term = qkv_grad(normed_one_t, grad_query_raw, key_value_raw, gain_term)
    grad_raw = jnp.concatenate(
        [grad_query_raw, key_value_raw, jnp.zeros((tokens, routing_columns), jnp.bfloat16)], axis=1
    )
    grad_one = dot_t(grad_raw, full_in)
    input_grad = grad_middle + norm_back(grad_one, input_rows, inverse_one, attn_gain)
    sum_in = lax.psum_scatter(in_term, both, scatter_dimension=0, tiled=True).astype(jnp.float32)
    own_gain = lax.dynamic_slice_in_dim(
        attn_gain, (lax.axis_index("ctx") * exp_count + exp_index) * own_rows, own_rows
    )
    attn_gain_grad = jnp.sum(sum_in[:, :edge] * attn_in.astype(jnp.float32), axis=1) / own_gain

    rest = [
        ((expert_act, grad_expert, down_arrived), total(1)),
        ((rows_all, shared_back, shared_in_arrived), total(0)),
        ((shared_act, grad_all, shared_down_arrived), total(0)),
    ]
    if pair:
        sum_o, rest = output_sum.finish(swapped, rest)
    else:
        rest = [work(*operands) for operands, work in rest]
    expert_down_grad = rest[0][None]
    shared_in_grad = rest[1].astype(jnp.bfloat16)
    sum_sd = rest[2][:own_hidden]
    shared_in_grad = lax.all_to_all(
        shared_in_grad.reshape(exp_count, own_rows, 2 * padded),
        "exp",
        split_axis=0,
        concat_axis=0,
        tiled=True,
    ).reshape(exp_count, own_rows, 2, ctx_count, padded_own)[..., :own_hidden]
    shared_in_grad = (
        jnp.transpose(shared_in_grad, (2, 1, 3, 0, 4))
        .reshape(2, own_rows, exp_count * ctx_count * own_hidden)
        .astype(jnp.float32)
    )
    return (
        output[None],
        input_grad[None],
        attn_gain_grad,
        sum_in[:, :QUERY_WIDTH],
        sum_in[:, QUERY_WIDTH : QUERY_WIDTH + KEY_WIDTH],
        sum_in[:, QUERY_WIDTH + KEY_WIDTH : edge],
        sum_o.astype(jnp.float32).T,
        sum_in[:, edge],
        shared_in_grad[0],
        shared_in_grad[1],
        sum_sd,
        expert_gate_grad,
        expert_up_grad,
        expert_down_grad,
    )


def solution(mesh):
    return jax.shard_map(
        on_device,
        mesh=mesh,
        in_specs=(
            P("exp", "ctx", None),
            P(),
            P(("ctx", "exp"), None),
            P(("ctx", "exp"), None),
            P(("ctx", "exp"), None),
            P(("ctx", "exp"), None),
            P(),
            P(("ctx", "exp"), None),
            P(("ctx", "exp"), None),
            P(("ctx", "exp"), None),
            P("exp", "ctx", None),
            P("exp", "ctx", None),
            P("exp", None, "ctx"),
            P("exp", "ctx", None),
            P("exp", "ctx", None),
            P("exp", "ctx", None),
        ),
        out_specs=(
            P("exp", "ctx", None),
            P("exp", "ctx", None),
            P(("ctx", "exp")),
            P(("ctx", "exp"), None),
            P(("ctx", "exp"), None),
            P(("ctx", "exp"), None),
            P(None, ("ctx", "exp")),
            P(("ctx", "exp")),
            P(("ctx", "exp"), None),
            P(("ctx", "exp"), None),
            P(("ctx", "exp"), None),
            P("exp", "ctx", None),
            P("exp", "ctx", None),
            P("exp", None, "ctx"),
        ),
        check_vma=False,
    )
```

```python
import functools

import jax
import jax.numpy as jnp
import numpy as np
from jax import lax
from jax.experimental import pallas as pl
from jax.experimental.pallas import tpu as pltpu
from jax.sharding import PartitionSpec as P

MODEL_WIDTH = 2560
QUERY_HEADS = 20
KEY_VALUE_HEADS = 4
HEAD_SIZE = 128
TOP = 6
GROUP = QUERY_HEADS // KEY_VALUE_HEADS
QUERY_WIDTH = QUERY_HEADS * HEAD_SIZE
KEY_WIDTH = KEY_VALUE_HEADS * HEAD_SIZE
KERNEL_VMEM = 56 * 1024 * 1024
COMBINE_VMEM = 60 * 1024 * 1024


norm_eps = 1e-05
rope_base = 500000.0
causal_masked_score = -1e30


def rope_tables(token_positions):
    half_width = HEAD_SIZE // 2
    frequency = rope_base ** (-(jnp.arange(half_width, dtype=jnp.float32) * 2.0 / HEAD_SIZE))
    angles = token_positions[:, None].astype(jnp.float32) * frequency[None, :]
    cosine, sine = jnp.cos(angles), jnp.sin(angles)
    return (
        jnp.concatenate([cosine, cosine], axis=1),
        jnp.concatenate([-sine, sine], axis=1),
    )


def rms_scale(value_rows_all):
    return lax.rsqrt(jnp.mean(value_rows_all * value_rows_all, axis=-1, keepdims=True) + norm_eps)


def norm_back(grad_normed, source, inverse, gain_vector):
    scaled = grad_normed * gain_vector
    return inverse * scaled - source * inverse**3 * jnp.mean(
        scaled * source, axis=-1, keepdims=True
    )


def dot32(left, right):
    return jnp.dot(left, right, preferred_element_type=jnp.float32)


def dot_t(left, right):
    return lax.dot_general(
        left, right, (((1,), (1,)), ((), ())), preferred_element_type=jnp.float32
    )


def t_dot(left, right):
    return lax.dot_general(
        left, right, (((0,), (0,)), ((), ())), preferred_element_type=jnp.float32
    )


def tie(*values):
    return lax.optimization_barrier(values)


def kernel_params(limit=KERNEL_VMEM):
    return pltpu.CompilerParams(vmem_limit_bytes=limit)


def cost(flops, bytes_accessed, transcendentals=0):
    return pl.CostEstimate(
        flops=int(flops), bytes_accessed=int(bytes_accessed), transcendentals=int(transcendentals)
    )


def turn(values, cosine, sine):
    return values * cosine + pltpu.roll(values, HEAD_SIZE // 2, 1) * sine


def project_kernel(plain_from, rows_ref, weight_ref, cos_ref, sin_ref, out_ref):
    product = dot32(rows_ref[...], weight_ref[...])
    plain = pl.program_id(0) >= plain_from
    cosine = jnp.where(plain, 1.0, cos_ref[...])
    sine = jnp.where(plain, 0.0, sin_ref[...])
    for head in range(product.shape[1] // HEAD_SIZE):
        lanes = slice(head * HEAD_SIZE, (head + 1) * HEAD_SIZE)
        out_ref[:, lanes] = turn(product[:, lanes], cosine, sine).astype(jnp.bfloat16)


def project(rows, weight, tables, first_block, blocks, plain_from):
    count = rows.shape[0]
    return pl.pallas_call(
        functools.partial(project_kernel, plain_from),
        grid=(blocks,),
        in_specs=[
            pl.BlockSpec(rows.shape, lambda j: (0, 0)),
            pl.BlockSpec((weight.shape[0], KEY_WIDTH), lambda j: (0, first_block + j)),
            pl.BlockSpec(tables[0].shape, lambda j: (0, 0)),
            pl.BlockSpec(tables[1].shape, lambda j: (0, 0)),
        ],
        out_specs=pl.BlockSpec((count, KEY_WIDTH), lambda j: (0, j)),
        out_shape=jax.ShapeDtypeStruct((count, blocks * KEY_WIDTH), jnp.bfloat16),
        compiler_params=kernel_params(),
        cost_estimate=cost(
            2 * count * weight.shape[0] * blocks * KEY_WIDTH,
            2 * weight.shape[0] * (blocks * KEY_WIDTH + count),
        ),
        name="project",
    )(rows, weight, *tables)


def attend_probs(offset, first_row, query, keys):
    scores = dot_t(query, keys) * HEAD_SIZE ** (-0.5)
    rows = lax.broadcasted_iota(jnp.int32, scores.shape, 0) + (offset + first_row)
    places = lax.broadcasted_iota(jnp.int32, scores.shape, 1)
    scores = jnp.where(rows >= places, scores, causal_masked_score)
    weights = jnp.exp(scores - jnp.max(scores, axis=1, keepdims=True))
    return weights * (1.0 / jnp.sum(weights, axis=1, keepdims=True))


def attend_kernel(tile, offset_ref, query_ref, key_ref, value_ref, out_ref):
    keys, values = key_ref[...], value_ref[...]
    for head in range(GROUP):
        lanes = slice(head * HEAD_SIZE, (head + 1) * HEAD_SIZE)
        for start in range(0, query_ref.shape[0], tile):
            rows = slice(start, start + tile)
            probs = attend_probs(offset_ref[0], start, query_ref[rows, lanes], keys)
            out_ref[rows, lanes] = dot32(probs.astype(jnp.bfloat16), values).astype(jnp.bfloat16)


def attend(offset, query, key_value):
    count, places = query.shape[0], key_value.shape[0]
    work = count * places * HEAD_SIZE * QUERY_HEADS
    return pl.pallas_call(
        functools.partial(attend_kernel, min(count, 256)),
        grid=(KEY_VALUE_HEADS,),
        in_specs=[
            pl.BlockSpec(memory_space=pltpu.SMEM),
            pl.BlockSpec((count, GROUP * HEAD_SIZE), lambda g: (0, g)),
            pl.BlockSpec((places, HEAD_SIZE), lambda g: (0, g)),
            pl.BlockSpec((places, HEAD_SIZE), lambda g: (0, KEY_VALUE_HEADS + g)),
        ],
        out_specs=pl.BlockSpec((count, GROUP * HEAD_SIZE), lambda g: (0, g)),
        out_shape=jax.ShapeDtypeStruct(query.shape, jnp.bfloat16),
        compiler_params=kernel_params(),
        cost_estimate=cost(4 * work, 4 * query.size + 2 * key_value.size, work // HEAD_SIZE),
        name="attend",
    )(offset, query, key_value, key_value)


def attend_back_kernel(
    tile,
    offset_ref,
    query_ref,
    key_ref,
    value_ref,
    grad_ref,
    cos_ref,
    sin_ref,
    key_cos_ref,
    key_sin_ref,
    query_out,
    key_out,
    value_out,
):
    scale = HEAD_SIZE ** (-0.5)
    keys, values = key_ref[...], value_ref[...]
    key_sum = jnp.zeros(keys.shape, jnp.float32)
    value_sum = jnp.zeros(values.shape, jnp.float32)
    for head in range(GROUP):
        lanes = slice(head * HEAD_SIZE, (head + 1) * HEAD_SIZE)
        for start in range(0, query_ref.shape[0], tile):
            rows = slice(start, start + tile)
            query, grad = query_ref[rows, lanes], grad_ref[rows, lanes]
            probs = attend_probs(offset_ref[0], start, query, keys)
            grad_probs = dot_t(grad, values)
            delta = jnp.sum(probs * grad_probs, axis=1, keepdims=True)
            grad_scores = (probs * (grad_probs - delta)).astype(jnp.bfloat16)
            query_grad = dot32(grad_scores, keys) * scale
            query_out[rows, lanes] = turn(
                query_grad, cos_ref[rows, :], -sin_ref[rows, :]
            ).astype(jnp.bfloat16)
            key_sum = key_sum + t_dot(grad_scores, query)
            value_sum = value_sum + t_dot(probs.astype(jnp.bfloat16), grad)
    key_out[...] = turn(key_sum * scale, key_cos_ref[...], -key_sin_ref[...])
    value_out[...] = value_sum


def attend_back(offset, query, key_value, grad, tables, key_tables):
    count, places = query.shape[0], key_value.shape[0]
    work = count * places * HEAD_SIZE * QUERY_HEADS
    heads = pl.BlockSpec((count, GROUP * HEAD_SIZE), lambda g: (0, g))
    table = pl.BlockSpec((count, HEAD_SIZE), lambda g: (0, 0))
    key_table = pl.BlockSpec((places, HEAD_SIZE), lambda g: (0, 0))
    key_heads = pl.BlockSpec((places, HEAD_SIZE), lambda g: (0, g))
    return pl.pallas_call(
        functools.partial(attend_back_kernel, min(count, 256)),
        grid=(KEY_VALUE_HEADS,),
        in_specs=[
            pl.BlockSpec(memory_space=pltpu.SMEM),
            heads,
            key_heads,
            pl.BlockSpec((places, HEAD_SIZE), lambda g: (0, KEY_VALUE_HEADS + g)),
            heads,
            table,
            table,
            key_table,
            key_table,
        ],
        out_specs=[heads, key_heads, key_heads],
        out_shape=[
            jax.ShapeDtypeStruct(query.shape, jnp.bfloat16),
            jax.ShapeDtypeStruct((places, KEY_WIDTH), jnp.float32),
            jax.ShapeDtypeStruct((places, KEY_WIDTH), jnp.float32),
        ],
        compiler_params=kernel_params(),
        cost_estimate=cost(
            10 * work, 6 * query.size + 6 * key_value.size, work // HEAD_SIZE
        ),
        name="attend_back",
    )(offset, query, key_value, key_value, grad, *tables, *key_tables)


def silu_parts(gate_val, up_val):
    sigmoid_val = jax.nn.sigmoid(gate_val)
    silu_val = gate_val * sigmoid_val
    slope = up_val * sigmoid_val * (1.0 + gate_val * (1.0 - sigmoid_val))
    return [part.astype(jnp.bfloat16) for part in (silu_val * up_val, slope, silu_val)]


def row_chunks(count):
    return [slice(start, start + min(count, 256)) for start in range(0, count, min(count, 256))]


def slot_match(slots, capacity):
    places = lax.broadcasted_iota(jnp.int32, (capacity, slots.shape[1]), 0).astype(jnp.float32)
    return slots == places


def enter_kernel(slot_ref, rows_ref, weight_ref, picked_ref, act_ref, slope_ref):
    hidden = act_ref.shape[2]
    for chunk in row_chunks(rows_ref.shape[1]):
        product = dot_t(rows_ref[0, chunk, :], weight_ref[...])
        act, slope, silu_val = silu_parts(product[:, :hidden], product[:, hidden:])
        act_ref[0, chunk, :] = act
        slope_ref[0, chunk, :hidden] = slope
        slope_ref[0, chunk, hidden:] = silu_val
    pick = jnp.where(slot_match(slot_ref[0, 0:1, :], picked_ref.shape[1]), 1.0, 0.0)
    picked_ref[0] = dot32(pick.astype(jnp.bfloat16), rows_ref[0]).astype(jnp.bfloat16)


def enter(slot_rows, rows, weight, capacity):
    count, tokens, width = rows.shape
    hidden = weight.shape[0] // 2
    block = lambda a, b: pl.BlockSpec((1, a, b), lambda i: (i, 0, 0))
    return pl.pallas_call(
        enter_kernel,
        grid=(count,),
        in_specs=[
            block(2, tokens),
            block(tokens, width),
            pl.BlockSpec(weight.shape, lambda i: (0, 0)),
        ],
        out_specs=[block(capacity, width), block(tokens, hidden), block(tokens, 2 * hidden)],
        out_shape=[
            jax.ShapeDtypeStruct((count, capacity, width), jnp.bfloat16),
            jax.ShapeDtypeStruct((count, tokens, hidden), jnp.bfloat16),
            jax.ShapeDtypeStruct((count, tokens, 2 * hidden), jnp.bfloat16),
        ],
        compiler_params=kernel_params(),
        cost_estimate=cost(
            2 * count * tokens * width * (capacity + 2 * hidden),
            2 * count * width * (tokens + capacity),
        ),
        name="enter",
    )(slot_rows, rows, weight)


def enter_back_kernel(slot_ref, rows_ref, weight_ref, slope_ref, picked_ref, grad_ref):
    rows = rows_ref[0]
    hidden = weight_ref.shape[0]
    for chunk in row_chunks(rows_ref.shape[1]):
        product = dot_t(rows_ref[0, chunk, :], weight_ref[...])
        for lanes in (slice(0, hidden), slice(hidden, 2 * hidden)):
            slope = slope_ref[0, chunk, lanes].astype(jnp.float32)
            grad_ref[0, chunk, lanes] = (product * slope).astype(jnp.bfloat16)
    match = slot_match(slot_ref[0, 0:1, :], picked_ref.shape[1])
    slot_weight = jnp.sum(jnp.where(match, slot_ref[0, 1:2, :], 0.0), axis=1, keepdims=True)
    pick = jnp.where(match, 1.0, 0.0).astype(jnp.bfloat16)
    picked_ref[0] = (dot32(pick, rows) * slot_weight).astype(jnp.bfloat16)


def enter_back(slot_rows, rows, weight, slope, capacity):
    count, tokens, width = rows.shape
    hidden = weight.shape[0]
    block = lambda a, b: pl.BlockSpec((1, a, b), lambda i: (i, 0, 0))
    return pl.pallas_call(
        enter_back_kernel,
        grid=(count,),
        in_specs=[
            block(2, tokens),
            block(tokens, width),
            pl.BlockSpec(weight.shape, lambda i: (0, 0)),
            block(tokens, 2 * hidden),
        ],
        out_specs=[block(capacity, width), block(tokens, 2 * hidden)],
        out_shape=[
            jax.ShapeDtypeStruct((count, capacity, width), jnp.bfloat16),
            jax.ShapeDtypeStruct((count, tokens, 2 * hidden), jnp.bfloat16),
        ],
        compiler_params=kernel_params(),
        cost_estimate=cost(
            2 * count * tokens * width * (capacity + hidden),
            2 * count * width * (tokens + capacity),
        ),
        name="enter_back",
    )(slot_rows, rows, weight, slope)


def expert_in_kernel(rows_ref, gate_ref, up_ref, act_ref, slope_ref, silu_ref):
    for chunk in row_chunks(rows_ref.shape[0]):
        rows = rows_ref[chunk, :]
        parts = silu_parts(dot32(rows, gate_ref[...]), dot32(rows, up_ref[...]))
        act_ref[chunk, :], slope_ref[chunk, :], silu_ref[chunk, :] = parts


def expert_in(rows, gate, up):
    count, width = rows.shape
    hidden = gate.shape[1]
    high, wide = min(count, 1024), 512
    weight = pl.BlockSpec((width, wide), lambda m, n: (0, n))
    out = pl.BlockSpec((high, wide), lambda m, n: (m, n))
    return pl.pallas_call(
        expert_in_kernel,
        grid=(count // high, hidden // wide),
        in_specs=[pl.BlockSpec((high, width), lambda m, n: (m, 0)), weight, weight],
        out_specs=[out] * 3,
        out_shape=[jax.ShapeDtypeStruct((count, hidden), jnp.bfloat16)] * 3,
        compiler_params=kernel_params(),
        cost_estimate=cost(4 * count * width * hidden, 2 * count * (width + 3 * hidden)),
        name="expert_in",
    )(rows, gate, up)


def expert_out_kernel(part_ref, act_ref, own_ref, other_ref, out_ref):
    for half, weight_ref in enumerate((own_ref, other_ref)):

        @pl.when(pl.program_id(0) == half)
        def _(weight_ref=weight_ref):
            out_ref[...] = dot32(act_ref[...], weight_ref[...]).astype(jnp.bfloat16)


def expert_out(parts, act, own, other):
    count, hidden = act.shape
    half = own.shape[1]
    high = min(count, 1024)
    whole = pl.BlockSpec((hidden, half), lambda h, m, p: (0, 0))
    return pl.pallas_call(
        expert_out_kernel,
        grid_spec=pltpu.PrefetchScalarGridSpec(
            num_scalar_prefetch=1,
            grid=(2, count // high),
            in_specs=[pl.BlockSpec((high, hidden), lambda h, m, p: (m, 0)), whole, whole],
            out_specs=pl.BlockSpec((high, half), lambda h, m, p: (m, p[h])),
        ),
        out_shape=jax.ShapeDtypeStruct((count, 2 * half), jnp.bfloat16),
        compiler_params=kernel_params(),
        cost_estimate=cost(4 * count * hidden * half, 2 * count * (2 * hidden + 2 * half)),
        name="expert_out",
    )(parts, act, own, other)


def expert_back_kernel(
    part_ref, own_rows_ref, other_rows_ref, own_ref, other_ref, slope_ref, silu_ref, *rest
):
    gate_out, up_out = rest[-2:]
    for chunk in row_chunks(own_rows_ref.shape[0]):
        product = dot_t(own_rows_ref[chunk, :], own_ref[...])
        product = product + dot_t(other_rows_ref[chunk, :], other_ref[...])
        slope = slope_ref[chunk, :].astype(jnp.float32)
        silu_val = silu_ref[chunk, :].astype(jnp.float32)
        gate_out[chunk, :] = (product * slope).astype(jnp.bfloat16)
        up_out[chunk, :] = (product * silu_val).astype(jnp.bfloat16)


def expert_back(parts, rows, own, other, slope, silu_val, half, earlier=()):
    count, width = rows.shape
    hidden = own.shape[0]
    high, wide = min(count // 2, 1024), 512
    first = half * (count // 2 // high)
    tile = pl.BlockSpec((high, wide), lambda m, n, p: (first + m, n))
    weight = pl.BlockSpec((wide, width // 2), lambda m, n, p: (n, 0))
    return pl.pallas_call(
        expert_back_kernel,
        grid_spec=pltpu.PrefetchScalarGridSpec(
            num_scalar_prefetch=1,
            grid=(count // 2 // high, hidden // wide),
            in_specs=[
                pl.BlockSpec((high, width // 2), lambda m, n, p: (first + m, p[0])),
                pl.BlockSpec((high, width // 2), lambda m, n, p: (first + m, p[1])),
                weight,
                weight,
                tile,
                tile,
            ]
            + [pl.BlockSpec(memory_space=pl.ANY)] * len(earlier),
            out_specs=[tile, tile],
        ),
        out_shape=[jax.ShapeDtypeStruct((count, hidden), jnp.bfloat16)] * 2,
        input_output_aliases={7 + i: i for i in range(len(earlier))},
        compiler_params=kernel_params(),
        cost_estimate=cost(count * width * hidden, count * (width + 4 * hidden)),
        name="expert_back",
    )(parts, rows, rows, own, other, slope, silu_val, *earlier)


def expert_rows_kernel(gate_grad_ref, up_grad_ref, gate_ref, up_ref, *rest):
    out_ref = rest[-1]
    total = dot_t(gate_grad_ref[...], gate_ref[...]) + dot_t(up_grad_ref[...], up_ref[...])
    out_ref[...] = total.astype(jnp.bfloat16)


def expert_grad_rows(gate_grad, up_grad, gate, up, column_half, half, earlier=()):
    count, hidden = gate_grad.shape
    wide = gate.shape[0] // 2
    high = min(count // 2, 512)
    first = half * (count // 2 // high)
    grad = pl.BlockSpec((high, hidden), lambda m: (first + m, 0))
    weight = pl.BlockSpec((wide, hidden), lambda m: (column_half, 0))
    return pl.pallas_call(
        expert_rows_kernel,
        grid=(count // 2 // high,),
        in_specs=[grad, grad, weight, weight] + [pl.BlockSpec(memory_space=pl.ANY)] * len(earlier),
        out_specs=pl.BlockSpec((high, wide), lambda m: (first + m, 0)),
        out_shape=jax.ShapeDtypeStruct((count, wide), jnp.bfloat16),
        input_output_aliases={4: 0} if earlier else {},
        compiler_params=kernel_params(),
        cost_estimate=cost(
            2 * count * wide * hidden, (2 * count + 4 * wide) * hidden + count * wide
        ),
        name="expert_grad_rows",
    )(gate_grad, up_grad, gate, up, *earlier)


def qkv_grad_kernel(rows_ref, query_ref, key_value_ref, gain_ref, out_ref):
    rows = rows_ref[...]
    edge = query_ref.shape[1]
    end = edge + key_value_ref.shape[1]
    out_ref[:, :edge] = dot32(rows, query_ref[...]).astype(jnp.bfloat16)
    out_ref[:, edge:end] = dot32(rows, key_value_ref[...]).astype(jnp.bfloat16)
    out_ref[:, end:] = gain_ref[...]


def qkv_grad(rows_t, query_grad, key_value_grad, gain_term):
    width, count = rows_t.shape
    high = 256
    columns = query_grad.shape[1] + key_value_grad.shape[1] + gain_term.shape[1]
    whole = lambda array: pl.BlockSpec(array.shape, lambda m: (0, 0))
    return pl.pallas_call(
        qkv_grad_kernel,
        grid=(width // high,),
        in_specs=[
            pl.BlockSpec((high, count), lambda m: (m, 0)),
            whole(query_grad),
            whole(key_value_grad),
            pl.BlockSpec((high, gain_term.shape[1]), lambda m: (m, 0)),
        ],
        out_specs=pl.BlockSpec((high, columns), lambda m: (m, 0)),
        out_shape=jax.ShapeDtypeStruct((width, columns), jnp.bfloat16),
        compiler_params=kernel_params(),
        cost_estimate=cost(2 * width * count * columns, 2 * width * (columns + count)),
        name="qkv_grad",
    )(rows_t, query_grad, key_value_grad, gain_term)


def combine_kernel(scaled, pieces, arrivals, added, unit_ref, info_ref, act_ref, weight_ref, *rest):
    rows_refs, rest = rest[:pieces], rest[pieces:]
    arrived_refs, rest = rest[:arrivals], rest[arrivals:]
    added_refs, out_refs = rest[:added], rest[added:]
    slot = info_ref[0, :, 0:1]
    capacity = rows_refs[0].shape[1]
    lanes = lax.broadcasted_iota(jnp.int32, (slot.shape[0], capacity), 1).astype(jnp.float32)
    pick = jnp.where(slot == lanes, 1.0, 0.0).astype(jnp.bfloat16)

    def store(way):
        total = dot32(pick, rows_refs[way % pieces][0])
        if scaled:
            total = total * info_ref[0, :, 1:2]
        total = total + dot32(act_ref[0], weight_ref[...])
        for added_ref in added_refs:
            total = total + added_ref[0].astype(jnp.float32)
        if arrivals:
            total = total + arrived_refs[way][0].astype(jnp.float32)
        out_ref = out_refs[way % len(out_refs)]
        out_ref[0] = total.astype(out_ref.dtype)

    if pieces == 1 and not arrivals and len(out_refs) == 1:
        store(0)
        return
    for way in range(2):

        @pl.when(pl.program_id(0) % 2 == way)
        def _(way=way):
            store(way)


def combine(
    units, info, rows, act, weight, scaled, arrived=(), partner=(), own=(), kind="units",
    out_dtype=jnp.bfloat16,
):
    units, first, count = units
    tokens = info.shape[1]
    width, hidden = weight.shape[1], act.shape[2]
    capacity = rows[0].shape[1]
    columns = width // 2
    unit_block = lambda array: pl.BlockSpec((1,) + array.shape[1:], lambda i, u: (u[first + i], 0, 0))
    fixed = pl.BlockSpec((1, tokens, columns), lambda i, u: (0, 0, 0))
    half = pl.BlockSpec((1, tokens, columns), lambda i, u: (0, 0, i % 2))
    in_specs = [
        unit_block(info),
        unit_block(act),
        pl.BlockSpec((hidden, columns), lambda i, u: (0, i % 2)),
    ]
    block = (1, capacity, columns)
    if len(rows) == 1:
        in_specs.append(pl.BlockSpec(block, lambda i, u: (u[first + i], 0, i % 2)))
    else:
        in_specs.append(pl.BlockSpec(block, lambda i, u: (u[first + i - i % 2], 0, 0)))
        in_specs.append(pl.BlockSpec(block, lambda i, u: (u[first + i - i % 2 + 1], 0, 0)))
    in_specs += [fixed] * len(arrived)
    added = [array for array, _ in partner] + list(own)
    for _, at in partner:
        in_specs.append(pl.BlockSpec((1, tokens, columns), lambda i, u, at=at: (at + i, 0, 0)))
    in_specs += [half] * len(own)
    out_specs, out_shape = {
        "units": (
            [pl.BlockSpec((1, tokens, columns), lambda i, u: (i, 0, 0))],
            [(count, tokens, columns)],
        ),
        "ways": ([fixed, fixed], [(1, tokens, columns)] * 2),
        "tokens": ([half], [(1, tokens, width)]),
    }[kind]
    return pl.pallas_call(
        functools.partial(combine_kernel, scaled, len(rows), len(arrived), len(added)),
        grid_spec=pltpu.PrefetchScalarGridSpec(
            num_scalar_prefetch=1, grid=(count,), in_specs=in_specs, out_specs=out_specs
        ),
        out_shape=[jax.ShapeDtypeStruct(shape, out_dtype) for shape in out_shape],
        compiler_params=kernel_params(COMBINE_VMEM),
        cost_estimate=cost(
            2 * count * tokens * columns * (capacity + hidden),
            2 * count * columns * (capacity + tokens * (1 + len(added) + len(arrived) // 2)),
        ),
        name="combine",
    )(units, info, act, weight, *rows, *arrived, *added)


def weight_grad_kernel(part_ref, left_ref, right_ref, *rest):
    *arrived_refs, out_ref, sum_ref = rest
    step = pl.program_id(0)
    product = t_dot(left_ref[...], right_ref[...])

    @pl.when(step == 0)
    def _():
        sum_ref[...] = product

    @pl.when(step > 0)
    def _():
        sum_ref[...] += product

    @pl.when(step == pl.num_programs(0) - 1)
    def _():
        total = sum_ref[...]
        for arrived_ref in arrived_refs:
            total = total + arrived_ref[...].astype(jnp.float32)
        out_ref[...] = total.astype(out_ref.dtype)


def weight_grad(left, right, axis, part, out_dtype, arrived=()):
    count = left.shape[0]
    high = min(count, 1024)
    widths = [left.shape[1], right.shape[1]]
    widths[axis] //= 2
    at = (lambda k, p: (k, p[0]), lambda k, p: (k, 0))
    whole = pl.BlockSpec(tuple(widths), lambda k, p: (0, 0))
    return pl.pallas_call(
        weight_grad_kernel,
        grid_spec=pltpu.PrefetchScalarGridSpec(
            num_scalar_prefetch=1,
            grid=(count // high,),
            in_specs=[
                pl.BlockSpec((high, widths[0]), at[axis]),
                pl.BlockSpec((high, widths[1]), at[1 - axis]),
            ]
            + [whole] * len(arrived),
            out_specs=whole,
            scratch_shapes=[pltpu.VMEM(tuple(widths), jnp.float32)],
        ),
        out_shape=jax.ShapeDtypeStruct(tuple(widths), out_dtype),
        compiler_params=kernel_params(),
        cost_estimate=cost(
            2 * count * widths[0] * widths[1], 2 * count * sum(widths) + 4 * widths[0] * widths[1]
        ),
        name="weight_grad",
    )(part, left, right, *arrived)


def exp_ring(chips):
    if chips % 2:
        return list(range(chips))
    return list(range(0, chips, 2)) + list(range(chips - 1, 0, -2))


class ChipRing:
    def __init__(self):
        exp_count = lax.axis_size("exp")
        self.chips = exp_count // 2
        ring = exp_ring(self.chips)
        place_of = np.argsort(np.array(ring)).astype(np.int32)
        index = lax.axis_index("exp")
        self.core = index % 2
        self.place = jnp.asarray(place_of)[index // 2]
        self.ring = np.array(ring, np.int32)
        self.swap = [(i, i ^ 1) for i in range(exp_count)]
        self.ways = ([], [])
        for at in range(self.chips):
            for core in range(2):
                here, there = ring[at] * 2 + core, ring[(at + 1) % self.chips] * 2 + core
                self.ways[0].append((here, there))
                self.ways[1].append((there, here))

    def table(self):
        steps = np.arange(1, self.chips + 1)[None, :, None]
        places = np.arange(self.chips)[:, None, None]
        at = np.concatenate([places - steps, places + steps], axis=2) % self.chips
        return jnp.asarray(self.ring[at].reshape(self.chips, -1), jnp.int32)[self.place]

    def move(self, totals):
        return [lax.ppermute(total, "exp", way) for total, way in zip(totals, self.ways)]

    def swap_cores(self, value):
        return lax.ppermute(value, "exp", self.swap)


class ExpRing:
    def __init__(self, part, out_dtype, own=(), late_from=(4,)):
        self.part, self.out_dtype, self.own = part, out_dtype, own
        self.line = ChipRing()
        self.arrived, self.step = (), 0
        self.swapped, self.partner = [], []
        self.late_from = list(late_from) + [self.line.chips + 1]
        chips = self.line.table() * 2
        self.own_units, other = chips + self.line.core, chips + 1 - self.line.core
        first = part((other, 0, 2))[0]
        first, other = tie(first, other)
        self.take(first)
        second = part((other, 2, 2 * (self.late_from[0] - 2)))[0]
        second, self.late_units = tie(second, other)
        self.take(second)

    def take(self, total):
        self.partner += [(len(self.swapped), 2 * i) for i in range(total.shape[0] // 2)]
        self.swapped.append(self.line.swap_cores(total))

    def from_partner(self, step):
        group, at = self.partner[step - 1]
        return ((self.swapped[group], at),)

    def late(self, which, units):
        start, end = self.late_from[which : which + 2]
        return self.part((units, 2 * (start - 1), 2 * (end - start)))[0]

    def totals(self):
        self.step += 1
        return self.part(
            (self.own_units, 2 * (self.step - 1), 2),
            arrived=self.arrived,
            partner=self.from_partner(self.step),
            kind="ways",
        )

    def finish(self):
        return self.part(
            (self.own_units, 2 * (self.line.chips - 1), 2),
            arrived=self.arrived,
            partner=self.from_partner(self.line.chips),
            own=self.own,
            kind="tokens",
            out_dtype=self.out_dtype,
        )[0][0]


def ring_step(rings, work, *operands):
    totals = [ring.totals() for ring in rings]
    totals, operands = tie(totals, operands)
    moved = [ring.line.move(total) for ring, total in zip(rings, totals)]
    swapped = [ring.swapped for ring in rings]
    moved, swapped, result = tie(moved, swapped, work(*operands))
    for ring, arrived, ring.swapped in zip(rings, moved, swapped):
        ring.arrived = tuple(arrived)
    return result


class SpreadSum:
    def __init__(self, term):
        self.line = ChipRing()
        rows = term.shape[0] // (4 * self.line.chips)
        self.term = term.reshape(2, self.line.chips, 2, rows, term.shape[1])
        self.arrived = self.line.swap_cores(self.pick(self.term, 1 - self.line.core, 2))

    def pick(self, array, index, axis):
        return lax.dynamic_index_in_dim(array, index, axis, keepdims=False)

    def add(self, *values):
        return sum(value.astype(jnp.float32) for value in values)

    def cores_done(self):
        own = self.pick(self.term, self.line.core, 2)
        return self.add(own, self.arrived).astype(jnp.bfloat16)

    def ctx_start(self, value):
        self.value = value
        return ctx_send(self.pick(value, 1 - lax.axis_index("ctx"), 0), 0)

    def ctx_done(self, arrived):
        own = self.pick(self.value, lax.axis_index("ctx"), 0)
        return self.add(own, arrived).astype(jnp.bfloat16)

    def finish(self, value, pieces):
        done = []
        targets = self.line.table()
        columns = value.shape[2] // 2
        halves = [value[..., :columns], value[..., columns:]]
        arrived = ([], [])
        for step in range(1, self.line.chips + 1):
            totals = [
                self.add(self.pick(halves[way], targets[2 * (step - 1) + way], 0), *arrived[way])
                for way in range(2)
            ]
            if step == self.line.chips:
                return jnp.concatenate(totals, axis=1), done
            totals = [total.astype(jnp.bfloat16) for total in totals]
            if step <= len(pieces):
                operands, work = pieces[step - 1]
                totals, operands = tie(totals, operands)
            moved = self.line.move(totals)
            if step <= len(pieces):
                moved, result = tie(moved, work(*operands))
                done.append(result)
            arrived = tuple([value] for value in moved)


def ctx_fetch(part, axis):
    if lax.axis_size("ctx") != 2:
        return lax.all_gather(part, "ctx", axis=axis, tiled=True)
    return lax.ppermute(part, "ctx", [(0, 1), (1, 0)])


def ctx_join(part, other, axis):
    if lax.axis_size("ctx") != 2:
        return other
    return lax.dynamic_update_slice_in_dim(
        jnp.concatenate([other, other], axis=axis),
        part,
        lax.axis_index("ctx") * part.shape[axis],
        axis,
    )


def ctx_gather(part, axis):
    return ctx_join(part, ctx_fetch(part, axis), axis)


def ctx_pair_part(which):
    return jnp.full((1,), which, jnp.int32)


def ctx_theirs(left, right, axis):
    if lax.axis_size("ctx") == 2:
        part = ctx_pair_part(1 - lax.axis_index("ctx"))
        return weight_grad(left, right, axis, part, jnp.bfloat16)
    return t_dot(left, right).astype(jnp.bfloat16)


def ctx_send(theirs, axis):
    if lax.axis_size("ctx") == 2:
        return lax.ppermute(theirs, "ctx", [(0, 1), (1, 0)])
    return lax.psum_scatter(theirs, "ctx", scatter_dimension=axis, tiled=True)


def ctx_total(left, right, axis, arrived):
    if lax.axis_size("ctx") == 2:
        part = ctx_pair_part(lax.axis_index("ctx"))
        return weight_grad(left, right, axis, part, jnp.float32, (arrived,))
    return arrived.astype(jnp.float32)


def on_device(
    block_input,
    attn_gain,
    query_weight,
    key_matrix,
    value_matrix,
    output_weight,
    ffn_gain,
    shared_gate,
    shared_up,
    shared_down,
    expert_gate,
    expert_up,
    expert_down,
    routes,
    route_weights,
    cotangent,
):
    input_rows = block_input[0].astype(jnp.float32)
    tokens = input_rows.shape[0]
    ctx_count = lax.axis_size("ctx")
    exp_count = lax.axis_size("exp")
    exp_index = lax.axis_index("exp")
    both = ("ctx", "exp")
    offset = lax.axis_index("ctx") * tokens
    offset_array = jnp.full((1,), offset, jnp.int32)
    tables = rope_tables(offset + jnp.arange(tokens, dtype=jnp.int32))
    key_tables = rope_tables(jnp.arange(ctx_count * tokens, dtype=jnp.int32))

    own_rows = shared_gate.shape[0]
    attn_in = jnp.concatenate([query_weight, key_matrix, value_matrix], axis=1)
    edge = attn_in.shape[1]
    own_weights = route_weights[0].T
    (weights_high,) = tie(own_weights.astype(jnp.bfloat16))
    weights_low = (own_weights - weights_high.astype(jnp.float32)).astype(jnp.bfloat16)
    routing = jnp.concatenate(
        [routes[0].T.astype(jnp.bfloat16), weights_high, weights_low], axis=0
    ).reshape(-1)
    routing_columns = -(-routing.shape[0] // (own_rows * 128)) * 128
    routing = jnp.pad(routing, (0, own_rows * routing_columns - routing.shape[0]))
    full_in = lax.all_gather(
        jnp.concatenate([attn_in, routing.reshape(own_rows, routing_columns)], axis=1),
        both,
        axis=0,
        tiled=True,
    )
    routing = lax.dynamic_slice(
        full_in,
        (lax.axis_index("ctx") * exp_count * own_rows, edge),
        (exp_count * own_rows, routing_columns),
    ).reshape(exp_count, own_rows * routing_columns)
    routing = routing[:, : 3 * TOP * tokens].reshape(exp_count, 3 * TOP, tokens)
    routing = routing.astype(jnp.float32)
    grad_low = cotangent[0]

    own_hidden = shared_down.shape[0]
    padded = -(-ctx_count * own_hidden // 256) * 256
    padded_own = padded // ctx_count
    shared_in = jnp.stack([shared_gate, shared_up]).reshape(
        2, own_rows, ctx_count, exp_count, own_hidden
    )
    shared_in = jnp.transpose(shared_in, (3, 1, 0, 2, 4)).reshape(
        exp_count, own_rows, 2 * ctx_count * own_hidden
    )
    shared_in = lax.all_to_all(shared_in, "exp", split_axis=0, concat_axis=0, tiled=True)
    shared_in = jnp.pad(
        shared_in.reshape(exp_count * own_rows, 2 * ctx_count, own_hidden),
        ((0, 0), (0, 0), (0, padded_own - own_hidden)),
    ).reshape(exp_count * own_rows, 2 * padded)
    shared_in = ctx_gather(shared_in, 0)
    shared_in_t = shared_in.T
    shared_out_w = ctx_gather(jnp.pad(shared_down, ((0, padded_own - own_hidden), (0, 0))), 0)

    capacity = tokens * TOP * 4 // (3 * exp_count)
    named = routing[:, :TOP] == exp_index.astype(jnp.float32)
    chosen = jnp.any(named, axis=1)
    token_weight = jnp.sum(
        jnp.where(named, routing[:, TOP : 2 * TOP] + routing[:, 2 * TOP :], 0.0), axis=1
    )
    upto = (jnp.arange(tokens)[:, None] <= jnp.arange(tokens)[None, :]).astype(jnp.bfloat16)
    slot = dot32(chosen.astype(jnp.bfloat16), upto).astype(jnp.int32) - 1
    slot = jnp.where(chosen, slot, -1)
    slot_rows = jnp.stack([slot.astype(jnp.float32), token_weight], axis=1)
    token_info = jnp.pad(
        jnp.stack([slot.astype(jnp.float32), token_weight], axis=2), ((0, 0), (0, 0), (0, 126))
    )

    inverse_one = rms_scale(input_rows)
    normed_one = (input_rows * inverse_one * attn_gain).astype(jnp.bfloat16)
    full_in, normed_one, shared_in_t, shared_out_w = tie(
        full_in, normed_one, shared_in_t, shared_out_w
    )
    output_weight, full_in = tie(output_weight, full_in)
    full_output = lax.all_gather(output_weight, both, axis=0, tiled=True)
    key_value = ctx_gather(
        project(normed_one, full_in, tables, QUERY_HEADS // KEY_VALUE_HEADS, 2, 1), 0
    )
    normed_one_t = normed_one.T
    query = project(normed_one, full_in, tables, 0, QUERY_HEADS // KEY_VALUE_HEADS, QUERY_HEADS)
    attended_low = attend(offset_array, query, key_value)

    full_output, gate_part, up_part, down_part = tie(
        full_output, expert_gate[0], expert_up[0], expert_down[0]
    )
    gate_w = ctx_gather(gate_part, 0)
    up_w = ctx_gather(up_part, 0)
    down_other = ctx_fetch(down_part, 1)

    middle = input_rows + dot32(attended_low, full_output)
    inverse_two = rms_scale(middle)
    normed_two = (middle * inverse_two * ffn_gain).astype(jnp.bfloat16)

    rows_all = lax.all_gather(normed_two, "exp", axis=0, tiled=True)
    rows_all, gate_w, up_w, grad_low, slot_rows, token_info = tie(
        rows_all, gate_w, up_w, grad_low, slot_rows, token_info
    )
    grad_all = lax.all_gather(grad_low, "exp", axis=0, tiled=True)

    def blocks(rows):
        return rows.reshape(exp_count, tokens, MODEL_WIDTH)

    def flat(rows):
        return rows.reshape(rows.shape[0] * rows.shape[1], rows.shape[2])

    received, shared_act, shared_slope = enter(slot_rows, blocks(rows_all), shared_in_t, capacity)
    received = flat(received)
    expert_act, expert_slope, expert_silu = expert_in(received, gate_w, up_w)
    expert_act, down_other = tie(expert_act, down_other)
    if ctx_count == 2:
        down_parts = lax.axis_index("ctx") ^ jnp.arange(2, dtype=jnp.int32)
    else:
        down_parts = jnp.arange(2, dtype=jnp.int32)
        down_part = down_other[:, : MODEL_WIDTH // 2]
        down_other = down_other[:, MODEL_WIDTH // 2 :]
    expert_rows = expert_out(down_parts, expert_act, down_part, down_other)

    def slots(rows):
        return rows.reshape(exp_count, capacity, rows.shape[1])

    pair = exp_count >= 4 and exp_count % 4 == 0 and ctx_count == 2

    def sum_over_exp(part):
        units = jnp.repeat(jnp.arange(exp_count, dtype=jnp.int32), 2)
        everything = part((units, 0, 2 * exp_count))[0].reshape(exp_count, 2, tokens, MODEL_WIDTH // 2)
        return lax.psum_scatter(
            jnp.swapaxes(everything, 1, 2).reshape(exp_count * tokens, MODEL_WIDTH),
            "exp",
            scatter_dimension=0,
            tiled=True,
        ).astype(jnp.float32)

    out_part = functools.partial(
        combine,
        info=token_info,
        rows=(slots(expert_rows),),
        act=shared_act,
        weight=shared_out_w,
        scaled=True,
    )
    shared_act = flat(shared_act)
    rings = []
    if pair:
        out_ring = ExpRing(out_part, jnp.bfloat16, (middle[None],))
        rings = [out_ring]
    grad_expert, shared_back = ring_step(
        rings,
        lambda *operands: enter_back(*operands, capacity),
        slot_rows,
        blocks(grad_all),
        shared_out_w,
        shared_slope,
    )
    grad_expert = flat(grad_expert)
    grad_eu = ()
    out_late = (out_ring.late_units,) if pair else ()

    def late(work, here):
        if not (pair and here):
            return work
        return lambda units, *operands: (work(*operands), out_ring.late(0, units))

    for half in range(2):
        grad_eu = ring_step(
            rings,
            late(lambda *operands: expert_back(*operands[:6], half, operands[6:]), half == 0),
            *out_late,
            down_parts,
            grad_expert,
            down_part,
            down_other,
            expert_slope,
            expert_silu,
            *grad_eu,
        )
        if pair and half == 0:
            grad_eu, rest = grad_eu
            out_ring.take(rest)
            out_late = ()
    grad_eg, grad_eu = grad_eu
    pieces = [(), ()]
    theirs = lambda axis: lambda left, right: ctx_theirs(left, right, axis)
    total = lambda axis: lambda left, right, arrived: ctx_total(left, right, axis, arrived)
    for column_half, half in ((0, 0), (0, 1), (1, 0), (1, 1)):
        if (column_half, half) == (1, 1):
            down_theirs = ring_step(rings, theirs(1), expert_act, grad_expert)
            down_theirs, grad_eg, grad_eu = tie(down_theirs, grad_eg, grad_eu)
            down_arrived = ctx_send(down_theirs, 1)
            rings = []
        piece = ring_step(
            rings,
            lambda *operands: expert_grad_rows(*operands[:4], column_half, half, operands[4:]),
            grad_eg,
            grad_eu,
            gate_w,
            up_w,
            *pieces[column_half],
        )
        pieces[column_half] = (piece,)
    grad_rows = [slots(piece) for (piece,) in pieces]

    grad_part = functools.partial(
        combine,
        info=token_info,
        rows=tuple(grad_rows),
        act=shared_back,
        weight=shared_in_t,
        scaled=False,
    )
    shared_back = flat(shared_back)
    if pair:
        output = out_ring.finish()
        grad_ring = ExpRing(grad_part, jnp.float32, late_from=(9,))
        rings = [grad_ring]
    else:
        output = (middle + sum_over_exp(out_part)).astype(jnp.bfloat16)

    def theirs_and_late(which, *operands):
        if not pair:
            return ring_step(rings, theirs(0), *operands)
        return ring_step(rings, theirs(0), *operands)

    gate_theirs = theirs_and_late(0, received, grad_eg)
    gate_arrived = ctx_send(gate_theirs, 0)
    up_theirs = theirs_and_late(1, received, grad_eu)
    up_arrived = ctx_send(up_theirs, 0)
    shared_in_theirs, shared_down_theirs = ring_step(
        rings,
        lambda a, b, c, d: (ctx_theirs(a, b, 0), ctx_theirs(c, d, 0)),
        rows_all,
        shared_back,
        shared_act,
        grad_all,
    )
    shared_in_arrived = ctx_send(shared_in_theirs, 0)
    shared_down_arrived = ctx_send(shared_down_theirs, 0)
    expert_down_grad = ring_step(rings, total(1), expert_act, grad_expert, down_arrived)[None]
    expert_gate_grad = ring_step(rings, total(0), received, grad_eg, gate_arrived)[None]
    if pair:
        ring_step(rings, lambda: ())
    expert_up_grad = ring_step(rings, total(0), received, grad_eu, up_arrived)[None]
    if pair:
        grad_two = grad_ring.finish()
    else:
        grad_two = sum_over_exp(grad_part)
    ffn_gain_term = jnp.sum(grad_two * middle * inverse_two, axis=0)
    gain_term = jnp.pad(ffn_gain_term[:, None], ((0, 0), (0, 127))).astype(jnp.bfloat16)
    grad_middle = grad_low.astype(jnp.float32) + norm_back(grad_two, middle, inverse_two, ffn_gain)
    grad_middle_low = grad_middle.astype(jnp.bfloat16)
    middle_column = QUERY_WIDTH // 2 if pair else QUERY_WIDTH
    if pair:
        output_sum = SpreadSum(
            t_dot(grad_middle_low, attended_low[:, middle_column:]).astype(jnp.bfloat16)
        )
    output_term = t_dot(grad_middle_low, attended_low[:, :middle_column]).astype(jnp.bfloat16)
    sum_o = lax.psum_scatter(output_term, both, scatter_dimension=0, tiled=True)
    attended_gradient = dot_t(grad_middle_low, full_output).astype(jnp.bfloat16)
    if pair:
        sum_o = sum_o.astype(jnp.float32)
        swapped, attended_gradient = tie(output_sum.cores_done(), attended_gradient)
        swapped = output_sum.ctx_start(swapped)

    grad_query_raw, key_terms, value_terms = attend_back(
        offset_array, query, key_value, attended_gradient, tables, key_tables
    )
    if pair:
        grad_query_raw, key_terms, value_terms, swapped = tie(
            grad_query_raw, key_terms, value_terms, swapped
        )
        swapped = output_sum.ctx_done(swapped)
    key_value_grad = jnp.concatenate([key_terms, value_terms], axis=1)
    if pair:
        own = lax.dynamic_slice_in_dim(key_value_grad, offset, tokens, axis=0)
        other = lax.dynamic_slice_in_dim(key_value_grad, tokens - offset, tokens, axis=0)
        key_value_raw = own + ctx_send(other.astype(jnp.bfloat16), 0).astype(jnp.float32)
    else:
        key_value_raw = ctx_send(key_value_grad.astype(jnp.bfloat16), 0)
    key_value_raw = key_value_raw.astype(jnp.bfloat16)
    in_term = qkv_grad(normed_one_t, grad_query_raw, key_value_raw, gain_term)
    grad_raw = jnp.concatenate(
        [grad_query_raw, key_value_raw, jnp.zeros((tokens, routing_columns), jnp.bfloat16)], axis=1
    )
    grad_one = dot_t(grad_raw, full_in)
    input_grad = grad_middle + norm_back(grad_one, input_rows, inverse_one, attn_gain)
    sum_in = lax.psum_scatter(in_term, both, scatter_dimension=0, tiled=True).astype(jnp.float32)
    own_gain = lax.dynamic_slice_in_dim(
        attn_gain, (lax.axis_index("ctx") * exp_count + exp_index) * own_rows, own_rows
    )
    attn_gain_grad = jnp.sum(sum_in[:, :edge] * attn_in.astype(jnp.float32), axis=1) / own_gain

    rest = [
        ((rows_all, shared_back, shared_in_arrived), total(0)),
        ((shared_act, grad_all, shared_down_arrived), total(0)),
    ]
    if pair:
        other_sum, rest = output_sum.finish(swapped, rest)
        sum_o = jnp.concatenate([sum_o, other_sum], axis=1)
    else:
        rest = [work(*operands) for operands, work in rest]
    shared_in_grad = rest[0].astype(jnp.bfloat16)
    sum_sd = rest[1][:own_hidden]
    shared_in_grad = lax.all_to_all(
        shared_in_grad.reshape(exp_count, own_rows, 2 * padded),
        "exp",
        split_axis=0,
        concat_axis=0,
        tiled=True,
    ).reshape(exp_count, own_rows, 2, ctx_count, padded_own)[..., :own_hidden]
    shared_in_grad = (
        jnp.transpose(shared_in_grad, (2, 1, 3, 0, 4))
        .reshape(2, own_rows, exp_count * ctx_count * own_hidden)
        .astype(jnp.float32)
    )
    return (
        output[None],
        input_grad[None],
        attn_gain_grad,
        sum_in[:, :QUERY_WIDTH],
        sum_in[:, QUERY_WIDTH : QUERY_WIDTH + KEY_WIDTH],
        sum_in[:, QUERY_WIDTH + KEY_WIDTH : edge],
        sum_o.astype(jnp.float32).T,
        sum_in[:, edge],
        shared_in_grad[0],
        shared_in_grad[1],
        sum_sd,
        expert_gate_grad,
        expert_up_grad,
        expert_down_grad,
    )


def solution(mesh):
    return jax.shard_map(
        on_device,
        mesh=mesh,
        in_specs=(
            P("exp", "ctx", None),
            P(),
            P(("ctx", "exp"), None),
            P(("ctx", "exp"), None),
            P(("ctx", "exp"), None),
            P(("ctx", "exp"), None),
            P(),
            P(("ctx", "exp"), None),
            P(("ctx", "exp"), None),
            P(("ctx", "exp"), None),
            P("exp", "ctx", None),
            P("exp", "ctx", None),
            P("exp", None, "ctx"),
            P("exp", "ctx", None),
            P("exp", "ctx", None),
            P("exp", "ctx", None),
        ),
        out_specs=(
            P("exp", "ctx", None),
            P("exp", "ctx", None),
            P(("ctx", "exp")),
            P(("ctx", "exp"), None),
            P(("ctx", "exp"), None),
            P(("ctx", "exp"), None),
            P(None, ("ctx", "exp")),
            P(("ctx", "exp")),
            P(("ctx", "exp"), None),
            P(("ctx", "exp"), None),
            P(("ctx", "exp"), None),
            P("exp", "ctx", None),
            P("exp", "ctx", None),
            P("exp", None, "ctx"),
        ),
        check_vma=False,
    )
```

```python
import functools

import jax
import jax.numpy as jnp
import numpy as np
from jax import lax
from jax.experimental import pallas as pl
from jax.experimental.pallas import tpu as pltpu
from jax.sharding import PartitionSpec as P

MODEL_WIDTH = 2560
QUERY_HEADS = 20
KEY_VALUE_HEADS = 4
HEAD_SIZE = 128
TOP = 6
GROUP = QUERY_HEADS // KEY_VALUE_HEADS
QUERY_WIDTH = QUERY_HEADS * HEAD_SIZE
KEY_WIDTH = KEY_VALUE_HEADS * HEAD_SIZE
KERNEL_VMEM = 56 * 1024 * 1024
COMBINE_VMEM = 60 * 1024 * 1024


norm_eps = 1e-05
rope_base = 500000.0
causal_masked_score = -1e30


def rope_tables(token_positions):
    half_width = HEAD_SIZE // 2
    frequency = rope_base ** (-(jnp.arange(half_width, dtype=jnp.float32) * 2.0 / HEAD_SIZE))
    angles = token_positions[:, None].astype(jnp.float32) * frequency[None, :]
    cosine, sine = jnp.cos(angles), jnp.sin(angles)
    return (
        jnp.concatenate([cosine, cosine], axis=1),
        jnp.concatenate([-sine, sine], axis=1),
    )


def rms_scale(value_rows_all):
    return lax.rsqrt(jnp.mean(value_rows_all * value_rows_all, axis=-1, keepdims=True) + norm_eps)


def norm_back(grad_normed, source, inverse, gain_vector):
    scaled = grad_normed * gain_vector
    return inverse * scaled - source * inverse**3 * jnp.mean(
        scaled * source, axis=-1, keepdims=True
    )


def dot32(left, right):
    return jnp.dot(left, right, preferred_element_type=jnp.float32)


def dot_t(left, right):
    return lax.dot_general(
        left, right, (((1,), (1,)), ((), ())), preferred_element_type=jnp.float32
    )


def t_dot(left, right):
    return lax.dot_general(
        left, right, (((0,), (0,)), ((), ())), preferred_element_type=jnp.float32
    )


def tie(*values):
    return lax.optimization_barrier(values)


def kernel_params(limit=KERNEL_VMEM):
    return pltpu.CompilerParams(vmem_limit_bytes=limit)


def cost(flops, bytes_accessed, transcendentals=0):
    return pl.CostEstimate(
        flops=int(flops), bytes_accessed=int(bytes_accessed), transcendentals=int(transcendentals)
    )


def turn(values, cosine, sine):
    return values * cosine + pltpu.roll(values, HEAD_SIZE // 2, 1) * sine


def project_kernel(plain_from, rows_ref, weight_ref, cos_ref, sin_ref, out_ref):
    product = dot32(rows_ref[...], weight_ref[...])
    plain = pl.program_id(0) >= plain_from
    cosine = jnp.where(plain, 1.0, cos_ref[...])
    sine = jnp.where(plain, 0.0, sin_ref[...])
    for head in range(product.shape[1] // HEAD_SIZE):
        lanes = slice(head * HEAD_SIZE, (head + 1) * HEAD_SIZE)
        out_ref[:, lanes] = turn(product[:, lanes], cosine, sine).astype(jnp.bfloat16)


def project(rows, weight, tables, first_block, blocks, plain_from):
    count = rows.shape[0]
    return pl.pallas_call(
        functools.partial(project_kernel, plain_from),
        grid=(blocks,),
        in_specs=[
            pl.BlockSpec(rows.shape, lambda j: (0, 0)),
            pl.BlockSpec((weight.shape[0], KEY_WIDTH), lambda j: (0, first_block + j)),
            pl.BlockSpec(tables[0].shape, lambda j: (0, 0)),
            pl.BlockSpec(tables[1].shape, lambda j: (0, 0)),
        ],
        out_specs=pl.BlockSpec((count, KEY_WIDTH), lambda j: (0, j)),
        out_shape=jax.ShapeDtypeStruct((count, blocks * KEY_WIDTH), jnp.bfloat16),
        compiler_params=kernel_params(),
        cost_estimate=cost(
            2 * count * weight.shape[0] * blocks * KEY_WIDTH,
            2 * weight.shape[0] * (blocks * KEY_WIDTH + count),
        ),
        name="project",
    )(rows, weight, *tables)


def attend_probs(offset, first_row, query, keys):
    scores = dot_t(query, keys) * HEAD_SIZE ** (-0.5)
    rows = lax.broadcasted_iota(jnp.int32, scores.shape, 0) + (offset + first_row)
    places = lax.broadcasted_iota(jnp.int32, scores.shape, 1)
    scores = jnp.where(rows >= places, scores, causal_masked_score)
    weights = jnp.exp(scores - jnp.max(scores, axis=1, keepdims=True))
    return weights * (1.0 / jnp.sum(weights, axis=1, keepdims=True))


def attend_kernel(tile, offset_ref, query_ref, key_ref, value_ref, out_ref):
    keys, values = key_ref[...], value_ref[...]
    for head in range(GROUP):
        lanes = slice(head * HEAD_SIZE, (head + 1) * HEAD_SIZE)
        for start in range(0, query_ref.shape[0], tile):
            rows = slice(start, start + tile)
            probs = attend_probs(offset_ref[0], start, query_ref[rows, lanes], keys)
            out_ref[rows, lanes] = dot32(probs.astype(jnp.bfloat16), values).astype(jnp.bfloat16)


def attend(offset, query, key_value):
    count, places = query.shape[0], key_value.shape[0]
    work = count * places * HEAD_SIZE * QUERY_HEADS
    return pl.pallas_call(
        functools.partial(attend_kernel, min(count, 256)),
        grid=(KEY_VALUE_HEADS,),
        in_specs=[
            pl.BlockSpec(memory_space=pltpu.SMEM),
            pl.BlockSpec((count, GROUP * HEAD_SIZE), lambda g: (0, g)),
            pl.BlockSpec((places, HEAD_SIZE), lambda g: (0, g)),
            pl.BlockSpec((places, HEAD_SIZE), lambda g: (0, KEY_VALUE_HEADS + g)),
        ],
        out_specs=pl.BlockSpec((count, GROUP * HEAD_SIZE), lambda g: (0, g)),
        out_shape=jax.ShapeDtypeStruct(query.shape, jnp.bfloat16),
        compiler_params=kernel_params(),
        cost_estimate=cost(4 * work, 4 * query.size + 2 * key_value.size, work // HEAD_SIZE),
        name="attend",
    )(offset, query, key_value, key_value)


def attend_back_kernel(
    tile,
    offset_ref,
    query_ref,
    key_ref,
    value_ref,
    grad_ref,
    cos_ref,
    sin_ref,
    key_cos_ref,
    key_sin_ref,
    query_out,
    key_out,
    value_out,
):
    scale = HEAD_SIZE ** (-0.5)
    keys, values = key_ref[...], value_ref[...]
    key_sum = jnp.zeros(keys.shape, jnp.float32)
    value_sum = jnp.zeros(values.shape, jnp.float32)
    for head in range(GROUP):
        lanes = slice(head * HEAD_SIZE, (head + 1) * HEAD_SIZE)
        for start in range(0, query_ref.shape[0], tile):
            rows = slice(start, start + tile)
            query, grad = query_ref[rows, lanes], grad_ref[rows, lanes]
            probs = attend_probs(offset_ref[0], start, query, keys)
            grad_probs = dot_t(grad, values)
            delta = jnp.sum(probs * grad_probs, axis=1, keepdims=True)
            grad_scores = (probs * (grad_probs - delta)).astype(jnp.bfloat16)
            query_grad = dot32(grad_scores, keys) * scale
            query_out[rows, lanes] = turn(
                query_grad, cos_ref[rows, :], -sin_ref[rows, :]
            ).astype(jnp.bfloat16)
            key_sum = key_sum + t_dot(grad_scores, query)
            value_sum = value_sum + t_dot(probs.astype(jnp.bfloat16), grad)
    key_out[...] = turn(key_sum * scale, key_cos_ref[...], -key_sin_ref[...])
    value_out[...] = value_sum


def attend_back(offset, query, key_value, grad, tables, key_tables):
    count, places = query.shape[0], key_value.shape[0]
    work = count * places * HEAD_SIZE * QUERY_HEADS
    heads = pl.BlockSpec((count, GROUP * HEAD_SIZE), lambda g: (0, g))
    table = pl.BlockSpec((count, HEAD_SIZE), lambda g: (0, 0))
    key_table = pl.BlockSpec((places, HEAD_SIZE), lambda g: (0, 0))
    key_heads = pl.BlockSpec((places, HEAD_SIZE), lambda g: (0, g))
    return pl.pallas_call(
        functools.partial(attend_back_kernel, min(count, 256)),
        grid=(KEY_VALUE_HEADS,),
        in_specs=[
            pl.BlockSpec(memory_space=pltpu.SMEM),
            heads,
            key_heads,
            pl.BlockSpec((places, HEAD_SIZE), lambda g: (0, KEY_VALUE_HEADS + g)),
            heads,
            table,
            table,
            key_table,
            key_table,
        ],
        out_specs=[heads, key_heads, key_heads],
        out_shape=[
            jax.ShapeDtypeStruct(query.shape, jnp.bfloat16),
            jax.ShapeDtypeStruct((places, KEY_WIDTH), jnp.float32),
            jax.ShapeDtypeStruct((places, KEY_WIDTH), jnp.float32),
        ],
        compiler_params=kernel_params(),
        cost_estimate=cost(
            10 * work, 6 * query.size + 6 * key_value.size, work // HEAD_SIZE
        ),
        name="attend_back",
    )(offset, query, key_value, key_value, grad, *tables, *key_tables)


def silu_parts(gate_val, up_val):
    sigmoid_val = jax.nn.sigmoid(gate_val)
    silu_val = gate_val * sigmoid_val
    slope = up_val * sigmoid_val * (1.0 + gate_val * (1.0 - sigmoid_val))
    return [part.astype(jnp.bfloat16) for part in (silu_val * up_val, slope, silu_val)]


def row_chunks(count):
    return [slice(start, start + min(count, 256)) for start in range(0, count, min(count, 256))]


def slot_match(slots, capacity):
    places = lax.broadcasted_iota(jnp.int32, (capacity, slots.shape[1]), 0).astype(jnp.float32)
    return slots == places


def enter_kernel(slot_ref, rows_ref, weight_t_ref, picked_ref, act_ref, slope_ref, weight_ref):
    hidden = act_ref.shape[2]

    @pl.when(pl.program_id(0) == 0)
    def _():
        weight_ref[...] = weight_t_ref[...].T

    for chunk in row_chunks(rows_ref.shape[1]):
        product = dot32(rows_ref[0, chunk, :], weight_ref[...])
        act, slope, silu_val = silu_parts(product[:, :hidden], product[:, hidden:])
        act_ref[0, chunk, :] = act
        slope_ref[0, chunk, :hidden] = slope
        slope_ref[0, chunk, hidden:] = silu_val
    pick = jnp.where(slot_match(slot_ref[0, 0:1, :], picked_ref.shape[1]), 1.0, 0.0)
    picked_ref[0] = dot32(pick.astype(jnp.bfloat16), rows_ref[0]).astype(jnp.bfloat16)


def enter(slot_rows, rows, weight, capacity):
    count, tokens, width = rows.shape
    hidden = weight.shape[0] // 2
    block = lambda a, b: pl.BlockSpec((1, a, b), lambda i: (i, 0, 0))
    return pl.pallas_call(
        enter_kernel,
        grid=(count,),
        in_specs=[
            block(2, tokens),
            block(tokens, width),
            pl.BlockSpec(weight.shape, lambda i: (0, 0)),
        ],
        out_specs=[block(capacity, width), block(tokens, hidden), block(tokens, 2 * hidden)],
        out_shape=[
            jax.ShapeDtypeStruct((count, capacity, width), jnp.bfloat16),
            jax.ShapeDtypeStruct((count, tokens, hidden), jnp.bfloat16),
            jax.ShapeDtypeStruct((count, tokens, 2 * hidden), jnp.bfloat16),
        ],
        scratch_shapes=[pltpu.VMEM((width, 2 * hidden), jnp.bfloat16)],
        compiler_params=kernel_params(),
        cost_estimate=cost(
            2 * count * tokens * width * (capacity + 2 * hidden),
            2 * count * width * (tokens + capacity),
        ),
        name="enter",
    )(slot_rows, rows, weight)


def enter_back_kernel(slot_ref, rows_ref, weight_ref, slope_ref, picked_ref, grad_ref):
    rows = rows_ref[0]
    hidden = weight_ref.shape[0]
    for chunk in row_chunks(rows_ref.shape[1]):
        product = dot_t(rows_ref[0, chunk, :], weight_ref[...])
        for lanes in (slice(0, hidden), slice(hidden, 2 * hidden)):
            slope = slope_ref[0, chunk, lanes].astype(jnp.float32)
            grad_ref[0, chunk, lanes] = (product * slope).astype(jnp.bfloat16)
    match = slot_match(slot_ref[0, 0:1, :], picked_ref.shape[1])
    slot_weight = jnp.sum(jnp.where(match, slot_ref[0, 1:2, :], 0.0), axis=1, keepdims=True)
    pick = jnp.where(match, 1.0, 0.0).astype(jnp.bfloat16)
    picked_ref[0] = (dot32(pick, rows) * slot_weight).astype(jnp.bfloat16)


def enter_back(slot_rows, rows, weight, slope, capacity):
    count, tokens, width = rows.shape
    hidden = weight.shape[0]
    block = lambda a, b: pl.BlockSpec((1, a, b), lambda i: (i, 0, 0))
    return pl.pallas_call(
        enter_back_kernel,
        grid=(count,),
        in_specs=[
            block(2, tokens),
            block(tokens, width),
            pl.BlockSpec(weight.shape, lambda i: (0, 0)),
            block(tokens, 2 * hidden),
        ],
        out_specs=[block(capacity, width), block(tokens, 2 * hidden)],
        out_shape=[
            jax.ShapeDtypeStruct((count, capacity, width), jnp.bfloat16),
            jax.ShapeDtypeStruct((count, tokens, 2 * hidden), jnp.bfloat16),
        ],
        compiler_params=kernel_params(),
        cost_estimate=cost(
            2 * count * tokens * width * (capacity + hidden),
            2 * count * width * (tokens + capacity),
        ),
        name="enter_back",
    )(slot_rows, rows, weight, slope)


def expert_in_kernel(rows_ref, gate_ref, up_ref, act_ref, slope_ref, silu_ref):
    for chunk in row_chunks(rows_ref.shape[0]):
        rows = rows_ref[chunk, :]
        parts = silu_parts(dot32(rows, gate_ref[...]), dot32(rows, up_ref[...]))
        act_ref[chunk, :], slope_ref[chunk, :], silu_ref[chunk, :] = parts


def expert_in(rows, gate, up):
    count, width = rows.shape
    hidden = gate.shape[1]
    high, wide = min(count, 1024), 512
    weight = pl.BlockSpec((width, wide), lambda m, n: (0, n))
    out = pl.BlockSpec((high, wide), lambda m, n: (m, n))
    return pl.pallas_call(
        expert_in_kernel,
        grid=(count // high, hidden // wide),
        in_specs=[pl.BlockSpec((high, width), lambda m, n: (m, 0)), weight, weight],
        out_specs=[out] * 3,
        out_shape=[jax.ShapeDtypeStruct((count, hidden), jnp.bfloat16)] * 3,
        compiler_params=kernel_params(),
        cost_estimate=cost(4 * count * width * hidden, 2 * count * (width + 3 * hidden)),
        name="expert_in",
    )(rows, gate, up)


def expert_out_kernel(part_ref, act_ref, own_ref, other_ref, out_ref):
    for half, weight_ref in enumerate((own_ref, other_ref)):

        @pl.when(pl.program_id(0) == half)
        def _(weight_ref=weight_ref):
            out_ref[...] = dot32(act_ref[...], weight_ref[...]).astype(jnp.bfloat16)


def expert_out(parts, act, own, other):
    count, hidden = act.shape
    half = own.shape[1]
    high = min(count, 1024)
    whole = pl.BlockSpec((hidden, half), lambda h, m, p: (0, 0))
    return pl.pallas_call(
        expert_out_kernel,
        grid_spec=pltpu.PrefetchScalarGridSpec(
            num_scalar_prefetch=1,
            grid=(2, count // high),
            in_specs=[pl.BlockSpec((high, hidden), lambda h, m, p: (m, 0)), whole, whole],
            out_specs=pl.BlockSpec((high, half), lambda h, m, p: (m, p[h])),
        ),
        out_shape=jax.ShapeDtypeStruct((count, 2 * half), jnp.bfloat16),
        compiler_params=kernel_params(),
        cost_estimate=cost(4 * count * hidden * half, 2 * count * (2 * hidden + 2 * half)),
        name="expert_out",
    )(parts, act, own, other)


def expert_back_kernel(
    part_ref, own_rows_ref, other_rows_ref, own_ref, other_ref, slope_ref, silu_ref, *rest
):
    gate_out, up_out = rest[-2:]
    for chunk in row_chunks(own_rows_ref.shape[0]):
        product = dot_t(own_rows_ref[chunk, :], own_ref[...])
        product = product + dot_t(other_rows_ref[chunk, :], other_ref[...])
        slope = slope_ref[chunk, :].astype(jnp.float32)
        silu_val = silu_ref[chunk, :].astype(jnp.float32)
        gate_out[chunk, :] = (product * slope).astype(jnp.bfloat16)
        up_out[chunk, :] = (product * silu_val).astype(jnp.bfloat16)


def expert_back(parts, rows, own, other, slope, silu_val, half, earlier=()):
    count, width = rows.shape
    hidden = own.shape[0]
    high, wide = min(count // 2, 1024), 512
    first = half * (count // 2 // high)
    tile = pl.BlockSpec((high, wide), lambda m, n, p: (first + m, n))
    weight = pl.BlockSpec((wide, width // 2), lambda m, n, p: (n, 0))
    return pl.pallas_call(
        expert_back_kernel,
        grid_spec=pltpu.PrefetchScalarGridSpec(
            num_scalar_prefetch=1,
            grid=(count // 2 // high, hidden // wide),
            in_specs=[
                pl.BlockSpec((high, width // 2), lambda m, n, p: (first + m, p[0])),
                pl.BlockSpec((high, width // 2), lambda m, n, p: (first + m, p[1])),
                weight,
                weight,
                tile,
                tile,
            ]
            + [pl.BlockSpec(memory_space=pl.ANY)] * len(earlier),
            out_specs=[tile, tile],
        ),
        out_shape=[jax.ShapeDtypeStruct((count, hidden), jnp.bfloat16)] * 2,
        input_output_aliases={7 + i: i for i in range(len(earlier))},
        compiler_params=kernel_params(),
        cost_estimate=cost(count * width * hidden, count * (width + 4 * hidden)),
        name="expert_back",
    )(parts, rows, rows, own, other, slope, silu_val, *earlier)


def expert_rows_kernel(gate_grad_ref, up_grad_ref, gate_ref, up_ref, *rest):
    out_ref = rest[-1]
    total = dot_t(gate_grad_ref[...], gate_ref[...]) + dot_t(up_grad_ref[...], up_ref[...])
    out_ref[...] = total.astype(jnp.bfloat16)


def expert_grad_rows(gate_grad, up_grad, gate, up, column_half, half, earlier=()):
    count, hidden = gate_grad.shape
    wide = gate.shape[0] // 2
    high = min(count // 2, 512)
    first = half * (count // 2 // high)
    grad = pl.BlockSpec((high, hidden), lambda m: (first + m, 0))
    weight = pl.BlockSpec((wide, hidden), lambda m: (column_half, 0))
    return pl.pallas_call(
        expert_rows_kernel,
        grid=(count // 2 // high,),
        in_specs=[grad, grad, weight, weight] + [pl.BlockSpec(memory_space=pl.ANY)] * len(earlier),
        out_specs=pl.BlockSpec((high, wide), lambda m: (first + m, 0)),
        out_shape=jax.ShapeDtypeStruct((count, wide), jnp.bfloat16),
        input_output_aliases={4: 0} if earlier else {},
        compiler_params=kernel_params(),
        cost_estimate=cost(
            2 * count * wide * hidden, (2 * count + 4 * wide) * hidden + count * wide
        ),
        name="expert_grad_rows",
    )(gate_grad, up_grad, gate, up, *earlier)


def qkv_grad_kernel(rows_ref, query_ref, key_value_ref, gain_ref, out_ref):
    rows = rows_ref[...]
    edge = query_ref.shape[1]
    end = edge + key_value_ref.shape[1]
    out_ref[:, :edge] = dot32(rows, query_ref[...]).astype(jnp.bfloat16)
    out_ref[:, edge:end] = dot32(rows, key_value_ref[...]).astype(jnp.bfloat16)
    out_ref[:, end:] = gain_ref[...]


def qkv_grad(rows_t, query_grad, key_value_grad, gain_term):
    width, count = rows_t.shape
    high = 256
    columns = query_grad.shape[1] + key_value_grad.shape[1] + gain_term.shape[1]
    whole = lambda array: pl.BlockSpec(array.shape, lambda m: (0, 0))
    return pl.pallas_call(
        qkv_grad_kernel,
        grid=(width // high,),
        in_specs=[
            pl.BlockSpec((high, count), lambda m: (m, 0)),
            whole(query_grad),
            whole(key_value_grad),
            pl.BlockSpec((high, gain_term.shape[1]), lambda m: (m, 0)),
        ],
        out_specs=pl.BlockSpec((high, columns), lambda m: (m, 0)),
        out_shape=jax.ShapeDtypeStruct((width, columns), jnp.bfloat16),
        compiler_params=kernel_params(),
        cost_estimate=cost(2 * width * count * columns, 2 * width * (columns + count)),
        name="qkv_grad",
    )(rows_t, query_grad, key_value_grad, gain_term)


def rows_grad_kernel(left_ref, right_ref, out_ref):
    out_ref[...] = t_dot(left_ref[...], right_ref[...]).astype(jnp.bfloat16)


def rows_grad(left, right):
    count, high = left.shape
    wide = right.shape[1]
    return pl.pallas_call(
        rows_grad_kernel,
        grid=(high // 256,),
        in_specs=[
            pl.BlockSpec((count, 256), lambda m: (0, m)),
            pl.BlockSpec((count, wide), lambda m: (0, 0)),
        ],
        out_specs=pl.BlockSpec((256, wide), lambda m: (m, 0)),
        out_shape=jax.ShapeDtypeStruct((high, wide), jnp.bfloat16),
        compiler_params=kernel_params(),
        cost_estimate=cost(2 * count * high * wide, 2 * (count * (high + wide) + high * wide)),
        name="rows_grad",
    )(left, right)


def combine_kernel(scaled, pieces, arrivals, added, unit_ref, info_ref, act_ref, weight_ref, *rest):
    rows_refs, rest = rest[:pieces], rest[pieces:]
    arrived_refs, rest = rest[:arrivals], rest[arrivals:]
    added_refs, out_refs = rest[:added], rest[added:]
    slot = info_ref[0, :, 0:1]
    capacity = rows_refs[0].shape[1]
    lanes = lax.broadcasted_iota(jnp.int32, (slot.shape[0], capacity), 1).astype(jnp.float32)
    pick = jnp.where(slot == lanes, 1.0, 0.0).astype(jnp.bfloat16)

    def store(way):
        total = dot32(pick, rows_refs[way % pieces][0])
        if scaled:
            total = total * info_ref[0, :, 1:2]
        total = total + dot32(act_ref[0], weight_ref[...])
        for added_ref in added_refs:
            total = total + added_ref[0].astype(jnp.float32)
        if arrivals:
            total = total + arrived_refs[way][0].astype(jnp.float32)
        out_ref = out_refs[way % len(out_refs)]
        out_ref[0] = total.astype(out_ref.dtype)

    if pieces == 1 and not arrivals and len(out_refs) == 1:
        store(0)
        return
    for way in range(2):

        @pl.when(pl.program_id(0) % 2 == way)
        def _(way=way):
            store(way)


def combine(
    units, info, rows, act, weight, scaled, arrived=(), partner=(), own=(), kind="units",
    out_dtype=jnp.bfloat16,
):
    units, first, count = units
    tokens = info.shape[1]
    width, hidden = weight.shape[1], act.shape[2]
    capacity = rows[0].shape[1]
    columns = width // 2
    unit_block = lambda array: pl.BlockSpec((1,) + array.shape[1:], lambda i, u: (u[first + i], 0, 0))
    fixed = pl.BlockSpec((1, tokens, columns), lambda i, u: (0, 0, 0))
    half = pl.BlockSpec((1, tokens, columns), lambda i, u: (0, 0, i % 2))
    in_specs = [
        unit_block(info),
        unit_block(act),
        pl.BlockSpec((hidden, columns), lambda i, u: (0, i % 2)),
    ]
    block = (1, capacity, columns)
    if len(rows) == 1:
        in_specs.append(pl.BlockSpec(block, lambda i, u: (u[first + i], 0, i % 2)))
    else:
        in_specs.append(pl.BlockSpec(block, lambda i, u: (u[first + i - i % 2], 0, 0)))
        in_specs.append(pl.BlockSpec(block, lambda i, u: (u[first + i - i % 2 + 1], 0, 0)))
    in_specs += [fixed] * len(arrived)
    added = [array for array, _ in partner] + list(own)
    for _, at in partner:
        in_specs.append(pl.BlockSpec((1, tokens, columns), lambda i, u, at=at: (at + i, 0, 0)))
    in_specs += [half] * len(own)
    out_specs, out_shape = {
        "units": (
            [pl.BlockSpec((1, tokens, columns), lambda i, u: (i, 0, 0))],
            [(count, tokens, columns)],
        ),
        "ways": ([fixed, fixed], [(1, tokens, columns)] * 2),
        "tokens": ([half], [(1, tokens, width)]),
    }[kind]
    return pl.pallas_call(
        functools.partial(combine_kernel, scaled, len(rows), len(arrived), len(added)),
        grid_spec=pltpu.PrefetchScalarGridSpec(
            num_scalar_prefetch=1, grid=(count,), in_specs=in_specs, out_specs=out_specs
        ),
        out_shape=[jax.ShapeDtypeStruct(shape, out_dtype) for shape in out_shape],
        compiler_params=kernel_params(COMBINE_VMEM),
        cost_estimate=cost(
            2 * count * tokens * columns * (capacity + hidden),
            2 * count * columns * (capacity + tokens * (1 + len(added) + len(arrived) // 2)),
        ),
        name="combine",
    )(units, info, act, weight, *rows, *arrived, *added)


def weight_grad_kernel(part_ref, left_ref, right_ref, *rest):
    *arrived_refs, out_ref, sum_ref = rest
    step = pl.program_id(0)
    last = pl.num_programs(0) - 1

    @pl.when(step == 0)
    def _():
        for chunk in row_chunks(sum_ref.shape[0]):
            sum_ref[chunk, :] = t_dot(left_ref[:, chunk], right_ref[...])

    @pl.when((step > 0) & (step < last))
    def _():
        for chunk in row_chunks(sum_ref.shape[0]):
            sum_ref[chunk, :] += t_dot(left_ref[:, chunk], right_ref[...])

    @pl.when((step > 0) & (step == last))
    def _():
        for chunk in row_chunks(sum_ref.shape[0]):
            total = sum_ref[chunk, :] + t_dot(left_ref[:, chunk], right_ref[...])
            for arrived_ref in arrived_refs:
                total = total + arrived_ref[chunk, :].astype(jnp.float32)
            out_ref[chunk, :] = total.astype(out_ref.dtype)


def weight_grad(left, right, axis, part, out_dtype, arrived=()):
    count = left.shape[0]
    high = min(count // 2, 1024)
    widths = [left.shape[1], right.shape[1]]
    widths[axis] //= 2
    at = (lambda k, p: (k, p[0]), lambda k, p: (k, 0))
    whole = pl.BlockSpec(tuple(widths), lambda k, p: (0, 0))
    return pl.pallas_call(
        weight_grad_kernel,
        grid_spec=pltpu.PrefetchScalarGridSpec(
            num_scalar_prefetch=1,
            grid=(count // high,),
            in_specs=[
                pl.BlockSpec((high, widths[0]), at[axis]),
                pl.BlockSpec((high, widths[1]), at[1 - axis]),
            ]
            + [whole] * len(arrived),
            out_specs=whole,
            scratch_shapes=[pltpu.VMEM(tuple(widths), jnp.float32)],
        ),
        out_shape=jax.ShapeDtypeStruct(tuple(widths), out_dtype),
        compiler_params=kernel_params(),
        cost_estimate=cost(
            2 * count * widths[0] * widths[1], 2 * count * sum(widths) + 4 * widths[0] * widths[1]
        ),
        name="weight_grad",
    )(part, left, right, *arrived)


def exp_ring(chips):
    if chips % 2:
        return list(range(chips))
    return list(range(0, chips, 2)) + list(range(chips - 1, 0, -2))


class ChipRing:
    def __init__(self):
        exp_count = lax.axis_size("exp")
        self.chips = exp_count // 2
        ring = exp_ring(self.chips)
        place_of = np.argsort(np.array(ring)).astype(np.int32)
        index = lax.axis_index("exp")
        self.core = index % 2
        self.place = jnp.asarray(place_of)[index // 2]
        self.ring = np.array(ring, np.int32)
        self.swap = [(i, i ^ 1) for i in range(exp_count)]
        self.ways = ([], [])
        for at in range(self.chips):
            for core in range(2):
                here, there = ring[at] * 2 + core, ring[(at + 1) % self.chips] * 2 + core
                self.ways[0].append((here, there))
                self.ways[1].append((there, here))

    def table(self):
        steps = np.arange(1, self.chips + 1)[None, :, None]
        places = np.arange(self.chips)[:, None, None]
        at = np.concatenate([places - steps, places + steps], axis=2) % self.chips
        return jnp.asarray(self.ring[at].reshape(self.chips, -1), jnp.int32)[self.place]

    def move(self, totals):
        return [lax.ppermute(total, "exp", way) for total, way in zip(totals, self.ways)]

    def swap_cores(self, value):
        return lax.ppermute(value, "exp", self.swap)


class ExpRing:
    def __init__(self, part, out_dtype, own=(), late_from=(4,)):
        self.part, self.out_dtype, self.own = part, out_dtype, own
        self.line = ChipRing()
        self.arrived, self.step = (), 0
        self.swapped, self.partner = [], []
        self.late_from = list(late_from) + [self.line.chips + 1]
        chips = self.line.table() * 2
        self.own_units, other = chips + self.line.core, chips + 1 - self.line.core
        first = part((other, 0, 2))[0]
        first, other = tie(first, other)
        self.take(first)
        second = part((other, 2, 2 * (self.late_from[0] - 2)))[0]
        second, self.late_units = tie(second, other)
        second, self.swapped[0] = tie(second, self.swapped[0])
        self.take(second)

    def take(self, total):
        self.partner += [(len(self.swapped), 2 * i) for i in range(total.shape[0] // 2)]
        self.swapped.append(self.line.swap_cores(total))

    def from_partner(self, step):
        group, at = self.partner[step - 1]
        return ((self.swapped[group], at),)

    def late(self, which, units):
        start, end = self.late_from[which : which + 2]
        return self.part((units, 2 * (start - 1), 2 * (end - start)))[0]

    def totals(self):
        self.step += 1
        return self.part(
            (self.own_units, 2 * (self.step - 1), 2),
            arrived=self.arrived,
            partner=self.from_partner(self.step),
            kind="ways",
        )

    def finish(self):
        return self.part(
            (self.own_units, 2 * (self.line.chips - 1), 2),
            arrived=self.arrived,
            partner=self.from_partner(self.line.chips),
            own=self.own,
            kind="tokens",
            out_dtype=self.out_dtype,
        )[0][0]


def ring_step(rings, work, *operands):
    totals = [ring.totals() for ring in rings]
    totals, operands = tie(totals, operands)
    moved = [ring.line.move(total) for ring, total in zip(rings, totals)]
    swapped = [ring.swapped for ring in rings]
    moved, swapped, result = tie(moved, swapped, work(*operands))
    for ring, arrived, ring.swapped in zip(rings, moved, swapped):
        ring.arrived = tuple(arrived)
    return result


def ctx_fetch(part, axis):
    if lax.axis_size("ctx") != 2:
        return lax.all_gather(part, "ctx", axis=axis, tiled=True)
    return lax.ppermute(part, "ctx", [(0, 1), (1, 0)])


def ctx_join(part, other, axis):
    if lax.axis_size("ctx") != 2:
        return other
    return lax.dynamic_update_slice_in_dim(
        jnp.concatenate([other, other], axis=axis),
        part,
        lax.axis_index("ctx") * part.shape[axis],
        axis,
    )


def ctx_gather(part, axis):
    return ctx_join(part, ctx_fetch(part, axis), axis)


def ctx_pair_part(which):
    return jnp.full((1,), which, jnp.int32)


def ctx_theirs(left, right, axis):
    if lax.axis_size("ctx") == 2:
        part = ctx_pair_part(1 - lax.axis_index("ctx"))
        return weight_grad(left, right, axis, part, jnp.bfloat16)
    return t_dot(left, right).astype(jnp.bfloat16)


def ctx_send(theirs, axis):
    if lax.axis_size("ctx") == 2:
        return lax.ppermute(theirs, "ctx", [(0, 1), (1, 0)])
    return lax.psum_scatter(theirs, "ctx", scatter_dimension=axis, tiled=True)


def ctx_total(left, right, axis, arrived):
    if lax.axis_size("ctx") == 2:
        part = ctx_pair_part(lax.axis_index("ctx"))
        return weight_grad(left, right, axis, part, jnp.float32, (arrived,))
    return arrived.astype(jnp.float32)


def on_device(
    block_input,
    attn_gain,
    query_weight,
    key_matrix,
    value_matrix,
    output_weight,
    ffn_gain,
    shared_gate,
    shared_up,
    shared_down,
    expert_gate,
    expert_up,
    expert_down,
    routes,
    route_weights,
    cotangent,
):
    input_rows = block_input[0].astype(jnp.float32)
    tokens = input_rows.shape[0]
    ctx_count = lax.axis_size("ctx")
    exp_count = lax.axis_size("exp")
    exp_index = lax.axis_index("exp")
    both = ("ctx", "exp")
    offset = lax.axis_index("ctx") * tokens
    offset_array = jnp.full((1,), offset, jnp.int32)
    tables = rope_tables(offset + jnp.arange(tokens, dtype=jnp.int32))
    key_tables = rope_tables(jnp.arange(ctx_count * tokens, dtype=jnp.int32))

    own_rows = shared_gate.shape[0]
    attn_in = jnp.concatenate([query_weight, key_matrix, value_matrix], axis=1)
    edge = attn_in.shape[1]
    own_weights = route_weights[0].T
    (weights_high,) = tie(own_weights.astype(jnp.bfloat16))
    weights_low = (own_weights - weights_high.astype(jnp.float32)).astype(jnp.bfloat16)
    routing = jnp.concatenate(
        [routes[0].T.astype(jnp.bfloat16), weights_high, weights_low], axis=0
    ).reshape(-1)
    routing_columns = -(-routing.shape[0] // (own_rows * 128)) * 128
    routing = jnp.pad(routing, (0, own_rows * routing_columns - routing.shape[0]))
    full_in = lax.all_gather(
        jnp.concatenate([attn_in, routing.reshape(own_rows, routing_columns)], axis=1),
        both,
        axis=0,
        tiled=True,
    )
    routing = lax.dynamic_slice(
        full_in,
        (lax.axis_index("ctx") * exp_count * own_rows, edge),
        (exp_count * own_rows, routing_columns),
    ).reshape(exp_count, own_rows * routing_columns)
    routing = routing[:, : 3 * TOP * tokens].reshape(exp_count, 3 * TOP, tokens)
    routing = routing.astype(jnp.float32)
    grad_low = cotangent[0]

    own_hidden = shared_down.shape[0]
    padded = -(-ctx_count * own_hidden // 256) * 256
    padded_own = padded // ctx_count
    shared_in = jnp.stack([shared_gate, shared_up]).reshape(
        2, own_rows, ctx_count, exp_count, own_hidden
    )
    shared_in = jnp.transpose(shared_in, (3, 1, 0, 2, 4)).reshape(
        exp_count, own_rows, 2 * ctx_count * own_hidden
    )
    shared_in = lax.all_to_all(shared_in, "exp", split_axis=0, concat_axis=0, tiled=True)
    shared_in = jnp.pad(
        shared_in.reshape(exp_count * own_rows, 2 * ctx_count, own_hidden),
        ((0, 0), (0, 0), (0, padded_own - own_hidden)),
    ).reshape(exp_count * own_rows, 2 * padded)
    shared_in = ctx_gather(shared_in, 0)
    shared_in_t = shared_in.T
    shared_out_w = ctx_gather(jnp.pad(shared_down, ((0, padded_own - own_hidden), (0, 0))), 0)

    capacity = tokens * TOP * 4 // (3 * exp_count)
    named = routing[:, :TOP] == exp_index.astype(jnp.float32)
    chosen = jnp.any(named, axis=1)
    token_weight = jnp.sum(
        jnp.where(named, routing[:, TOP : 2 * TOP] + routing[:, 2 * TOP :], 0.0), axis=1
    )
    upto = (jnp.arange(tokens)[:, None] <= jnp.arange(tokens)[None, :]).astype(jnp.bfloat16)
    slot = dot32(chosen.astype(jnp.bfloat16), upto).astype(jnp.int32) - 1
    slot = jnp.where(chosen, slot, -1)
    slot_rows = jnp.stack([slot.astype(jnp.float32), token_weight], axis=1)
    token_info = jnp.pad(
        jnp.stack([slot.astype(jnp.float32), token_weight], axis=2), ((0, 0), (0, 0), (0, 126))
    )

    inverse_one = rms_scale(input_rows)
    normed_one = (input_rows * inverse_one * attn_gain).astype(jnp.bfloat16)
    full_in, normed_one, shared_in_t, shared_out_w = tie(
        full_in, normed_one, shared_in_t, shared_out_w
    )
    output_weight, full_in = tie(output_weight, full_in)
    full_output = lax.all_gather(output_weight, both, axis=0, tiled=True)
    key_value = ctx_gather(
        project(normed_one, full_in, tables, QUERY_HEADS // KEY_VALUE_HEADS, 2, 1), 0
    )
    normed_one_t = normed_one.T
    query = project(normed_one, full_in, tables, 0, QUERY_HEADS // KEY_VALUE_HEADS, QUERY_HEADS)
    attended_low = attend(offset_array, query, key_value)

    full_output, gate_part, up_part, down_part = tie(
        full_output, expert_gate[0], expert_up[0], expert_down[0]
    )
    gate_w = ctx_gather(gate_part, 0)
    up_w = ctx_gather(up_part, 0)
    down_other = ctx_fetch(down_part, 1)

    middle = input_rows + dot32(attended_low, full_output)
    inverse_two = rms_scale(middle)
    normed_two = (middle * inverse_two * ffn_gain).astype(jnp.bfloat16)

    rows_all = lax.all_gather(normed_two, "exp", axis=0, tiled=True)
    rows_all, gate_w, up_w, grad_sent, slot_rows, token_info = tie(
        rows_all, gate_w, up_w, grad_low, slot_rows, token_info
    )
    grad_all = lax.all_gather(grad_sent, "exp", axis=0, tiled=True)

    def blocks(rows):
        return rows.reshape(exp_count, tokens, MODEL_WIDTH)

    def flat(rows):
        return rows.reshape(rows.shape[0] * rows.shape[1], rows.shape[2])

    received, shared_act, shared_slope = enter(slot_rows, blocks(rows_all), shared_in_t, capacity)
    received = flat(received)
    expert_act, expert_slope, expert_silu = expert_in(received, gate_w, up_w)
    expert_act, down_other = tie(expert_act, down_other)
    if ctx_count == 2:
        down_parts = lax.axis_index("ctx") ^ jnp.arange(2, dtype=jnp.int32)
    else:
        down_parts = jnp.arange(2, dtype=jnp.int32)
        down_part = down_other[:, : MODEL_WIDTH // 2]
        down_other = down_other[:, MODEL_WIDTH // 2 :]
    expert_rows = expert_out(down_parts, expert_act, down_part, down_other)

    def slots(rows):
        return rows.reshape(exp_count, capacity, rows.shape[1])

    pair = exp_count >= 4 and exp_count % 4 == 0 and ctx_count == 2

    def sum_over_exp(part):
        units = jnp.repeat(jnp.arange(exp_count, dtype=jnp.int32), 2)
        everything = part((units, 0, 2 * exp_count))[0].reshape(exp_count, 2, tokens, MODEL_WIDTH // 2)
        return lax.psum_scatter(
            jnp.swapaxes(everything, 1, 2).reshape(exp_count * tokens, MODEL_WIDTH),
            "exp",
            scatter_dimension=0,
            tiled=True,
        ).astype(jnp.float32)

    out_part = functools.partial(
        combine,
        info=token_info,
        rows=(slots(expert_rows),),
        act=shared_act,
        weight=shared_out_w,
        scaled=True,
    )
    shared_act = flat(shared_act)
    rings = []
    if pair:
        out_ring = ExpRing(out_part, jnp.bfloat16, (middle[None],))
        rings = [out_ring]
    grad_expert, shared_back = ring_step(
        rings,
        lambda *operands: enter_back(*operands, capacity),
        slot_rows,
        blocks(grad_all),
        shared_out_w,
        shared_slope,
    )
    grad_expert = flat(grad_expert)
    grad_eu = ()
    out_late = (out_ring.late_units,) if pair else ()

    def late(work, here):
        if not (pair and here):
            return work
        return lambda units, *operands: (work(*operands), out_ring.late(0, units))

    for half in range(2):
        grad_eu = ring_step(
            rings,
            late(lambda *operands: expert_back(*operands[:6], half, operands[6:]), half == 0),
            *out_late,
            down_parts,
            grad_expert,
            down_part,
            down_other,
            expert_slope,
            expert_silu,
            *grad_eu,
        )
        if pair and half == 0:
            grad_eu, rest = grad_eu
            out_ring.take(rest)
            out_late = ()
    grad_eg, grad_eu = grad_eu
    pieces = [(), ()]
    theirs = lambda axis: lambda left, right: ctx_theirs(left, right, axis)
    total = lambda axis: lambda left, right, arrived: ctx_total(left, right, axis, arrived)
    for column_half, half in ((0, 0), (0, 1), (1, 0), (1, 1)):
        if (column_half, half) == (1, 1):
            down_theirs = ring_step(rings, theirs(1), expert_act, grad_expert)
            down_theirs, grad_eg, grad_eu = tie(down_theirs, grad_eg, grad_eu)
            down_arrived = ctx_send(down_theirs, 1)
            rings = []
        piece = ring_step(
            rings,
            lambda *operands: expert_grad_rows(*operands[:4], column_half, half, operands[4:]),
            grad_eg,
            grad_eu,
            gate_w,
            up_w,
            *pieces[column_half],
        )
        pieces[column_half] = (piece,)
    grad_rows = [slots(piece) for (piece,) in pieces]

    grad_part = functools.partial(
        combine,
        info=token_info,
        rows=tuple(grad_rows),
        act=shared_back,
        weight=shared_in_t,
        scaled=False,
    )
    shared_back = flat(shared_back)
    if pair:
        output = out_ring.finish()
        grad_ring = ExpRing(grad_part, jnp.float32, late_from=(9,))
        rings = [grad_ring]
    else:
        output = (middle + sum_over_exp(out_part)).astype(jnp.bfloat16)

    def theirs_and_late(which, *operands):
        if not pair:
            return ring_step(rings, theirs(0), *operands)
        return ring_step(rings, theirs(0), *operands)

    gate_theirs = theirs_and_late(0, received, grad_eg)
    gate_arrived = ctx_send(gate_theirs, 0)
    up_theirs = theirs_and_late(1, received, grad_eu)
    up_arrived = ctx_send(up_theirs, 0)
    shared_in_theirs, shared_down_theirs = ring_step(
        rings,
        lambda a, b, c, d: (ctx_theirs(a, b, 0), ctx_theirs(c, d, 0)),
        rows_all,
        shared_back,
        shared_act,
        grad_all,
    )
    shared_in_arrived = ctx_send(shared_in_theirs, 0)
    shared_down_arrived = ctx_send(shared_down_theirs, 0)
    expert_down_grad = ring_step(rings, total(1), expert_act, grad_expert, down_arrived)[None]
    expert_gate_grad = ring_step(rings, total(0), received, grad_eg, gate_arrived)[None]
    shared_in_grad, sum_sd = ring_step(
        rings,
        lambda a, b, c, d, e, f: (
            ctx_total(a, b, 0, c).astype(jnp.bfloat16),
            ctx_total(d, e, 0, f),
        ),
        rows_all,
        shared_back,
        shared_in_arrived,
        shared_act,
        grad_all,
        shared_down_arrived,
    )
    sum_sd = sum_sd[:own_hidden]
    shared_in_grad = lax.all_to_all(
        shared_in_grad.reshape(exp_count, own_rows, 2 * padded),
        "exp",
        split_axis=0,
        concat_axis=0,
        tiled=True,
    ).reshape(exp_count, own_rows, 2, ctx_count, padded_own)[..., :own_hidden]
    shared_in_grad = (
        jnp.transpose(shared_in_grad, (2, 1, 3, 0, 4))
        .reshape(2, own_rows, exp_count * ctx_count * own_hidden)
        .astype(jnp.float32)
    )
    expert_up_grad = ring_step(rings, total(0), received, grad_eu, up_arrived)[None]
    if pair:
        grad_two = grad_ring.finish()
    else:
        grad_two = sum_over_exp(grad_part)
    ffn_gain_term = jnp.sum(grad_two * middle * inverse_two, axis=0)
    gain_term = jnp.pad(ffn_gain_term[:, None], ((0, 0), (0, 127))).astype(jnp.bfloat16)
    grad_middle = grad_low.astype(jnp.float32) + norm_back(grad_two, middle, inverse_two, ffn_gain)
    grad_middle_low = grad_middle.astype(jnp.bfloat16)
    output_term = rows_grad(grad_middle_low, attended_low)
    sum_o = lax.psum_scatter(output_term, both, scatter_dimension=0, tiled=True)
    attended_gradient = dot_t(grad_middle_low, full_output).astype(jnp.bfloat16)

    grad_query_raw, key_terms, value_terms = attend_back(
        offset_array, query, key_value, attended_gradient, tables, key_tables
    )
    key_value_grad = jnp.concatenate([key_terms, value_terms], axis=1)
    if pair:
        own = lax.dynamic_slice_in_dim(key_value_grad, offset, tokens, axis=0)
        other = lax.dynamic_slice_in_dim(key_value_grad, tokens - offset, tokens, axis=0)
        key_value_raw = own + ctx_send(other.astype(jnp.bfloat16), 0).astype(jnp.float32)
    else:
        key_value_raw = ctx_send(key_value_grad.astype(jnp.bfloat16), 0)
    key_value_raw = key_value_raw.astype(jnp.bfloat16)
    in_term = qkv_grad(normed_one_t, grad_query_raw, key_value_raw, gain_term)
    grad_raw = jnp.concatenate(
        [grad_query_raw, key_value_raw, jnp.zeros((tokens, routing_columns), jnp.bfloat16)], axis=1
    )
    grad_one = dot_t(grad_raw, full_in)
    input_grad = grad_middle + norm_back(grad_one, input_rows, inverse_one, attn_gain)
    sum_in = lax.psum_scatter(in_term, both, scatter_dimension=0, tiled=True).astype(jnp.float32)
    own_gain = lax.dynamic_slice_in_dim(
        attn_gain, (lax.axis_index("ctx") * exp_count + exp_index) * own_rows, own_rows
    )
    attn_gain_grad = jnp.sum(sum_in[:, :edge] * attn_in.astype(jnp.float32), axis=1) / own_gain

    return (
        output[None],
        input_grad[None],
        attn_gain_grad,
        sum_in[:, :QUERY_WIDTH],
        sum_in[:, QUERY_WIDTH : QUERY_WIDTH + KEY_WIDTH],
        sum_in[:, QUERY_WIDTH + KEY_WIDTH : edge],
        sum_o.astype(jnp.float32).T,
        sum_in[:, edge],
        shared_in_grad[0],
        shared_in_grad[1],
        sum_sd,
        expert_gate_grad,
        expert_up_grad,
        expert_down_grad,
    )


def solution(mesh):
    return jax.shard_map(
        on_device,
        mesh=mesh,
        in_specs=(
            P("exp", "ctx", None),
            P(),
            P(("ctx", "exp"), None),
            P(("ctx", "exp"), None),
            P(("ctx", "exp"), None),
            P(("ctx", "exp"), None),
            P(),
            P(("ctx", "exp"), None),
            P(("ctx", "exp"), None),
            P(("ctx", "exp"), None),
            P("exp", "ctx", None),
            P("exp", "ctx", None),
            P("exp", None, "ctx"),
            P("exp", "ctx", None),
            P("exp", "ctx", None),
            P("exp", "ctx", None),
        ),
        out_specs=(
            P("exp", "ctx", None),
            P("exp", "ctx", None),
            P(("ctx", "exp")),
            P(("ctx", "exp"), None),
            P(("ctx", "exp"), None),
            P(("ctx", "exp"), None),
            P(None, ("ctx", "exp")),
            P(("ctx", "exp")),
            P(("ctx", "exp"), None),
            P(("ctx", "exp"), None),
            P(("ctx", "exp"), None),
            P("exp", "ctx", None),
            P("exp", "ctx", None),
            P("exp", None, "ctx"),
        ),
        check_vma=False,
    )
```

```python
import functools

import jax
import jax.numpy as jnp
import numpy as np
from jax import lax
from jax.experimental import pallas as pl
from jax.experimental.pallas import tpu as pltpu
from jax.sharding import PartitionSpec as P

MODEL_WIDTH = 2560
QUERY_HEADS = 20
KEY_VALUE_HEADS = 4
HEAD_SIZE = 128
TOP = 6
GROUP = QUERY_HEADS // KEY_VALUE_HEADS
QUERY_WIDTH = QUERY_HEADS * HEAD_SIZE
KEY_WIDTH = KEY_VALUE_HEADS * HEAD_SIZE
KERNEL_VMEM = 56 * 1024 * 1024
COMBINE_VMEM = 60 * 1024 * 1024


norm_eps = 1e-05
rope_base = 500000.0
causal_masked_score = -1e30


def rope_tables(token_positions):
    half_width = HEAD_SIZE // 2
    frequency = rope_base ** (-(jnp.arange(half_width, dtype=jnp.float32) * 2.0 / HEAD_SIZE))
    angles = token_positions[:, None].astype(jnp.float32) * frequency[None, :]
    cosine, sine = jnp.cos(angles), jnp.sin(angles)
    return (
        jnp.concatenate([cosine, cosine], axis=1),
        jnp.concatenate([-sine, sine], axis=1),
    )


def rms_scale(value_rows_all):
    return lax.rsqrt(jnp.mean(value_rows_all * value_rows_all, axis=-1, keepdims=True) + norm_eps)


def norm_back(grad_normed, source, inverse, gain_vector):
    scaled = grad_normed * gain_vector
    return inverse * scaled - source * inverse**3 * jnp.mean(
        scaled * source, axis=-1, keepdims=True
    )


def dot32(left, right):
    return jnp.dot(left, right, preferred_element_type=jnp.float32)


def dot_t(left, right):
    return lax.dot_general(
        left, right, (((1,), (1,)), ((), ())), preferred_element_type=jnp.float32
    )


def t_dot(left, right):
    return lax.dot_general(
        left, right, (((0,), (0,)), ((), ())), preferred_element_type=jnp.float32
    )


def tie(*values):
    return lax.optimization_barrier(values)


def kernel_params(limit=KERNEL_VMEM):
    return pltpu.CompilerParams(vmem_limit_bytes=limit)


def cost(flops, bytes_accessed, transcendentals=0):
    return pl.CostEstimate(
        flops=int(flops), bytes_accessed=int(bytes_accessed), transcendentals=int(transcendentals)
    )


def turn(values, cosine, sine):
    return values * cosine + pltpu.roll(values, HEAD_SIZE // 2, 1) * sine


def project_kernel(plain_from, rows_ref, weight_ref, cos_ref, sin_ref, out_ref):
    product = dot32(rows_ref[...], weight_ref[...])
    plain = pl.program_id(0) >= plain_from
    cosine = jnp.where(plain, 1.0, cos_ref[...])
    sine = jnp.where(plain, 0.0, sin_ref[...])
    for head in range(product.shape[1] // HEAD_SIZE):
        lanes = slice(head * HEAD_SIZE, (head + 1) * HEAD_SIZE)
        out_ref[:, lanes] = turn(product[:, lanes], cosine, sine).astype(jnp.bfloat16)


def project(rows, weight, tables, first_block, blocks, plain_from):
    count = rows.shape[0]
    return pl.pallas_call(
        functools.partial(project_kernel, plain_from),
        grid=(blocks,),
        in_specs=[
            pl.BlockSpec(rows.shape, lambda j: (0, 0)),
            pl.BlockSpec((weight.shape[0], KEY_WIDTH), lambda j: (0, first_block + j)),
            pl.BlockSpec(tables[0].shape, lambda j: (0, 0)),
            pl.BlockSpec(tables[1].shape, lambda j: (0, 0)),
        ],
        out_specs=pl.BlockSpec((count, KEY_WIDTH), lambda j: (0, j)),
        out_shape=jax.ShapeDtypeStruct((count, blocks * KEY_WIDTH), jnp.bfloat16),
        compiler_params=kernel_params(),
        cost_estimate=cost(
            2 * count * weight.shape[0] * blocks * KEY_WIDTH,
            2 * weight.shape[0] * (blocks * KEY_WIDTH + count),
        ),
        name="project",
    )(rows, weight, *tables)


def attend_probs(offset, first_row, query, keys):
    scores = dot_t(query, keys) * HEAD_SIZE ** (-0.5)
    rows = lax.broadcasted_iota(jnp.int32, scores.shape, 0) + (offset + first_row)
    places = lax.broadcasted_iota(jnp.int32, scores.shape, 1)
    scores = jnp.where(rows >= places, scores, causal_masked_score)
    weights = jnp.exp(scores - jnp.max(scores, axis=1, keepdims=True))
    return weights * (1.0 / jnp.sum(weights, axis=1, keepdims=True))


def attend_kernel(tile, offset_ref, query_ref, key_ref, value_ref, out_ref):
    keys, values = key_ref[...], value_ref[...]
    for head in range(GROUP):
        lanes = slice(head * HEAD_SIZE, (head + 1) * HEAD_SIZE)
        for start in range(0, query_ref.shape[0], tile):
            rows = slice(start, start + tile)
            probs = attend_probs(offset_ref[0], start, query_ref[rows, lanes], keys)
            out_ref[rows, lanes] = dot32(probs.astype(jnp.bfloat16), values).astype(jnp.bfloat16)


def attend(offset, query, key_value):
    count, places = query.shape[0], key_value.shape[0]
    work = count * places * HEAD_SIZE * QUERY_HEADS
    return pl.pallas_call(
        functools.partial(attend_kernel, min(count, 256)),
        grid=(KEY_VALUE_HEADS,),
        in_specs=[
            pl.BlockSpec(memory_space=pltpu.SMEM),
            pl.BlockSpec((count, GROUP * HEAD_SIZE), lambda g: (0, g)),
            pl.BlockSpec((places, HEAD_SIZE), lambda g: (0, g)),
            pl.BlockSpec((places, HEAD_SIZE), lambda g: (0, KEY_VALUE_HEADS + g)),
        ],
        out_specs=pl.BlockSpec((count, GROUP * HEAD_SIZE), lambda g: (0, g)),
        out_shape=jax.ShapeDtypeStruct(query.shape, jnp.bfloat16),
        compiler_params=kernel_params(),
        cost_estimate=cost(4 * work, 4 * query.size + 2 * key_value.size, work // HEAD_SIZE),
        name="attend",
    )(offset, query, key_value, key_value)


def attend_back_kernel(
    tile,
    offset_ref,
    query_ref,
    key_ref,
    value_ref,
    grad_ref,
    cos_ref,
    sin_ref,
    key_cos_ref,
    key_sin_ref,
    query_out,
    key_out,
    value_out,
):
    scale = HEAD_SIZE ** (-0.5)
    keys, values = key_ref[...], value_ref[...]
    key_sum = jnp.zeros(keys.shape, jnp.float32)
    value_sum = jnp.zeros(values.shape, jnp.float32)
    for head in range(GROUP):
        lanes = slice(head * HEAD_SIZE, (head + 1) * HEAD_SIZE)
        for start in range(0, query_ref.shape[0], tile):
            rows = slice(start, start + tile)
            query, grad = query_ref[rows, lanes], grad_ref[rows, lanes]
            probs = attend_probs(offset_ref[0], start, query, keys)
            grad_probs = dot_t(grad, values)
            delta = jnp.sum(probs * grad_probs, axis=1, keepdims=True)
            grad_scores = (probs * (grad_probs - delta)).astype(jnp.bfloat16)
            query_grad = dot32(grad_scores, keys) * scale
            query_out[rows, lanes] = turn(
                query_grad, cos_ref[rows, :], -sin_ref[rows, :]
            ).astype(jnp.bfloat16)
            key_sum = key_sum + t_dot(grad_scores, query)
            value_sum = value_sum + t_dot(probs.astype(jnp.bfloat16), grad)
    key_out[...] = turn(key_sum * scale, key_cos_ref[...], -key_sin_ref[...])
    value_out[...] = value_sum


def attend_back(offset, query, key_value, grad, tables, key_tables):
    count, places = query.shape[0], key_value.shape[0]
    work = count * places * HEAD_SIZE * QUERY_HEADS
    heads = pl.BlockSpec((count, GROUP * HEAD_SIZE), lambda g: (0, g))
    table = pl.BlockSpec((count, HEAD_SIZE), lambda g: (0, 0))
    key_table = pl.BlockSpec((places, HEAD_SIZE), lambda g: (0, 0))
    key_heads = pl.BlockSpec((places, HEAD_SIZE), lambda g: (0, g))
    return pl.pallas_call(
        functools.partial(attend_back_kernel, min(count, 256)),
        grid=(KEY_VALUE_HEADS,),
        in_specs=[
            pl.BlockSpec(memory_space=pltpu.SMEM),
            heads,
            key_heads,
            pl.BlockSpec((places, HEAD_SIZE), lambda g: (0, KEY_VALUE_HEADS + g)),
            heads,
            table,
            table,
            key_table,
            key_table,
        ],
        out_specs=[heads, key_heads, key_heads],
        out_shape=[
            jax.ShapeDtypeStruct(query.shape, jnp.bfloat16),
            jax.ShapeDtypeStruct((places, KEY_WIDTH), jnp.float32),
            jax.ShapeDtypeStruct((places, KEY_WIDTH), jnp.float32),
        ],
        compiler_params=kernel_params(),
        cost_estimate=cost(
            10 * work, 6 * query.size + 6 * key_value.size, work // HEAD_SIZE
        ),
        name="attend_back",
    )(offset, query, key_value, key_value, grad, *tables, *key_tables)


def silu_parts(gate_val, up_val):
    sigmoid_val = jax.nn.sigmoid(gate_val)
    silu_val = gate_val * sigmoid_val
    slope = up_val * sigmoid_val * (1.0 + gate_val * (1.0 - sigmoid_val))
    return [part.astype(jnp.bfloat16) for part in (silu_val * up_val, slope, silu_val)]


def row_chunks(count):
    return [slice(start, start + min(count, 256)) for start in range(0, count, min(count, 256))]


def slot_match(slots, capacity):
    places = lax.broadcasted_iota(jnp.int32, (capacity, slots.shape[1]), 0).astype(jnp.float32)
    return slots == places


def enter_kernel(slot_ref, rows_ref, weight_t_ref, picked_ref, act_ref, slope_ref, weight_ref):
    hidden = act_ref.shape[2]

    @pl.when(pl.program_id(0) == 0)
    def _():
        weight_ref[...] = weight_t_ref[...].T

    for chunk in row_chunks(rows_ref.shape[1]):
        product = dot32(rows_ref[0, chunk, :], weight_ref[...])
        act, slope, silu_val = silu_parts(product[:, :hidden], product[:, hidden:])
        act_ref[0, chunk, :] = act
        slope_ref[0, chunk, :hidden] = slope
        slope_ref[0, chunk, hidden:] = silu_val
    pick = jnp.where(slot_match(slot_ref[0, 0:1, :], picked_ref.shape[1]), 1.0, 0.0)
    picked_ref[0] = dot32(pick.astype(jnp.bfloat16), rows_ref[0]).astype(jnp.bfloat16)


def enter(slot_rows, rows, weight, capacity):
    count, tokens, width = rows.shape
    hidden = weight.shape[0] // 2
    block = lambda a, b: pl.BlockSpec((1, a, b), lambda i: (i, 0, 0))
    return pl.pallas_call(
        enter_kernel,
        grid=(count,),
        in_specs=[
            block(2, tokens),
            block(tokens, width),
            pl.BlockSpec(weight.shape, lambda i: (0, 0)),
        ],
        out_specs=[block(capacity, width), block(tokens, hidden), block(tokens, 2 * hidden)],
        out_shape=[
            jax.ShapeDtypeStruct((count, capacity, width), jnp.bfloat16),
            jax.ShapeDtypeStruct((count, tokens, hidden), jnp.bfloat16),
            jax.ShapeDtypeStruct((count, tokens, 2 * hidden), jnp.bfloat16),
        ],
        scratch_shapes=[pltpu.VMEM((width, 2 * hidden), jnp.bfloat16)],
        compiler_params=kernel_params(),
        cost_estimate=cost(
            2 * count * tokens * width * (capacity + 2 * hidden),
            2 * count * width * (tokens + capacity),
        ),
        name="enter",
    )(slot_rows, rows, weight)


def enter_back_kernel(slot_ref, rows_ref, weight_ref, slope_ref, picked_ref, grad_ref):
    rows = rows_ref[0]
    hidden = weight_ref.shape[0]
    for chunk in row_chunks(rows_ref.shape[1]):
        product = dot_t(rows_ref[0, chunk, :], weight_ref[...])
        for lanes in (slice(0, hidden), slice(hidden, 2 * hidden)):
            slope = slope_ref[0, chunk, lanes].astype(jnp.float32)
            grad_ref[0, chunk, lanes] = (product * slope).astype(jnp.bfloat16)
    match = slot_match(slot_ref[0, 0:1, :], picked_ref.shape[1])
    slot_weight = jnp.sum(jnp.where(match, slot_ref[0, 1:2, :], 0.0), axis=1, keepdims=True)
    pick = jnp.where(match, 1.0, 0.0).astype(jnp.bfloat16)
    picked_ref[0] = (dot32(pick, rows) * slot_weight).astype(jnp.bfloat16)


def enter_back(slot_rows, rows, weight, slope, capacity):
    count, tokens, width = rows.shape
    hidden = weight.shape[0]
    block = lambda a, b: pl.BlockSpec((1, a, b), lambda i: (i, 0, 0))
    return pl.pallas_call(
        enter_back_kernel,
        grid=(count,),
        in_specs=[
            block(2, tokens),
            block(tokens, width),
            pl.BlockSpec(weight.shape, lambda i: (0, 0)),
            block(tokens, 2 * hidden),
        ],
        out_specs=[block(capacity, width), block(tokens, 2 * hidden)],
        out_shape=[
            jax.ShapeDtypeStruct((count, capacity, width), jnp.bfloat16),
            jax.ShapeDtypeStruct((count, tokens, 2 * hidden), jnp.bfloat16),
        ],
        compiler_params=kernel_params(),
        cost_estimate=cost(
            2 * count * tokens * width * (capacity + hidden),
            2 * count * width * (tokens + capacity),
        ),
        name="enter_back",
    )(slot_rows, rows, weight, slope)


def expert_in_kernel(rows_ref, gate_ref, up_ref, act_ref, slope_ref, silu_ref):
    for chunk in row_chunks(rows_ref.shape[0]):
        rows = rows_ref[chunk, :]
        parts = silu_parts(dot32(rows, gate_ref[...]), dot32(rows, up_ref[...]))
        act_ref[chunk, :], slope_ref[chunk, :], silu_ref[chunk, :] = parts


def expert_in(rows, gate, up):
    count, width = rows.shape
    hidden = gate.shape[1]
    high, wide = min(count, 1024), 512
    weight = pl.BlockSpec((width, wide), lambda m, n: (0, n))
    out = pl.BlockSpec((high, wide), lambda m, n: (m, n))
    return pl.pallas_call(
        expert_in_kernel,
        grid=(count // high, hidden // wide),
        in_specs=[pl.BlockSpec((high, width), lambda m, n: (m, 0)), weight, weight],
        out_specs=[out] * 3,
        out_shape=[jax.ShapeDtypeStruct((count, hidden), jnp.bfloat16)] * 3,
        compiler_params=kernel_params(),
        cost_estimate=cost(4 * count * width * hidden, 2 * count * (width + 3 * hidden)),
        name="expert_in",
    )(rows, gate, up)


def expert_out_kernel(part_ref, act_ref, own_ref, other_ref, out_ref):
    for half, weight_ref in enumerate((own_ref, other_ref)):

        @pl.when(pl.program_id(0) == half)
        def _(weight_ref=weight_ref):
            out_ref[...] = dot32(act_ref[...], weight_ref[...]).astype(jnp.bfloat16)


def expert_out(parts, act, own, other):
    count, hidden = act.shape
    half = own.shape[1]
    high = min(count, 1024)
    whole = pl.BlockSpec((hidden, half), lambda h, m, p: (0, 0))
    return pl.pallas_call(
        expert_out_kernel,
        grid_spec=pltpu.PrefetchScalarGridSpec(
            num_scalar_prefetch=1,
            grid=(2, count // high),
            in_specs=[pl.BlockSpec((high, hidden), lambda h, m, p: (m, 0)), whole, whole],
            out_specs=pl.BlockSpec((high, half), lambda h, m, p: (m, p[h])),
        ),
        out_shape=jax.ShapeDtypeStruct((count, 2 * half), jnp.bfloat16),
        compiler_params=kernel_params(),
        cost_estimate=cost(4 * count * hidden * half, 2 * count * (2 * hidden + 2 * half)),
        name="expert_out",
    )(parts, act, own, other)


def expert_back_kernel(
    part_ref, own_rows_ref, other_rows_ref, own_ref, other_ref, slope_ref, silu_ref, *rest
):
    gate_out, up_out = rest[-2:]
    for chunk in row_chunks(own_rows_ref.shape[0]):
        product = dot_t(own_rows_ref[chunk, :], own_ref[...])
        product = product + dot_t(other_rows_ref[chunk, :], other_ref[...])
        slope = slope_ref[chunk, :].astype(jnp.float32)
        silu_val = silu_ref[chunk, :].astype(jnp.float32)
        gate_out[chunk, :] = (product * slope).astype(jnp.bfloat16)
        up_out[chunk, :] = (product * silu_val).astype(jnp.bfloat16)


def expert_back(parts, rows, own, other, slope, silu_val, half, earlier=()):
    count, width = rows.shape
    hidden = own.shape[0]
    high, wide = min(count // 2, 1024), 512
    first = half * (count // 2 // high)
    tile = pl.BlockSpec((high, wide), lambda m, n, p: (first + m, n))
    weight = pl.BlockSpec((wide, width // 2), lambda m, n, p: (n, 0))
    return pl.pallas_call(
        expert_back_kernel,
        grid_spec=pltpu.PrefetchScalarGridSpec(
            num_scalar_prefetch=1,
            grid=(count // 2 // high, hidden // wide),
            in_specs=[
                pl.BlockSpec((high, width // 2), lambda m, n, p: (first + m, p[0])),
                pl.BlockSpec((high, width // 2), lambda m, n, p: (first + m, p[1])),
                weight,
                weight,
                tile,
                tile,
            ]
            + [pl.BlockSpec(memory_space=pl.ANY)] * len(earlier),
            out_specs=[tile, tile],
        ),
        out_shape=[jax.ShapeDtypeStruct((count, hidden), jnp.bfloat16)] * 2,
        input_output_aliases={7 + i: i for i in range(len(earlier))},
        compiler_params=kernel_params(),
        cost_estimate=cost(count * width * hidden, count * (width + 4 * hidden)),
        name="expert_back",
    )(parts, rows, rows, own, other, slope, silu_val, *earlier)


def expert_rows_kernel(gate_grad_ref, up_grad_ref, gate_ref, up_ref, *rest):
    out_ref = rest[-1]
    total = dot_t(gate_grad_ref[...], gate_ref[...]) + dot_t(up_grad_ref[...], up_ref[...])
    out_ref[...] = total.astype(jnp.bfloat16)


def expert_grad_rows(gate_grad, up_grad, gate, up, column_half, half, earlier=()):
    count, hidden = gate_grad.shape
    wide = gate.shape[0] // 2
    high = min(count // 2, 512)
    first = half * (count // 2 // high)
    grad = pl.BlockSpec((high, hidden), lambda m: (first + m, 0))
    weight = pl.BlockSpec((wide, hidden), lambda m: (column_half, 0))
    return pl.pallas_call(
        expert_rows_kernel,
        grid=(count // 2 // high,),
        in_specs=[grad, grad, weight, weight] + [pl.BlockSpec(memory_space=pl.ANY)] * len(earlier),
        out_specs=pl.BlockSpec((high, wide), lambda m: (first + m, 0)),
        out_shape=jax.ShapeDtypeStruct((count, wide), jnp.bfloat16),
        input_output_aliases={4: 0} if earlier else {},
        compiler_params=kernel_params(),
        cost_estimate=cost(
            2 * count * wide * hidden, (2 * count + 4 * wide) * hidden + count * wide
        ),
        name="expert_grad_rows",
    )(gate_grad, up_grad, gate, up, *earlier)


def qkv_grad_kernel(rows_ref, query_ref, key_value_ref, gain_ref, out_ref):
    rows = rows_ref[...]
    edge = query_ref.shape[1]
    end = edge + key_value_ref.shape[1]
    out_ref[:, :edge] = dot32(rows, query_ref[...]).astype(jnp.bfloat16)
    out_ref[:, edge:end] = dot32(rows, key_value_ref[...]).astype(jnp.bfloat16)
    out_ref[:, end:] = gain_ref[...]


def qkv_grad(rows_t, query_grad, key_value_grad, gain_term):
    width, count = rows_t.shape
    high = 256
    columns = query_grad.shape[1] + key_value_grad.shape[1] + gain_term.shape[1]
    whole = lambda array: pl.BlockSpec(array.shape, lambda m: (0, 0))
    return pl.pallas_call(
        qkv_grad_kernel,
        grid=(width // high,),
        in_specs=[
            pl.BlockSpec((high, count), lambda m: (m, 0)),
            whole(query_grad),
            whole(key_value_grad),
            pl.BlockSpec((high, gain_term.shape[1]), lambda m: (m, 0)),
        ],
        out_specs=pl.BlockSpec((high, columns), lambda m: (m, 0)),
        out_shape=jax.ShapeDtypeStruct((width, columns), jnp.bfloat16),
        compiler_params=kernel_params(),
        cost_estimate=cost(2 * width * count * columns, 2 * width * (columns + count)),
        name="qkv_grad",
    )(rows_t, query_grad, key_value_grad, gain_term)


def rows_grad_kernel(left_ref, right_ref, out_ref):
    out_ref[...] = t_dot(left_ref[...], right_ref[...]).astype(jnp.bfloat16)


def rows_grad(left, right):
    count, high = left.shape
    wide = right.shape[1]
    return pl.pallas_call(
        rows_grad_kernel,
        grid=(high // 256,),
        in_specs=[
            pl.BlockSpec((count, 256), lambda m: (0, m)),
            pl.BlockSpec((count, wide), lambda m: (0, 0)),
        ],
        out_specs=pl.BlockSpec((256, wide), lambda m: (m, 0)),
        out_shape=jax.ShapeDtypeStruct((high, wide), jnp.bfloat16),
        compiler_params=kernel_params(),
        cost_estimate=cost(2 * count * high * wide, 2 * (count * (high + wide) + high * wide)),
        name="rows_grad",
    )(left, right)


def combine_kernel(scaled, pieces, arrivals, added, unit_ref, info_ref, act_ref, weight_ref, *rest):
    rows_refs, rest = rest[:pieces], rest[pieces:]
    arrived_refs, rest = rest[:arrivals], rest[arrivals:]
    added_refs, out_refs = rest[:added], rest[added:]
    slot = info_ref[0, :, 0:1]
    capacity = rows_refs[0].shape[1]
    lanes = lax.broadcasted_iota(jnp.int32, (slot.shape[0], capacity), 1).astype(jnp.float32)
    pick = jnp.where(slot == lanes, 1.0, 0.0).astype(jnp.bfloat16)

    def store(way):
        total = dot32(pick, rows_refs[way % pieces][0])
        if scaled:
            total = total * info_ref[0, :, 1:2]
        total = total + dot32(act_ref[0], weight_ref[...])
        for added_ref in added_refs:
            total = total + added_ref[0].astype(jnp.float32)
        if arrivals:
            total = total + arrived_refs[way][0].astype(jnp.float32)
        out_ref = out_refs[way % len(out_refs)]
        out_ref[0] = total.astype(out_ref.dtype)

    if pieces == 1 and not arrivals and len(out_refs) == 1:
        store(0)
        return
    for way in range(2):

        @pl.when(pl.program_id(0) % 2 == way)
        def _(way=way):
            store(way)


def combine(
    units, info, rows, act, weight, scaled, arrived=(), partner=(), own=(), kind="units",
    out_dtype=jnp.bfloat16,
):
    units, first, count = units
    tokens = info.shape[1]
    width, hidden = weight.shape[1], act.shape[2]
    capacity = rows[0].shape[1]
    columns = width // 2
    unit_block = lambda array: pl.BlockSpec((1,) + array.shape[1:], lambda i, u: (u[first + i], 0, 0))
    fixed = pl.BlockSpec((1, tokens, columns), lambda i, u: (0, 0, 0))
    half = pl.BlockSpec((1, tokens, columns), lambda i, u: (0, 0, i % 2))
    in_specs = [
        unit_block(info),
        unit_block(act),
        pl.BlockSpec((hidden, columns), lambda i, u: (0, i % 2)),
    ]
    block = (1, capacity, columns)
    if len(rows) == 1:
        in_specs.append(pl.BlockSpec(block, lambda i, u: (u[first + i], 0, i % 2)))
    else:
        in_specs.append(pl.BlockSpec(block, lambda i, u: (u[first + i - i % 2], 0, 0)))
        in_specs.append(pl.BlockSpec(block, lambda i, u: (u[first + i - i % 2 + 1], 0, 0)))
    in_specs += [fixed] * len(arrived)
    added = [array for array, _ in partner] + list(own)
    for _, at in partner:
        in_specs.append(pl.BlockSpec((1, tokens, columns), lambda i, u, at=at: (at + i, 0, 0)))
    in_specs += [half] * len(own)
    out_specs, out_shape = {
        "units": (
            [pl.BlockSpec((1, tokens, columns), lambda i, u: (i, 0, 0))],
            [(count, tokens, columns)],
        ),
        "ways": ([fixed, fixed], [(1, tokens, columns)] * 2),
        "tokens": ([half], [(1, tokens, width)]),
    }[kind]
    return pl.pallas_call(
        functools.partial(combine_kernel, scaled, len(rows), len(arrived), len(added)),
        grid_spec=pltpu.PrefetchScalarGridSpec(
            num_scalar_prefetch=1, grid=(count,), in_specs=in_specs, out_specs=out_specs
        ),
        out_shape=[jax.ShapeDtypeStruct(shape, out_dtype) for shape in out_shape],
        compiler_params=kernel_params(COMBINE_VMEM),
        cost_estimate=cost(
            2 * count * tokens * columns * (capacity + hidden),
            2 * count * columns * (capacity + tokens * (1 + len(added) + len(arrived) // 2)),
        ),
        name="combine",
    )(units, info, act, weight, *rows, *arrived, *added)


def weight_grad_kernel(part_ref, left_ref, right_ref, *rest):
    *arrived_refs, out_ref, sum_ref = rest
    step = pl.program_id(0)
    last = pl.num_programs(0) - 1

    @pl.when(step == 0)
    def _():
        for chunk in row_chunks(sum_ref.shape[0]):
            sum_ref[chunk, :] = t_dot(left_ref[:, chunk], right_ref[...])

    @pl.when((step > 0) & (step < last))
    def _():
        for chunk in row_chunks(sum_ref.shape[0]):
            sum_ref[chunk, :] += t_dot(left_ref[:, chunk], right_ref[...])

    @pl.when((step > 0) & (step == last))
    def _():
        for chunk in row_chunks(sum_ref.shape[0]):
            total = sum_ref[chunk, :] + t_dot(left_ref[:, chunk], right_ref[...])
            for arrived_ref in arrived_refs:
                total = total + arrived_ref[chunk, :].astype(jnp.float32)
            out_ref[chunk, :] = total.astype(out_ref.dtype)


def weight_grad(left, right, axis, part, out_dtype, arrived=()):
    count = left.shape[0]
    high = min(count // 2, 1024)
    widths = [left.shape[1], right.shape[1]]
    widths[axis] //= 2
    at = (lambda k, p: (k, p[0]), lambda k, p: (k, 0))
    whole = pl.BlockSpec(tuple(widths), lambda k, p: (0, 0))
    return pl.pallas_call(
        weight_grad_kernel,
        grid_spec=pltpu.PrefetchScalarGridSpec(
            num_scalar_prefetch=1,
            grid=(count // high,),
            in_specs=[
                pl.BlockSpec((high, widths[0]), at[axis]),
                pl.BlockSpec((high, widths[1]), at[1 - axis]),
            ]
            + [whole] * len(arrived),
            out_specs=whole,
            scratch_shapes=[pltpu.VMEM(tuple(widths), jnp.float32)],
        ),
        out_shape=jax.ShapeDtypeStruct(tuple(widths), out_dtype),
        compiler_params=kernel_params(),
        cost_estimate=cost(
            2 * count * widths[0] * widths[1], 2 * count * sum(widths) + 4 * widths[0] * widths[1]
        ),
        name="weight_grad",
    )(part, left, right, *arrived)


def exp_ring(chips):
    if chips % 2:
        return list(range(chips))
    return list(range(0, chips, 2)) + list(range(chips - 1, 0, -2))


class ChipRing:
    def __init__(self):
        exp_count = lax.axis_size("exp")
        self.chips = exp_count // 2
        ring = exp_ring(self.chips)
        place_of = np.argsort(np.array(ring)).astype(np.int32)
        index = lax.axis_index("exp")
        self.core = index % 2
        self.place = jnp.asarray(place_of)[index // 2]
        self.ring = np.array(ring, np.int32)
        self.swap = [(i, i ^ 1) for i in range(exp_count)]
        self.ways = ([], [])
        for at in range(self.chips):
            for core in range(2):
                here, there = ring[at] * 2 + core, ring[(at + 1) % self.chips] * 2 + core
                self.ways[0].append((here, there))
                self.ways[1].append((there, here))

    def table(self):
        steps = np.arange(1, self.chips + 1)[None, :, None]
        places = np.arange(self.chips)[:, None, None]
        at = np.concatenate([places - steps, places + steps], axis=2) % self.chips
        return jnp.asarray(self.ring[at].reshape(self.chips, -1), jnp.int32)[self.place]

    def move(self, totals):
        return [lax.ppermute(total, "exp", way) for total, way in zip(totals, self.ways)]

    def swap_cores(self, value):
        return lax.ppermute(value, "exp", self.swap)


class ExpRing:
    def __init__(self, part, out_dtype, own=(), late_from=(4,)):
        self.part, self.out_dtype, self.own = part, out_dtype, own
        self.line = ChipRing()
        self.arrived, self.step = (), 0
        self.swapped, self.partner = [], []
        self.late_from = list(late_from) + [self.line.chips + 1]
        chips = self.line.table() * 2
        self.own_units, other = chips + self.line.core, chips + 1 - self.line.core
        first = part((other, 0, 2))[0]
        first, other = tie(first, other)
        self.take(first)
        second = part((other, 2, 2 * (self.late_from[0] - 2)))[0]
        second, self.late_units = tie(second, other)
        second, self.swapped[0] = tie(second, self.swapped[0])
        self.take(second)

    def take(self, total):
        self.partner += [(len(self.swapped), 2 * i) for i in range(total.shape[0] // 2)]
        self.swapped.append(self.line.swap_cores(total))

    def from_partner(self, step):
        group, at = self.partner[step - 1]
        return ((self.swapped[group], at),)

    def late(self, which, units):
        start, end = self.late_from[which : which + 2]
        return self.part((units, 2 * (start - 1), 2 * (end - start)))[0]

    def totals(self):
        self.step += 1
        return self.part(
            (self.own_units, 2 * (self.step - 1), 2),
            arrived=self.arrived,
            partner=self.from_partner(self.step),
            kind="ways",
        )

    def finish(self):
        return self.part(
            (self.own_units, 2 * (self.line.chips - 1), 2),
            arrived=self.arrived,
            partner=self.from_partner(self.line.chips),
            own=self.own,
            kind="tokens",
            out_dtype=self.out_dtype,
        )[0][0]


def ring_step(rings, work, *operands, also=()):
    totals = [ring.totals() for ring in rings]
    totals, operands = tie(totals, operands)
    moved = [ring.line.move(total) for ring, total in zip(rings, totals)]
    swapped = [ring.swapped for ring in rings]
    moved, swapped, result, also = tie(moved, swapped, work(*operands), also)
    for ring, arrived, ring.swapped in zip(rings, moved, swapped):
        ring.arrived = tuple(arrived)
    return (result, *also) if also else result


def ctx_fetch(part, axis):
    if lax.axis_size("ctx") != 2:
        return lax.all_gather(part, "ctx", axis=axis, tiled=True)
    return lax.ppermute(part, "ctx", [(0, 1), (1, 0)])


def ctx_half(array, mine):
    half = array.shape[1] // 2
    index = lax.axis_index("ctx")
    return lax.dynamic_slice_in_dim(array, (index if mine else 1 - index) * half, half, axis=1)


def ctx_join(part, other, axis):
    if lax.axis_size("ctx") != 2:
        return other
    return lax.dynamic_update_slice_in_dim(
        jnp.concatenate([other, other], axis=axis),
        part,
        lax.axis_index("ctx") * part.shape[axis],
        axis,
    )


def ctx_gather(part, axis):
    return ctx_join(part, ctx_fetch(part, axis), axis)


def ctx_pair_part(which):
    return jnp.full((1,), which, jnp.int32)


def ctx_theirs(left, right, axis):
    if lax.axis_size("ctx") == 2:
        part = ctx_pair_part(1 - lax.axis_index("ctx"))
        return weight_grad(left, right, axis, part, jnp.bfloat16)
    return t_dot(left, right).astype(jnp.bfloat16)


def ctx_send(theirs, axis):
    if lax.axis_size("ctx") == 2:
        return lax.ppermute(theirs, "ctx", [(0, 1), (1, 0)])
    return lax.psum_scatter(theirs, "ctx", scatter_dimension=axis, tiled=True)


def ctx_total(left, right, axis, arrived):
    if lax.axis_size("ctx") == 2:
        part = ctx_pair_part(lax.axis_index("ctx"))
        return weight_grad(left, right, axis, part, jnp.float32, (arrived,))
    return arrived.astype(jnp.float32)


def on_device(
    block_input,
    attn_gain,
    query_weight,
    key_matrix,
    value_matrix,
    output_weight,
    ffn_gain,
    shared_gate,
    shared_up,
    shared_down,
    expert_gate,
    expert_up,
    expert_down,
    routes,
    route_weights,
    cotangent,
):
    input_rows = block_input[0].astype(jnp.float32)
    tokens = input_rows.shape[0]
    ctx_count = lax.axis_size("ctx")
    exp_count = lax.axis_size("exp")
    exp_index = lax.axis_index("exp")
    both = ("ctx", "exp")
    offset = lax.axis_index("ctx") * tokens
    offset_array = jnp.full((1,), offset, jnp.int32)
    tables = rope_tables(offset + jnp.arange(tokens, dtype=jnp.int32))
    key_tables = rope_tables(jnp.arange(ctx_count * tokens, dtype=jnp.int32))

    own_rows = shared_gate.shape[0]
    attn_in = jnp.concatenate([query_weight, key_matrix, value_matrix], axis=1)
    edge = attn_in.shape[1]
    own_weights = route_weights[0].T
    (weights_high,) = tie(own_weights.astype(jnp.bfloat16))
    weights_low = (own_weights - weights_high.astype(jnp.float32)).astype(jnp.bfloat16)
    routing = jnp.concatenate(
        [routes[0].T.astype(jnp.bfloat16), weights_high, weights_low], axis=0
    ).reshape(-1)
    routing_columns = -(-routing.shape[0] // (own_rows * 128)) * 128
    routing = jnp.pad(routing, (0, own_rows * routing_columns - routing.shape[0]))
    full_in = lax.all_gather(
        jnp.concatenate([attn_in, routing.reshape(own_rows, routing_columns)], axis=1),
        both,
        axis=0,
        tiled=True,
    )
    routing = lax.dynamic_slice(
        full_in,
        (lax.axis_index("ctx") * exp_count * own_rows, edge),
        (exp_count * own_rows, routing_columns),
    ).reshape(exp_count, own_rows * routing_columns)
    routing = routing[:, : 3 * TOP * tokens].reshape(exp_count, 3 * TOP, tokens)
    routing = routing.astype(jnp.float32)
    grad_low = cotangent[0]

    own_hidden = shared_down.shape[0]
    padded = -(-ctx_count * own_hidden // 256) * 256
    padded_own = padded // ctx_count
    shared_in = jnp.stack([shared_gate, shared_up]).reshape(
        2, own_rows, ctx_count, exp_count, own_hidden
    )
    shared_in = jnp.transpose(shared_in, (3, 1, 0, 2, 4)).reshape(
        exp_count, own_rows, 2 * ctx_count * own_hidden
    )
    shared_in = lax.all_to_all(shared_in, "exp", split_axis=0, concat_axis=0, tiled=True)
    shared_in = jnp.pad(
        shared_in.reshape(exp_count * own_rows, 2 * ctx_count, own_hidden),
        ((0, 0), (0, 0), (0, padded_own - own_hidden)),
    ).reshape(exp_count * own_rows, 2 * padded)
    shared_in = ctx_gather(shared_in, 0)
    shared_in_t = shared_in.T
    shared_out_w = ctx_gather(jnp.pad(shared_down, ((0, padded_own - own_hidden), (0, 0))), 0)

    capacity = tokens * TOP * 4 // (3 * exp_count)
    named = routing[:, :TOP] == exp_index.astype(jnp.float32)
    chosen = jnp.any(named, axis=1)
    token_weight = jnp.sum(
        jnp.where(named, routing[:, TOP : 2 * TOP] + routing[:, 2 * TOP :], 0.0), axis=1
    )
    upto = (jnp.arange(tokens)[:, None] <= jnp.arange(tokens)[None, :]).astype(jnp.bfloat16)
    slot = dot32(chosen.astype(jnp.bfloat16), upto).astype(jnp.int32) - 1
    slot = jnp.where(chosen, slot, -1)
    slot_rows = jnp.stack([slot.astype(jnp.float32), token_weight], axis=1)
    token_info = jnp.pad(
        jnp.stack([slot.astype(jnp.float32), token_weight], axis=2), ((0, 0), (0, 0), (0, 126))
    )

    inverse_one = rms_scale(input_rows)
    normed_one = (input_rows * inverse_one * attn_gain).astype(jnp.bfloat16)
    full_in, normed_one, shared_in_t, shared_out_w = tie(
        full_in, normed_one, shared_in_t, shared_out_w
    )
    output_weight, full_in = tie(output_weight, full_in)
    full_output = lax.all_gather(output_weight, both, axis=0, tiled=True)
    key_value = ctx_gather(
        project(normed_one, full_in, tables, QUERY_HEADS // KEY_VALUE_HEADS, 2, 1), 0
    )
    query = project(normed_one, full_in, tables, 0, QUERY_HEADS // KEY_VALUE_HEADS, QUERY_HEADS)
    attended_low = attend(offset_array, query, key_value)

    full_output, gate_part, up_part, down_part = tie(
        full_output, expert_gate[0], expert_up[0], expert_down[0]
    )
    gate_w = ctx_gather(gate_part, 0)
    up_w = ctx_gather(up_part, 0)
    down_other = ctx_fetch(down_part, 1)

    middle = input_rows + dot32(attended_low, full_output)
    inverse_two = rms_scale(middle)
    normed_two = (middle * inverse_two * ffn_gain).astype(jnp.bfloat16)

    rows_all = lax.all_gather(normed_two, "exp", axis=0, tiled=True)
    rows_all, gate_w, up_w, grad_sent, slot_rows, token_info = tie(
        rows_all, gate_w, up_w, grad_low, slot_rows, token_info
    )
    grad_all = lax.all_gather(grad_sent, "exp", axis=0, tiled=True)

    def blocks(rows):
        return rows.reshape(exp_count, tokens, MODEL_WIDTH)

    def flat(rows):
        return rows.reshape(rows.shape[0] * rows.shape[1], rows.shape[2])

    received, shared_act, shared_slope = enter(slot_rows, blocks(rows_all), shared_in_t, capacity)
    received = flat(received)
    expert_act, expert_slope, expert_silu = expert_in(received, gate_w, up_w)
    expert_act, down_other = tie(expert_act, down_other)
    if ctx_count == 2:
        down_parts = lax.axis_index("ctx") ^ jnp.arange(2, dtype=jnp.int32)
    else:
        down_parts = jnp.arange(2, dtype=jnp.int32)
        down_part = down_other[:, : MODEL_WIDTH // 2]
        down_other = down_other[:, MODEL_WIDTH // 2 :]
    expert_rows = expert_out(down_parts, expert_act, down_part, down_other)

    def slots(rows):
        return rows.reshape(exp_count, capacity, rows.shape[1])

    pair = exp_count >= 4 and exp_count % 4 == 0 and ctx_count == 2

    def sum_over_exp(part):
        units = jnp.repeat(jnp.arange(exp_count, dtype=jnp.int32), 2)
        everything = part((units, 0, 2 * exp_count))[0].reshape(exp_count, 2, tokens, MODEL_WIDTH // 2)
        return lax.psum_scatter(
            jnp.swapaxes(everything, 1, 2).reshape(exp_count * tokens, MODEL_WIDTH),
            "exp",
            scatter_dimension=0,
            tiled=True,
        ).astype(jnp.float32)

    out_part = functools.partial(
        combine,
        info=token_info,
        rows=(slots(expert_rows),),
        act=shared_act,
        weight=shared_out_w,
        scaled=True,
    )
    shared_act = flat(shared_act)
    rings = []
    if pair:
        out_ring = ExpRing(out_part, jnp.bfloat16, (middle[None],), late_from=(9,))
        rings = [out_ring]
    grad_expert, shared_back = ring_step(
        rings,
        lambda *operands: enter_back(*operands, capacity),
        slot_rows,
        blocks(grad_all),
        shared_out_w,
        shared_slope,
    )
    grad_expert = flat(grad_expert)
    grad_eu = ()
    early = ()
    if pair:
        early = (ctx_send(ctx_half(normed_one, False), 0), ctx_send(attended_low, 0))
    for half in range(2):
        grad_eu = ring_step(
            rings,
            lambda *operands: expert_back(*operands[:6], half, operands[6:]),
            down_parts,
            grad_expert,
            down_part,
            down_other,
            expert_slope,
            expert_silu,
            *grad_eu,
            also=early if half == 0 else (),
        )
        if pair and half == 0:
            grad_eu, normed_other, attended_other = grad_eu
    grad_eg, grad_eu = grad_eu
    pieces = [(), ()]
    theirs = lambda axis: lambda left, right: ctx_theirs(left, right, axis)
    total = lambda axis: lambda left, right, arrived: ctx_total(left, right, axis, arrived)
    for column_half, half in ((0, 0), (0, 1), (1, 0), (1, 1)):
        if (column_half, half) == (1, 1):
            down_theirs = ring_step(rings, theirs(1), expert_act, grad_expert)
            down_theirs, grad_eg, grad_eu = tie(down_theirs, grad_eg, grad_eu)
            down_arrived = ctx_send(down_theirs, 1)
            rings = []
        piece = ring_step(
            rings,
            lambda *operands: expert_grad_rows(*operands[:4], column_half, half, operands[4:]),
            grad_eg,
            grad_eu,
            gate_w,
            up_w,
            *pieces[column_half],
        )
        pieces[column_half] = (piece,)
    grad_rows = [slots(piece) for (piece,) in pieces]

    grad_part = functools.partial(
        combine,
        info=token_info,
        rows=tuple(grad_rows),
        act=shared_back,
        weight=shared_in_t,
        scaled=False,
    )
    shared_back = flat(shared_back)
    if pair:
        output = out_ring.finish()
        grad_ring = ExpRing(grad_part, jnp.float32, late_from=(9,))
        rings = [grad_ring]
    else:
        output = (middle + sum_over_exp(out_part)).astype(jnp.bfloat16)

    def theirs_and_late(which, *operands):
        if not pair:
            return ring_step(rings, theirs(0), *operands)
        return ring_step(rings, theirs(0), *operands)

    gate_theirs = theirs_and_late(0, received, grad_eg)
    gate_arrived = ctx_send(gate_theirs, 0)
    up_theirs = theirs_and_late(1, received, grad_eu)
    up_arrived = ctx_send(up_theirs, 0)
    shared_in_theirs, shared_down_theirs = ring_step(
        rings,
        lambda a, b, c, d: (ctx_theirs(a, b, 0), ctx_theirs(c, d, 0)),
        rows_all,
        shared_back,
        shared_act,
        grad_all,
    )
    shared_in_arrived = ctx_send(shared_in_theirs, 0)
    shared_down_arrived = ctx_send(shared_down_theirs, 0)
    expert_down_grad = ring_step(rings, total(1), expert_act, grad_expert, down_arrived)[None]
    expert_gate_grad = ring_step(rings, total(0), received, grad_eg, gate_arrived)[None]
    if pair:
        ring_step(rings, lambda: ())
    expert_up_grad = ring_step(rings, total(0), received, grad_eu, up_arrived)[None]
    if pair:
        grad_two = grad_ring.finish()
    else:
        grad_two = sum_over_exp(grad_part)
    ffn_gain_term = jnp.sum(grad_two * middle * inverse_two, axis=0)
    grad_middle = grad_low.astype(jnp.float32) + norm_back(grad_two, middle, inverse_two, ffn_gain)
    grad_middle_low = grad_middle.astype(jnp.bfloat16)
    attended_gradient = dot_t(grad_middle_low, full_output).astype(jnp.bfloat16)
    if pair:
        middle_other = ctx_send(ctx_half(grad_middle_low, False), 0)
        gain_half = ffn_gain_term.reshape(2, -1)
        gain_other = ctx_send(lax.dynamic_index_in_dim(gain_half, 1 - lax.axis_index("ctx"), 0), 0)
        gain_half = lax.dynamic_index_in_dim(gain_half, lax.axis_index("ctx"), 0)
        attended_gradient, gain_other = tie(attended_gradient, gain_other)
        gain_term = (gain_half + gain_other).T
    else:
        gain_term = ffn_gain_term[:, None]
    gain_term = jnp.pad(gain_term, ((0, 0), (0, 127))).astype(jnp.bfloat16)

    grad_query_raw, key_terms, value_terms = attend_back(
        offset_array, query, key_value, attended_gradient, tables, key_tables
    )
    key_value_grad = jnp.concatenate([key_terms, value_terms], axis=1)
    if pair:
        grad_query_raw, key_value_grad, middle_other = tie(
            grad_query_raw, key_value_grad, middle_other
        )
        key_value_other = ctx_send(key_value_grad.astype(jnp.bfloat16), 0)
        query_other = ctx_send(grad_query_raw, 0)
        output_term = rows_grad(
            jnp.concatenate([ctx_half(grad_middle_low, True), middle_other], axis=0),
            jnp.concatenate([attended_low, attended_other], axis=0),
        )
        sum_o = lax.psum_scatter(output_term, "exp", scatter_dimension=0, tiled=True)
        key_value_all = (key_value_grad + key_value_other.astype(jnp.float32)).astype(jnp.bfloat16)
        key_value_raw = lax.dynamic_slice_in_dim(key_value_all, offset, tokens, axis=0)
        key_value_both = jnp.concatenate(
            [
                key_value_raw,
                lax.dynamic_slice_in_dim(key_value_all, tokens - offset, tokens, axis=0),
            ],
            axis=0,
        )
        in_term = qkv_grad(
            jnp.concatenate([ctx_half(normed_one, True), normed_other], axis=0).T,
            jnp.concatenate([grad_query_raw, query_other], axis=0),
            key_value_both,
            gain_term,
        )
        sum_in = lax.psum_scatter(in_term, "exp", scatter_dimension=0, tiled=True)
    else:
        key_value_raw = ctx_send(key_value_grad.astype(jnp.bfloat16), 0)
        in_term = qkv_grad(normed_one.T, grad_query_raw, key_value_raw, gain_term)
        sum_in = lax.psum_scatter(in_term, both, scatter_dimension=0, tiled=True)
        output_term = rows_grad(grad_middle_low, attended_low)
        sum_o = lax.psum_scatter(output_term, both, scatter_dimension=0, tiled=True)
    sum_in = sum_in.astype(jnp.float32)
    grad_raw = jnp.concatenate(
        [grad_query_raw, key_value_raw, jnp.zeros((tokens, routing_columns), jnp.bfloat16)], axis=1
    )
    grad_one = dot_t(grad_raw, full_in)
    input_grad = grad_middle + norm_back(grad_one, input_rows, inverse_one, attn_gain)
    own_gain = lax.dynamic_slice_in_dim(
        attn_gain, (lax.axis_index("ctx") * exp_count + exp_index) * own_rows, own_rows
    )
    attn_gain_grad = jnp.sum(sum_in[:, :edge] * attn_in.astype(jnp.float32), axis=1) / own_gain

    shared_in_grad = ctx_total(rows_all, shared_back, 0, shared_in_arrived).astype(jnp.bfloat16)
    sum_sd = ctx_total(shared_act, grad_all, 0, shared_down_arrived)[:own_hidden]
    shared_in_grad = lax.all_to_all(
        shared_in_grad.reshape(exp_count, own_rows, 2 * padded),
        "exp",
        split_axis=0,
        concat_axis=0,
        tiled=True,
    ).reshape(exp_count, own_rows, 2, ctx_count, padded_own)[..., :own_hidden]
    shared_in_grad = (
        jnp.transpose(shared_in_grad, (2, 1, 3, 0, 4))
        .reshape(2, own_rows, exp_count * ctx_count * own_hidden)
        .astype(jnp.float32)
    )
    return (
        output[None],
        input_grad[None],
        attn_gain_grad,
        sum_in[:, :QUERY_WIDTH],
        sum_in[:, QUERY_WIDTH : QUERY_WIDTH + KEY_WIDTH],
        sum_in[:, QUERY_WIDTH + KEY_WIDTH : edge],
        sum_o.astype(jnp.float32).T,
        sum_in[:, edge],
        shared_in_grad[0],
        shared_in_grad[1],
        sum_sd,
        expert_gate_grad,
        expert_up_grad,
        expert_down_grad,
    )


def solution(mesh):
    return jax.shard_map(
        on_device,
        mesh=mesh,
        in_specs=(
            P("exp", "ctx", None),
            P(),
            P(("ctx", "exp"), None),
            P(("ctx", "exp"), None),
            P(("ctx", "exp"), None),
            P(("ctx", "exp"), None),
            P(),
            P(("ctx", "exp"), None),
            P(("ctx", "exp"), None),
            P(("ctx", "exp"), None),
            P("exp", "ctx", None),
            P("exp", "ctx", None),
            P("exp", None, "ctx"),
            P("exp", "ctx", None),
            P("exp", "ctx", None),
            P("exp", "ctx", None),
        ),
        out_specs=(
            P("exp", "ctx", None),
            P("exp", "ctx", None),
            P(("ctx", "exp")),
            P(("ctx", "exp"), None),
            P(("ctx", "exp"), None),
            P(("ctx", "exp"), None),
            P(None, ("ctx", "exp")),
            P(("ctx", "exp")),
            P(("ctx", "exp"), None),
            P(("ctx", "exp"), None),
            P(("ctx", "exp"), None),
            P("exp", "ctx", None),
            P("exp", "ctx", None),
            P("exp", None, "ctx"),
        ),
        check_vma=False,
    )
```

```python
import functools

import jax
import jax.numpy as jnp
import numpy as np
from jax import lax
from jax.experimental import pallas as pl
from jax.experimental.pallas import tpu as pltpu
from jax.sharding import PartitionSpec as P

MODEL_WIDTH = 2560
QUERY_HEADS = 20
KEY_VALUE_HEADS = 4
HEAD_SIZE = 128
TOP = 6
GROUP = QUERY_HEADS // KEY_VALUE_HEADS
QUERY_WIDTH = QUERY_HEADS * HEAD_SIZE
KEY_WIDTH = KEY_VALUE_HEADS * HEAD_SIZE
KERNEL_VMEM = 56 * 1024 * 1024
COMBINE_VMEM = 60 * 1024 * 1024


norm_eps = 1e-05
rope_base = 500000.0
causal_masked_score = -1e30


def rope_tables(token_positions):
    half_width = HEAD_SIZE // 2
    frequency = rope_base ** (-(jnp.arange(half_width, dtype=jnp.float32) * 2.0 / HEAD_SIZE))
    angles = token_positions[:, None].astype(jnp.float32) * frequency[None, :]
    cosine, sine = jnp.cos(angles), jnp.sin(angles)
    return (
        jnp.concatenate([cosine, cosine], axis=1),
        jnp.concatenate([-sine, sine], axis=1),
    )


def rms_scale(value_rows_all):
    return lax.rsqrt(jnp.mean(value_rows_all * value_rows_all, axis=-1, keepdims=True) + norm_eps)


def norm_back(grad_normed, source, inverse, gain_vector):
    scaled = grad_normed * gain_vector
    return inverse * scaled - source * inverse**3 * jnp.mean(
        scaled * source, axis=-1, keepdims=True
    )


def dot32(left, right):
    return jnp.dot(left, right, preferred_element_type=jnp.float32)


def dot_t(left, right):
    return lax.dot_general(
        left, right, (((1,), (1,)), ((), ())), preferred_element_type=jnp.float32
    )


def t_dot(left, right):
    return lax.dot_general(
        left, right, (((0,), (0,)), ((), ())), preferred_element_type=jnp.float32
    )


def tie(*values):
    return lax.optimization_barrier(values)


def kernel_params(limit=KERNEL_VMEM):
    return pltpu.CompilerParams(vmem_limit_bytes=limit)


def cost(flops, bytes_accessed, transcendentals=0):
    return pl.CostEstimate(
        flops=int(flops), bytes_accessed=int(bytes_accessed), transcendentals=int(transcendentals)
    )


def turn(values, cosine, sine):
    return values * cosine + pltpu.roll(values, HEAD_SIZE // 2, 1) * sine


def project_kernel(plain_from, rows_ref, weight_ref, cos_ref, sin_ref, out_ref):
    product = dot32(rows_ref[...], weight_ref[...])
    plain = pl.program_id(0) >= plain_from
    cosine = jnp.where(plain, 1.0, cos_ref[...])
    sine = jnp.where(plain, 0.0, sin_ref[...])
    for head in range(product.shape[1] // HEAD_SIZE):
        lanes = slice(head * HEAD_SIZE, (head + 1) * HEAD_SIZE)
        out_ref[:, lanes] = turn(product[:, lanes], cosine, sine).astype(jnp.bfloat16)


def project(rows, weight, tables, first_block, blocks, plain_from):
    count = rows.shape[0]
    return pl.pallas_call(
        functools.partial(project_kernel, plain_from),
        grid=(blocks,),
        in_specs=[
            pl.BlockSpec(rows.shape, lambda j: (0, 0)),
            pl.BlockSpec((weight.shape[0], KEY_WIDTH), lambda j: (0, first_block + j)),
            pl.BlockSpec(tables[0].shape, lambda j: (0, 0)),
            pl.BlockSpec(tables[1].shape, lambda j: (0, 0)),
        ],
        out_specs=pl.BlockSpec((count, KEY_WIDTH), lambda j: (0, j)),
        out_shape=jax.ShapeDtypeStruct((count, blocks * KEY_WIDTH), jnp.bfloat16),
        compiler_params=kernel_params(),
        cost_estimate=cost(
            2 * count * weight.shape[0] * blocks * KEY_WIDTH,
            2 * weight.shape[0] * (blocks * KEY_WIDTH + count),
        ),
        name="project",
    )(rows, weight, *tables)


def attend_probs(offset, first_row, query, keys):
    scores = dot_t(query, keys) * HEAD_SIZE ** (-0.5)
    rows = lax.broadcasted_iota(jnp.int32, scores.shape, 0) + (offset + first_row)
    places = lax.broadcasted_iota(jnp.int32, scores.shape, 1)
    scores = jnp.where(rows >= places, scores, causal_masked_score)
    weights = jnp.exp(scores - jnp.max(scores, axis=1, keepdims=True))
    return weights * (1.0 / jnp.sum(weights, axis=1, keepdims=True))


def attend_kernel(tile, offset_ref, query_ref, key_ref, value_ref, out_ref):
    keys, values = key_ref[...], value_ref[...]
    for head in range(GROUP):
        lanes = slice(head * HEAD_SIZE, (head + 1) * HEAD_SIZE)
        for start in range(0, query_ref.shape[0], tile):
            rows = slice(start, start + tile)
            probs = attend_probs(offset_ref[0], start, query_ref[rows, lanes], keys)
            out_ref[rows, lanes] = dot32(probs.astype(jnp.bfloat16), values).astype(jnp.bfloat16)


def attend(offset, query, key_value):
    count, places = query.shape[0], key_value.shape[0]
    work = count * places * HEAD_SIZE * QUERY_HEADS
    return pl.pallas_call(
        functools.partial(attend_kernel, min(count, 256)),
        grid=(KEY_VALUE_HEADS,),
        in_specs=[
            pl.BlockSpec(memory_space=pltpu.SMEM),
            pl.BlockSpec((count, GROUP * HEAD_SIZE), lambda g: (0, g)),
            pl.BlockSpec((places, HEAD_SIZE), lambda g: (0, g)),
            pl.BlockSpec((places, HEAD_SIZE), lambda g: (0, KEY_VALUE_HEADS + g)),
        ],
        out_specs=pl.BlockSpec((count, GROUP * HEAD_SIZE), lambda g: (0, g)),
        out_shape=jax.ShapeDtypeStruct(query.shape, jnp.bfloat16),
        compiler_params=kernel_params(),
        cost_estimate=cost(4 * work, 4 * query.size + 2 * key_value.size, work // HEAD_SIZE),
        name="attend",
    )(offset, query, key_value, key_value)


def attend_back_kernel(
    tile,
    offset_ref,
    query_ref,
    key_ref,
    value_ref,
    grad_ref,
    cos_ref,
    sin_ref,
    key_cos_ref,
    key_sin_ref,
    query_out,
    key_out,
    value_out,
):
    scale = HEAD_SIZE ** (-0.5)
    keys, values = key_ref[...], value_ref[...]
    key_sum = jnp.zeros(keys.shape, jnp.float32)
    value_sum = jnp.zeros(values.shape, jnp.float32)
    for head in range(GROUP):
        lanes = slice(head * HEAD_SIZE, (head + 1) * HEAD_SIZE)
        for start in range(0, query_ref.shape[0], tile):
            rows = slice(start, start + tile)
            query, grad = query_ref[rows, lanes], grad_ref[rows, lanes]
            probs = attend_probs(offset_ref[0], start, query, keys)
            grad_probs = dot_t(grad, values)
            delta = jnp.sum(probs * grad_probs, axis=1, keepdims=True)
            grad_scores = (probs * (grad_probs - delta)).astype(jnp.bfloat16)
            query_grad = dot32(grad_scores, keys) * scale
            query_out[rows, lanes] = turn(
                query_grad, cos_ref[rows, :], -sin_ref[rows, :]
            ).astype(jnp.bfloat16)
            key_sum = key_sum + t_dot(grad_scores, query)
            value_sum = value_sum + t_dot(probs.astype(jnp.bfloat16), grad)
    key_out[...] = turn(key_sum * scale, key_cos_ref[...], -key_sin_ref[...])
    value_out[...] = value_sum


def attend_back(offset, query, key_value, grad, tables, key_tables):
    count, places = query.shape[0], key_value.shape[0]
    work = count * places * HEAD_SIZE * QUERY_HEADS
    heads = pl.BlockSpec((count, GROUP * HEAD_SIZE), lambda g: (0, g))
    table = pl.BlockSpec((count, HEAD_SIZE), lambda g: (0, 0))
    key_table = pl.BlockSpec((places, HEAD_SIZE), lambda g: (0, 0))
    key_heads = pl.BlockSpec((places, HEAD_SIZE), lambda g: (0, g))
    return pl.pallas_call(
        functools.partial(attend_back_kernel, min(count, 256)),
        grid=(KEY_VALUE_HEADS,),
        in_specs=[
            pl.BlockSpec(memory_space=pltpu.SMEM),
            heads,
            key_heads,
            pl.BlockSpec((places, HEAD_SIZE), lambda g: (0, KEY_VALUE_HEADS + g)),
            heads,
            table,
            table,
            key_table,
            key_table,
        ],
        out_specs=[heads, key_heads, key_heads],
        out_shape=[
            jax.ShapeDtypeStruct(query.shape, jnp.bfloat16),
            jax.ShapeDtypeStruct((places, KEY_WIDTH), jnp.float32),
            jax.ShapeDtypeStruct((places, KEY_WIDTH), jnp.float32),
        ],
        compiler_params=kernel_params(),
        cost_estimate=cost(
            10 * work, 6 * query.size + 6 * key_value.size, work // HEAD_SIZE
        ),
        name="attend_back",
    )(offset, query, key_value, key_value, grad, *tables, *key_tables)


def silu_parts(gate_val, up_val):
    sigmoid_val = jax.nn.sigmoid(gate_val)
    silu_val = gate_val * sigmoid_val
    slope = up_val * sigmoid_val * (1.0 + gate_val * (1.0 - sigmoid_val))
    return [part.astype(jnp.bfloat16) for part in (silu_val * up_val, slope, silu_val)]


def row_chunks(count):
    return [slice(start, start + min(count, 256)) for start in range(0, count, min(count, 256))]


def slot_match(slots, capacity):
    places = lax.broadcasted_iota(jnp.int32, (capacity, slots.shape[1]), 0).astype(jnp.float32)
    return slots == places


def enter_kernel(slot_ref, rows_ref, weight_t_ref, picked_ref, act_ref, slope_ref, weight_ref):
    hidden = act_ref.shape[2]

    @pl.when(pl.program_id(0) == 0)
    def _():
        weight_ref[...] = weight_t_ref[...].T

    for chunk in row_chunks(rows_ref.shape[1]):
        product = dot32(rows_ref[0, chunk, :], weight_ref[...])
        act, slope, silu_val = silu_parts(product[:, :hidden], product[:, hidden:])
        act_ref[0, chunk, :] = act
        slope_ref[0, chunk, :hidden] = slope
        slope_ref[0, chunk, hidden:] = silu_val
    pick = jnp.where(slot_match(slot_ref[0, 0:1, :], picked_ref.shape[1]), 1.0, 0.0)
    picked_ref[0] = dot32(pick.astype(jnp.bfloat16), rows_ref[0]).astype(jnp.bfloat16)


def enter(slot_rows, rows, weight, capacity):
    count, tokens, width = rows.shape
    hidden = weight.shape[0] // 2
    block = lambda a, b: pl.BlockSpec((1, a, b), lambda i: (i, 0, 0))
    return pl.pallas_call(
        enter_kernel,
        grid=(count,),
        in_specs=[
            block(2, tokens),
            block(tokens, width),
            pl.BlockSpec(weight.shape, lambda i: (0, 0)),
        ],
        out_specs=[block(capacity, width), block(tokens, hidden), block(tokens, 2 * hidden)],
        out_shape=[
            jax.ShapeDtypeStruct((count, capacity, width), jnp.bfloat16),
            jax.ShapeDtypeStruct((count, tokens, hidden), jnp.bfloat16),
            jax.ShapeDtypeStruct((count, tokens, 2 * hidden), jnp.bfloat16),
        ],
        scratch_shapes=[pltpu.VMEM((width, 2 * hidden), jnp.bfloat16)],
        compiler_params=kernel_params(),
        cost_estimate=cost(
            2 * count * tokens * width * (capacity + 2 * hidden),
            2 * count * width * (tokens + capacity),
        ),
        name="enter",
    )(slot_rows, rows, weight)


def enter_back_kernel(slot_ref, rows_ref, weight_ref, slope_ref, picked_ref, grad_ref):
    rows = rows_ref[0]
    hidden = weight_ref.shape[0]
    for chunk in row_chunks(rows_ref.shape[1]):
        product = dot_t(rows_ref[0, chunk, :], weight_ref[...])
        for lanes in (slice(0, hidden), slice(hidden, 2 * hidden)):
            slope = slope_ref[0, chunk, lanes].astype(jnp.float32)
            grad_ref[0, chunk, lanes] = (product * slope).astype(jnp.bfloat16)
    match = slot_match(slot_ref[0, 0:1, :], picked_ref.shape[1])
    slot_weight = jnp.sum(jnp.where(match, slot_ref[0, 1:2, :], 0.0), axis=1, keepdims=True)
    pick = jnp.where(match, 1.0, 0.0).astype(jnp.bfloat16)
    picked_ref[0] = (dot32(pick, rows) * slot_weight).astype(jnp.bfloat16)


def enter_back(slot_rows, rows, weight, slope, capacity):
    count, tokens, width = rows.shape
    hidden = weight.shape[0]
    block = lambda a, b: pl.BlockSpec((1, a, b), lambda i: (i, 0, 0))
    return pl.pallas_call(
        enter_back_kernel,
        grid=(count,),
        in_specs=[
            block(2, tokens),
            block(tokens, width),
            pl.BlockSpec(weight.shape, lambda i: (0, 0)),
            block(tokens, 2 * hidden),
        ],
        out_specs=[block(capacity, width), block(tokens, 2 * hidden)],
        out_shape=[
            jax.ShapeDtypeStruct((count, capacity, width), jnp.bfloat16),
            jax.ShapeDtypeStruct((count, tokens, 2 * hidden), jnp.bfloat16),
        ],
        compiler_params=kernel_params(),
        cost_estimate=cost(
            2 * count * tokens * width * (capacity + hidden),
            2 * count * width * (tokens + capacity),
        ),
        name="enter_back",
    )(slot_rows, rows, weight, slope)


def expert_in_kernel(rows_ref, gate_ref, up_ref, act_ref, slope_ref, silu_ref):
    for chunk in row_chunks(rows_ref.shape[0]):
        rows = rows_ref[chunk, :]
        parts = silu_parts(dot32(rows, gate_ref[...]), dot32(rows, up_ref[...]))
        act_ref[chunk, :], slope_ref[chunk, :], silu_ref[chunk, :] = parts


def expert_in(rows, gate, up):
    count, width = rows.shape
    hidden = gate.shape[1]
    high, wide = min(count, 1024), 512
    weight = pl.BlockSpec((width, wide), lambda m, n: (0, n))
    out = pl.BlockSpec((high, wide), lambda m, n: (m, n))
    return pl.pallas_call(
        expert_in_kernel,
        grid=(count // high, hidden // wide),
        in_specs=[pl.BlockSpec((high, width), lambda m, n: (m, 0)), weight, weight],
        out_specs=[out] * 3,
        out_shape=[jax.ShapeDtypeStruct((count, hidden), jnp.bfloat16)] * 3,
        compiler_params=kernel_params(),
        cost_estimate=cost(4 * count * width * hidden, 2 * count * (width + 3 * hidden)),
        name="expert_in",
    )(rows, gate, up)


def expert_out_kernel(part_ref, act_ref, own_ref, other_ref, out_ref):
    for half, weight_ref in enumerate((own_ref, other_ref)):

        @pl.when(pl.program_id(0) == half)
        def _(weight_ref=weight_ref):
            out_ref[...] = dot32(act_ref[...], weight_ref[...]).astype(jnp.bfloat16)


def expert_out(parts, act, own, other):
    count, hidden = act.shape
    half = own.shape[1]
    high = min(count, 1024)
    whole = pl.BlockSpec((hidden, half), lambda h, m, p: (0, 0))
    return pl.pallas_call(
        expert_out_kernel,
        grid_spec=pltpu.PrefetchScalarGridSpec(
            num_scalar_prefetch=1,
            grid=(2, count // high),
            in_specs=[pl.BlockSpec((high, hidden), lambda h, m, p: (m, 0)), whole, whole],
            out_specs=pl.BlockSpec((high, half), lambda h, m, p: (m, p[h])),
        ),
        out_shape=jax.ShapeDtypeStruct((count, 2 * half), jnp.bfloat16),
        compiler_params=kernel_params(),
        cost_estimate=cost(4 * count * hidden * half, 2 * count * (2 * hidden + 2 * half)),
        name="expert_out",
    )(parts, act, own, other)


def expert_back_kernel(
    part_ref, own_rows_ref, other_rows_ref, own_ref, other_ref, slope_ref, silu_ref, *rest
):
    gate_out, up_out = rest[-2:]
    for chunk in row_chunks(own_rows_ref.shape[0]):
        product = dot_t(own_rows_ref[chunk, :], own_ref[...])
        product = product + dot_t(other_rows_ref[chunk, :], other_ref[...])
        slope = slope_ref[chunk, :].astype(jnp.float32)
        silu_val = silu_ref[chunk, :].astype(jnp.float32)
        gate_out[chunk, :] = (product * slope).astype(jnp.bfloat16)
        up_out[chunk, :] = (product * silu_val).astype(jnp.bfloat16)


def expert_back(parts, rows, own, other, slope, silu_val, half, earlier=()):
    count, width = rows.shape
    hidden = own.shape[0]
    high, wide = min(count // 2, 1024), 512
    first = half * (count // 2 // high)
    tile = pl.BlockSpec((high, wide), lambda m, n, p: (first + m, n))
    weight = pl.BlockSpec((wide, width // 2), lambda m, n, p: (n, 0))
    return pl.pallas_call(
        expert_back_kernel,
        grid_spec=pltpu.PrefetchScalarGridSpec(
            num_scalar_prefetch=1,
            grid=(count // 2 // high, hidden // wide),
            in_specs=[
                pl.BlockSpec((high, width // 2), lambda m, n, p: (first + m, p[0])),
                pl.BlockSpec((high, width // 2), lambda m, n, p: (first + m, p[1])),
                weight,
                weight,
                tile,
                tile,
            ]
            + [pl.BlockSpec(memory_space=pl.ANY)] * len(earlier),
            out_specs=[tile, tile],
        ),
        out_shape=[jax.ShapeDtypeStruct((count, hidden), jnp.bfloat16)] * 2,
        input_output_aliases={7 + i: i for i in range(len(earlier))},
        compiler_params=kernel_params(),
        cost_estimate=cost(count * width * hidden, count * (width + 4 * hidden)),
        name="expert_back",
    )(parts, rows, rows, own, other, slope, silu_val, *earlier)


def expert_rows_kernel(gate_grad_ref, up_grad_ref, gate_ref, up_ref, *rest):
    out_ref = rest[-1]
    total = dot_t(gate_grad_ref[...], gate_ref[...]) + dot_t(up_grad_ref[...], up_ref[...])
    out_ref[...] = total.astype(jnp.bfloat16)


def expert_grad_rows(gate_grad, up_grad, gate, up, column_half, half, earlier=()):
    count, hidden = gate_grad.shape
    wide = gate.shape[0] // 2
    high = min(count // 2, 512)
    first = half * (count // 2 // high)
    grad = pl.BlockSpec((high, hidden), lambda m: (first + m, 0))
    weight = pl.BlockSpec((wide, hidden), lambda m: (column_half, 0))
    return pl.pallas_call(
        expert_rows_kernel,
        grid=(count // 2 // high,),
        in_specs=[grad, grad, weight, weight] + [pl.BlockSpec(memory_space=pl.ANY)] * len(earlier),
        out_specs=pl.BlockSpec((high, wide), lambda m: (first + m, 0)),
        out_shape=jax.ShapeDtypeStruct((count, wide), jnp.bfloat16),
        input_output_aliases={4: 0} if earlier else {},
        compiler_params=kernel_params(),
        cost_estimate=cost(
            2 * count * wide * hidden, (2 * count + 4 * wide) * hidden + count * wide
        ),
        name="expert_grad_rows",
    )(gate_grad, up_grad, gate, up, *earlier)


def qkv_grad_kernel(rows_ref, query_ref, key_value_ref, gain_ref, out_ref):
    rows = rows_ref[...]
    edge = query_ref.shape[1]
    end = edge + key_value_ref.shape[1]
    out_ref[:, :edge] = dot32(rows, query_ref[...]).astype(jnp.bfloat16)
    out_ref[:, edge:end] = dot32(rows, key_value_ref[...]).astype(jnp.bfloat16)
    out_ref[:, end:] = gain_ref[...]


def qkv_grad(rows_t, query_grad, key_value_grad, gain_term):
    width, count = rows_t.shape
    high = 256
    columns = query_grad.shape[1] + key_value_grad.shape[1] + gain_term.shape[1]
    whole = lambda array: pl.BlockSpec(array.shape, lambda m: (0, 0))
    return pl.pallas_call(
        qkv_grad_kernel,
        grid=(width // high,),
        in_specs=[
            pl.BlockSpec((high, count), lambda m: (m, 0)),
            whole(query_grad),
            whole(key_value_grad),
            pl.BlockSpec((high, gain_term.shape[1]), lambda m: (m, 0)),
        ],
        out_specs=pl.BlockSpec((high, columns), lambda m: (m, 0)),
        out_shape=jax.ShapeDtypeStruct((width, columns), jnp.bfloat16),
        compiler_params=kernel_params(),
        cost_estimate=cost(2 * width * count * columns, 2 * width * (columns + count)),
        name="qkv_grad",
    )(rows_t, query_grad, key_value_grad, gain_term)


def rows_grad_kernel(left_ref, right_ref, out_ref):
    out_ref[...] = t_dot(left_ref[...], right_ref[...]).astype(jnp.bfloat16)


def rows_grad(left, right):
    count, high = left.shape
    wide = right.shape[1]
    return pl.pallas_call(
        rows_grad_kernel,
        grid=(high // 256,),
        in_specs=[
            pl.BlockSpec((count, 256), lambda m: (0, m)),
            pl.BlockSpec((count, wide), lambda m: (0, 0)),
        ],
        out_specs=pl.BlockSpec((256, wide), lambda m: (m, 0)),
        out_shape=jax.ShapeDtypeStruct((high, wide), jnp.bfloat16),
        compiler_params=kernel_params(),
        cost_estimate=cost(2 * count * high * wide, 2 * (count * (high + wide) + high * wide)),
        name="rows_grad",
    )(left, right)


def combine_kernel(scaled, pieces, arrivals, added, unit_ref, info_ref, act_ref, weight_ref, *rest):
    rows_refs, rest = rest[:pieces], rest[pieces:]
    arrived_refs, rest = rest[:arrivals], rest[arrivals:]
    added_refs, out_refs = rest[:added], rest[added:]
    slot = info_ref[0, :, 0:1]
    capacity = rows_refs[0].shape[1]
    lanes = lax.broadcasted_iota(jnp.int32, (slot.shape[0], capacity), 1).astype(jnp.float32)
    pick = jnp.where(slot == lanes, 1.0, 0.0).astype(jnp.bfloat16)

    def store(way):
        total = dot32(pick, rows_refs[way % pieces][0])
        if scaled:
            total = total * info_ref[0, :, 1:2]
        total = total + dot32(act_ref[0], weight_ref[...])
        for added_ref in added_refs:
            total = total + added_ref[0].astype(jnp.float32)
        if arrivals:
            total = total + arrived_refs[way][0].astype(jnp.float32)
        out_ref = out_refs[way % len(out_refs)]
        out_ref[0] = total.astype(out_ref.dtype)

    if pieces == 1 and not arrivals and len(out_refs) == 1:
        store(0)
        return
    for way in range(2):

        @pl.when(pl.program_id(0) % 2 == way)
        def _(way=way):
            store(way)


def combine(
    units, info, rows, act, weight, scaled, arrived=(), partner=(), own=(), kind="units",
    out_dtype=jnp.bfloat16,
):
    units, first, count = units
    tokens = info.shape[1]
    width, hidden = weight.shape[1], act.shape[2]
    capacity = rows[0].shape[1]
    columns = width // 2
    unit_block = lambda array: pl.BlockSpec((1,) + array.shape[1:], lambda i, u: (u[first + i], 0, 0))
    fixed = pl.BlockSpec((1, tokens, columns), lambda i, u: (0, 0, 0))
    half = pl.BlockSpec((1, tokens, columns), lambda i, u: (0, 0, i % 2))
    in_specs = [
        unit_block(info),
        unit_block(act),
        pl.BlockSpec((hidden, columns), lambda i, u: (0, i % 2)),
    ]
    block = (1, capacity, columns)
    if len(rows) == 1:
        in_specs.append(pl.BlockSpec(block, lambda i, u: (u[first + i], 0, i % 2)))
    else:
        in_specs.append(pl.BlockSpec(block, lambda i, u: (u[first + i - i % 2], 0, 0)))
        in_specs.append(pl.BlockSpec(block, lambda i, u: (u[first + i - i % 2 + 1], 0, 0)))
    in_specs += [fixed] * len(arrived)
    added = [array for array, _ in partner] + list(own)
    for _, at in partner:
        in_specs.append(pl.BlockSpec((1, tokens, columns), lambda i, u, at=at: (at + i, 0, 0)))
    in_specs += [half] * len(own)
    out_specs, out_shape = {
        "units": (
            [pl.BlockSpec((1, tokens, columns), lambda i, u: (i, 0, 0))],
            [(count, tokens, columns)],
        ),
        "ways": ([fixed, fixed], [(1, tokens, columns)] * 2),
        "tokens": ([half], [(1, tokens, width)]),
    }[kind]
    return pl.pallas_call(
        functools.partial(combine_kernel, scaled, len(rows), len(arrived), len(added)),
        grid_spec=pltpu.PrefetchScalarGridSpec(
            num_scalar_prefetch=1, grid=(count,), in_specs=in_specs, out_specs=out_specs
        ),
        out_shape=[jax.ShapeDtypeStruct(shape, out_dtype) for shape in out_shape],
        compiler_params=kernel_params(COMBINE_VMEM),
        cost_estimate=cost(
            2 * count * tokens * columns * (capacity + hidden),
            2 * count * columns * (capacity + tokens * (1 + len(added) + len(arrived) // 2)),
        ),
        name="combine",
    )(units, info, act, weight, *rows, *arrived, *added)


def weight_grad_kernel(part_ref, left_ref, right_ref, *rest):
    *arrived_refs, out_ref, sum_ref = rest
    step = pl.program_id(0)
    last = pl.num_programs(0) - 1

    @pl.when(step == 0)
    def _():
        for chunk in row_chunks(sum_ref.shape[0]):
            sum_ref[chunk, :] = t_dot(left_ref[:, chunk], right_ref[...])

    @pl.when((step > 0) & (step < last))
    def _():
        for chunk in row_chunks(sum_ref.shape[0]):
            sum_ref[chunk, :] += t_dot(left_ref[:, chunk], right_ref[...])

    @pl.when((step > 0) & (step == last))
    def _():
        for chunk in row_chunks(sum_ref.shape[0]):
            total = sum_ref[chunk, :] + t_dot(left_ref[:, chunk], right_ref[...])
            for arrived_ref in arrived_refs:
                total = total + arrived_ref[chunk, :].astype(jnp.float32)
            out_ref[chunk, :] = total.astype(out_ref.dtype)


def weight_grad(left, right, axis, part, out_dtype, arrived=()):
    count = left.shape[0]
    high = min(count // 2, 1024)
    widths = [left.shape[1], right.shape[1]]
    widths[axis] //= 2
    at = (lambda k, p: (k, p[0]), lambda k, p: (k, 0))
    whole = pl.BlockSpec(tuple(widths), lambda k, p: (0, 0))
    return pl.pallas_call(
        weight_grad_kernel,
        grid_spec=pltpu.PrefetchScalarGridSpec(
            num_scalar_prefetch=1,
            grid=(count // high,),
            in_specs=[
                pl.BlockSpec((high, widths[0]), at[axis]),
                pl.BlockSpec((high, widths[1]), at[1 - axis]),
            ]
            + [whole] * len(arrived),
            out_specs=whole,
            scratch_shapes=[pltpu.VMEM(tuple(widths), jnp.float32)],
        ),
        out_shape=jax.ShapeDtypeStruct(tuple(widths), out_dtype),
        compiler_params=kernel_params(),
        cost_estimate=cost(
            2 * count * widths[0] * widths[1], 2 * count * sum(widths) + 4 * widths[0] * widths[1]
        ),
        name="weight_grad",
    )(part, left, right, *arrived)


def exp_ring(chips):
    if chips % 2:
        return list(range(chips))
    return list(range(0, chips, 2)) + list(range(chips - 1, 0, -2))


class ChipRing:
    def __init__(self):
        exp_count = lax.axis_size("exp")
        self.chips = exp_count // 2
        ring = exp_ring(self.chips)
        place_of = np.argsort(np.array(ring)).astype(np.int32)
        index = lax.axis_index("exp")
        self.core = index % 2
        self.place = jnp.asarray(place_of)[index // 2]
        self.ring = np.array(ring, np.int32)
        self.swap = [(i, i ^ 1) for i in range(exp_count)]
        self.ways = ([], [])
        for at in range(self.chips):
            for core in range(2):
                here, there = ring[at] * 2 + core, ring[(at + 1) % self.chips] * 2 + core
                self.ways[0].append((here, there))
                self.ways[1].append((there, here))

    def table(self):
        steps = np.arange(1, self.chips + 1)[None, :, None]
        places = np.arange(self.chips)[:, None, None]
        at = np.concatenate([places - steps, places + steps], axis=2) % self.chips
        return jnp.asarray(self.ring[at].reshape(self.chips, -1), jnp.int32)[self.place]

    def move(self, totals):
        return [lax.ppermute(total, "exp", way) for total, way in zip(totals, self.ways)]

    def swap_cores(self, value):
        return lax.ppermute(value, "exp", self.swap)


class ExpRing:
    def __init__(self, part, out_dtype, own=(), late_from=(4,)):
        self.part, self.out_dtype, self.own = part, out_dtype, own
        self.line = ChipRing()
        self.arrived, self.step = (), 0
        self.swapped, self.partner = [], []
        self.late_from = list(late_from) + [self.line.chips + 1]
        chips = self.line.table() * 2
        self.own_units, other = chips + self.line.core, chips + 1 - self.line.core
        first = part((other, 0, 2))[0]
        first, other = tie(first, other)
        self.take(first)
        second = part((other, 2, 2 * (self.late_from[0] - 2)))[0]
        second, self.late_units = tie(second, other)
        second, self.swapped[0] = tie(second, self.swapped[0])
        self.take(second)

    def take(self, total):
        self.partner += [(len(self.swapped), 2 * i) for i in range(total.shape[0] // 2)]
        self.swapped.append(self.line.swap_cores(total))

    def from_partner(self, step):
        group, at = self.partner[step - 1]
        return ((self.swapped[group], at),)

    def late(self, which, units):
        start, end = self.late_from[which : which + 2]
        return self.part((units, 2 * (start - 1), 2 * (end - start)))[0]

    def totals(self):
        self.step += 1
        return self.part(
            (self.own_units, 2 * (self.step - 1), 2),
            arrived=self.arrived,
            partner=self.from_partner(self.step),
            kind="ways",
        )

    def finish(self):
        return self.part(
            (self.own_units, 2 * (self.line.chips - 1), 2),
            arrived=self.arrived,
            partner=self.from_partner(self.line.chips),
            own=self.own,
            kind="tokens",
            out_dtype=self.out_dtype,
        )[0][0]


def ring_step(rings, work, *operands, also=()):
    totals = [ring.totals() for ring in rings]
    totals, operands = tie(totals, operands)
    moved = [ring.line.move(total) for ring, total in zip(rings, totals)]
    swapped = [ring.swapped for ring in rings]
    moved, swapped, result, also = tie(moved, swapped, work(*operands), also)
    for ring, arrived, ring.swapped in zip(rings, moved, swapped):
        ring.arrived = tuple(arrived)
    return (result, *also) if also else result


def ctx_fetch(part, axis):
    if lax.axis_size("ctx") != 2:
        return lax.all_gather(part, "ctx", axis=axis, tiled=True)
    return lax.ppermute(part, "ctx", [(0, 1), (1, 0)])


def ctx_half(array, mine):
    half = array.shape[1] // 2
    index = lax.axis_index("ctx")
    return lax.dynamic_slice_in_dim(array, (index if mine else 1 - index) * half, half, axis=1)


def ctx_join(part, other, axis):
    if lax.axis_size("ctx") != 2:
        return other
    return lax.dynamic_update_slice_in_dim(
        jnp.concatenate([other, other], axis=axis),
        part,
        lax.axis_index("ctx") * part.shape[axis],
        axis,
    )


def ctx_gather(part, axis):
    return ctx_join(part, ctx_fetch(part, axis), axis)


def ctx_pair_part(which):
    return jnp.full((1,), which, jnp.int32)


def ctx_theirs(left, right, axis):
    if lax.axis_size("ctx") == 2:
        part = ctx_pair_part(1 - lax.axis_index("ctx"))
        return weight_grad(left, right, axis, part, jnp.bfloat16)
    return t_dot(left, right).astype(jnp.bfloat16)


def ctx_send(theirs, axis):
    if lax.axis_size("ctx") == 2:
        return lax.ppermute(theirs, "ctx", [(0, 1), (1, 0)])
    return lax.psum_scatter(theirs, "ctx", scatter_dimension=axis, tiled=True)


def ctx_total(left, right, axis, arrived):
    if lax.axis_size("ctx") == 2:
        part = ctx_pair_part(lax.axis_index("ctx"))
        return weight_grad(left, right, axis, part, jnp.float32, (arrived,))
    return arrived.astype(jnp.float32)


def on_device(
    block_input,
    attn_gain,
    query_weight,
    key_matrix,
    value_matrix,
    output_weight,
    ffn_gain,
    shared_gate,
    shared_up,
    shared_down,
    expert_gate,
    expert_up,
    expert_down,
    routes,
    route_weights,
    cotangent,
):
    input_rows = block_input[0].astype(jnp.float32)
    tokens = input_rows.shape[0]
    ctx_count = lax.axis_size("ctx")
    exp_count = lax.axis_size("exp")
    exp_index = lax.axis_index("exp")
    both = ("ctx", "exp")
    offset = lax.axis_index("ctx") * tokens
    offset_array = jnp.full((1,), offset, jnp.int32)
    tables = rope_tables(offset + jnp.arange(tokens, dtype=jnp.int32))
    key_tables = rope_tables(jnp.arange(ctx_count * tokens, dtype=jnp.int32))

    own_rows = shared_gate.shape[0]
    attn_in = jnp.concatenate([query_weight, key_matrix, value_matrix], axis=1)
    edge = attn_in.shape[1]
    own_weights = route_weights[0].T
    (weights_high,) = tie(own_weights.astype(jnp.bfloat16))
    weights_low = (own_weights - weights_high.astype(jnp.float32)).astype(jnp.bfloat16)
    routing = jnp.concatenate(
        [routes[0].T.astype(jnp.bfloat16), weights_high, weights_low], axis=0
    ).reshape(-1)
    routing_columns = -(-routing.shape[0] // (own_rows * 128)) * 128
    routing = jnp.pad(routing, (0, own_rows * routing_columns - routing.shape[0]))
    full_in = lax.all_gather(
        jnp.concatenate([attn_in, routing.reshape(own_rows, routing_columns)], axis=1),
        both,
        axis=0,
        tiled=True,
    )
    routing = lax.dynamic_slice(
        full_in,
        (lax.axis_index("ctx") * exp_count * own_rows, edge),
        (exp_count * own_rows, routing_columns),
    ).reshape(exp_count, own_rows * routing_columns)
    routing = routing[:, : 3 * TOP * tokens].reshape(exp_count, 3 * TOP, tokens)
    routing = routing.astype(jnp.float32)
    grad_low = cotangent[0]

    own_hidden = shared_down.shape[0]
    padded = -(-ctx_count * own_hidden // 256) * 256
    padded_own = padded // ctx_count
    shared_in = jnp.stack([shared_gate, shared_up]).reshape(
        2, own_rows, ctx_count, exp_count, own_hidden
    )
    shared_in = jnp.transpose(shared_in, (3, 1, 0, 2, 4)).reshape(
        exp_count, own_rows, 2 * ctx_count * own_hidden
    )
    shared_in = lax.all_to_all(shared_in, "exp", split_axis=0, concat_axis=0, tiled=True)
    shared_in = jnp.pad(
        shared_in.reshape(exp_count * own_rows, 2 * ctx_count, own_hidden),
        ((0, 0), (0, 0), (0, padded_own - own_hidden)),
    ).reshape(exp_count * own_rows, 2 * padded)
    shared_in = ctx_gather(shared_in, 0)
    shared_in_t = shared_in.T
    shared_out_w = ctx_gather(jnp.pad(shared_down, ((0, padded_own - own_hidden), (0, 0))), 0)

    capacity = tokens * TOP * 4 // (3 * exp_count)
    named = routing[:, :TOP] == exp_index.astype(jnp.float32)
    chosen = jnp.any(named, axis=1)
    token_weight = jnp.sum(
        jnp.where(named, routing[:, TOP : 2 * TOP] + routing[:, 2 * TOP :], 0.0), axis=1
    )
    upto = (jnp.arange(tokens)[:, None] <= jnp.arange(tokens)[None, :]).astype(jnp.bfloat16)
    slot = dot32(chosen.astype(jnp.bfloat16), upto).astype(jnp.int32) - 1
    slot = jnp.where(chosen, slot, -1)
    slot_rows = jnp.stack([slot.astype(jnp.float32), token_weight], axis=1)
    token_info = jnp.pad(
        jnp.stack([slot.astype(jnp.float32), token_weight], axis=2), ((0, 0), (0, 0), (0, 126))
    )

    inverse_one = rms_scale(input_rows)
    normed_one = (input_rows * inverse_one * attn_gain).astype(jnp.bfloat16)
    full_in, normed_one, shared_in_t, shared_out_w = tie(
        full_in, normed_one, shared_in_t, shared_out_w
    )
    output_weight, full_in = tie(output_weight, full_in)
    full_output = lax.all_gather(output_weight, both, axis=0, tiled=True)
    key_value = ctx_gather(
        project(normed_one, full_in, tables, QUERY_HEADS // KEY_VALUE_HEADS, 2, 1), 0
    )
    query = project(normed_one, full_in, tables, 0, QUERY_HEADS // KEY_VALUE_HEADS, QUERY_HEADS)
    attended_low = attend(offset_array, query, key_value)

    full_output, gate_part, up_part, down_part = tie(
        full_output, expert_gate[0], expert_up[0], expert_down[0]
    )
    gate_w = ctx_gather(gate_part, 0)
    up_w = ctx_gather(up_part, 0)
    down_other = ctx_fetch(down_part, 1)

    middle = input_rows + dot32(attended_low, full_output)
    inverse_two = rms_scale(middle)
    normed_two = (middle * inverse_two * ffn_gain).astype(jnp.bfloat16)

    rows_all = lax.all_gather(normed_two, "exp", axis=0, tiled=True)
    rows_all, gate_w, up_w, grad_sent, slot_rows, token_info = tie(
        rows_all, gate_w, up_w, grad_low, slot_rows, token_info
    )
    grad_all = lax.all_gather(grad_sent, "exp", axis=0, tiled=True)

    def blocks(rows):
        return rows.reshape(exp_count, tokens, MODEL_WIDTH)

    def flat(rows):
        return rows.reshape(rows.shape[0] * rows.shape[1], rows.shape[2])

    received, shared_act, shared_slope = enter(slot_rows, blocks(rows_all), shared_in_t, capacity)
    received = flat(received)
    expert_act, expert_slope, expert_silu = expert_in(received, gate_w, up_w)
    expert_act, down_other = tie(expert_act, down_other)
    if ctx_count == 2:
        down_parts = lax.axis_index("ctx") ^ jnp.arange(2, dtype=jnp.int32)
    else:
        down_parts = jnp.arange(2, dtype=jnp.int32)
        down_part = down_other[:, : MODEL_WIDTH // 2]
        down_other = down_other[:, MODEL_WIDTH // 2 :]
    expert_rows = expert_out(down_parts, expert_act, down_part, down_other)

    def slots(rows):
        return rows.reshape(exp_count, capacity, rows.shape[1])

    pair = exp_count >= 4 and exp_count % 4 == 0 and ctx_count == 2

    def sum_over_exp(part):
        units = jnp.repeat(jnp.arange(exp_count, dtype=jnp.int32), 2)
        everything = part((units, 0, 2 * exp_count))[0].reshape(exp_count, 2, tokens, MODEL_WIDTH // 2)
        return lax.psum_scatter(
            jnp.swapaxes(everything, 1, 2).reshape(exp_count * tokens, MODEL_WIDTH),
            "exp",
            scatter_dimension=0,
            tiled=True,
        ).astype(jnp.float32)

    out_part = functools.partial(
        combine,
        info=token_info,
        rows=(slots(expert_rows),),
        act=shared_act,
        weight=shared_out_w,
        scaled=True,
    )
    shared_act = flat(shared_act)
    rings = []
    if pair:
        out_ring = ExpRing(out_part, jnp.bfloat16, (middle[None],), late_from=(9,))
        rings = [out_ring]
    grad_expert, shared_back = ring_step(
        rings,
        lambda *operands: enter_back(*operands, capacity),
        slot_rows,
        blocks(grad_all),
        shared_out_w,
        shared_slope,
    )
    grad_expert = flat(grad_expert)
    grad_eu = ()
    early = ()
    if pair:
        early = (ctx_send(ctx_half(normed_one, False), 0), ctx_send(attended_low, 0))
    for half in range(2):
        grad_eu = ring_step(
            rings,
            lambda *operands: expert_back(*operands[:6], half, operands[6:]),
            down_parts,
            grad_expert,
            down_part,
            down_other,
            expert_slope,
            expert_silu,
            *grad_eu,
            also=early if half == 0 else (),
        )
        if pair and half == 0:
            grad_eu, normed_other, attended_other = grad_eu
    grad_eg, grad_eu = grad_eu
    pieces = [(), ()]
    theirs = lambda axis: lambda left, right: ctx_theirs(left, right, axis)
    total = lambda axis: lambda left, right, arrived: ctx_total(left, right, axis, arrived)
    for column_half, half in ((0, 0), (0, 1), (1, 0), (1, 1)):
        if (column_half, half) == (1, 1):
            down_theirs = ring_step(rings, theirs(1), expert_act, grad_expert)
            down_theirs, grad_eg, grad_eu = tie(down_theirs, grad_eg, grad_eu)
            down_arrived = ctx_send(down_theirs, 1)
            rings = []
        piece = ring_step(
            rings,
            lambda *operands: expert_grad_rows(*operands[:4], column_half, half, operands[4:]),
            grad_eg,
            grad_eu,
            gate_w,
            up_w,
            *pieces[column_half],
        )
        pieces[column_half] = (piece,)
    grad_rows = [slots(piece) for (piece,) in pieces]

    grad_part = functools.partial(
        combine,
        info=token_info,
        rows=tuple(grad_rows),
        act=shared_back,
        weight=shared_in_t,
        scaled=False,
    )
    shared_back = flat(shared_back)
    if pair:
        output = out_ring.finish()
        grad_ring = ExpRing(grad_part, jnp.float32, late_from=(9,))
        rings = [grad_ring]
    else:
        output = (middle + sum_over_exp(out_part)).astype(jnp.bfloat16)

    def theirs_and_late(which, *operands):
        if not pair:
            return ring_step(rings, theirs(0), *operands)
        return ring_step(rings, theirs(0), *operands)

    gate_theirs = theirs_and_late(0, received, grad_eg)
    gate_arrived = ctx_send(gate_theirs, 0)
    up_theirs = theirs_and_late(1, received, grad_eu)
    up_arrived = ctx_send(up_theirs, 0)
    shared_in_theirs, shared_down_theirs = ring_step(
        rings,
        lambda a, b, c, d: (ctx_theirs(a, b, 0), ctx_theirs(c, d, 0)),
        rows_all,
        shared_back,
        shared_act,
        grad_all,
    )
    shared_in_arrived = ctx_send(shared_in_theirs, 0)
    shared_down_arrived = ctx_send(shared_down_theirs, 0)
    expert_down_grad = ring_step(rings, total(1), expert_act, grad_expert, down_arrived)[None]
    expert_gate_grad = ring_step(rings, total(0), received, grad_eg, gate_arrived)[None]
    if pair:
        ring_step(rings, lambda: ())
    expert_up_grad = ring_step(rings, total(0), received, grad_eu, up_arrived)[None]
    if pair:
        grad_two = grad_ring.finish()
        grad_two, shared_in_arrived, shared_down_arrived = tie(
            grad_two, shared_in_arrived, shared_down_arrived
        )
    else:
        grad_two = sum_over_exp(grad_part)
    ffn_gain_term = jnp.sum(grad_two * middle * inverse_two, axis=0)
    grad_middle = grad_low.astype(jnp.float32) + norm_back(grad_two, middle, inverse_two, ffn_gain)
    grad_middle_low = grad_middle.astype(jnp.bfloat16)
    attended_gradient = dot_t(grad_middle_low, full_output).astype(jnp.bfloat16)
    if pair:
        middle_other = ctx_send(ctx_half(grad_middle_low, False), 0)
        gain_half = ffn_gain_term.reshape(2, -1)
        gain_other = ctx_send(lax.dynamic_index_in_dim(gain_half, 1 - lax.axis_index("ctx"), 0), 0)
        gain_half = lax.dynamic_index_in_dim(gain_half, lax.axis_index("ctx"), 0)
        attended_gradient, gain_other = tie(attended_gradient, gain_other)
        gain_term = (gain_half + gain_other).T
    else:
        gain_term = ffn_gain_term[:, None]
    gain_term = jnp.pad(gain_term, ((0, 0), (0, 127))).astype(jnp.bfloat16)

    shared_in_grad = ctx_total(rows_all, shared_back, 0, shared_in_arrived)
    sum_sd = ctx_total(shared_act, grad_all, 0, shared_down_arrived)
    grad_query_raw, key_terms, value_terms = attend_back(
        offset_array, query, key_value, attended_gradient, tables, key_tables
    )
    key_value_grad = jnp.concatenate([key_terms, value_terms], axis=1)
    if pair:
        grad_query_raw, key_value_grad, middle_other = tie(
            grad_query_raw, key_value_grad, middle_other
        )
        key_value_other = ctx_send(key_value_grad.astype(jnp.bfloat16), 0)
        query_other = ctx_send(grad_query_raw, 0)
        output_term = rows_grad(
            jnp.concatenate([ctx_half(grad_middle_low, True), middle_other], axis=0),
            jnp.concatenate([attended_low, attended_other], axis=0),
        )
        sum_o = lax.psum_scatter(output_term, "exp", scatter_dimension=0, tiled=True)
        query_other, shared_in_grad, sum_sd = tie(query_other, shared_in_grad, sum_sd)
        key_value_all = (key_value_grad + key_value_other.astype(jnp.float32)).astype(jnp.bfloat16)
        key_value_raw = lax.dynamic_slice_in_dim(key_value_all, offset, tokens, axis=0)
        key_value_both = jnp.concatenate(
            [
                key_value_raw,
                lax.dynamic_slice_in_dim(key_value_all, tokens - offset, tokens, axis=0),
            ],
            axis=0,
        )
        in_term = qkv_grad(
            jnp.concatenate([ctx_half(normed_one, True), normed_other], axis=0).T,
            jnp.concatenate([grad_query_raw, query_other], axis=0),
            key_value_both,
            gain_term,
        )
        sum_in = lax.psum_scatter(in_term, "exp", scatter_dimension=0, tiled=True)
    else:
        key_value_raw = ctx_send(key_value_grad.astype(jnp.bfloat16), 0)
        in_term = qkv_grad(normed_one.T, grad_query_raw, key_value_raw, gain_term)
        sum_in = lax.psum_scatter(in_term, both, scatter_dimension=0, tiled=True)
        output_term = rows_grad(grad_middle_low, attended_low)
        sum_o = lax.psum_scatter(output_term, both, scatter_dimension=0, tiled=True)
    sum_in = sum_in.astype(jnp.float32)
    grad_raw = jnp.concatenate(
        [grad_query_raw, key_value_raw, jnp.zeros((tokens, routing_columns), jnp.bfloat16)], axis=1
    )
    grad_one = dot_t(grad_raw, full_in)
    input_grad = grad_middle + norm_back(grad_one, input_rows, inverse_one, attn_gain)
    own_gain = lax.dynamic_slice_in_dim(
        attn_gain, (lax.axis_index("ctx") * exp_count + exp_index) * own_rows, own_rows
    )
    attn_gain_grad = jnp.sum(sum_in[:, :edge] * attn_in.astype(jnp.float32), axis=1) / own_gain

    shared_in_grad = shared_in_grad.astype(jnp.bfloat16)
    sum_sd = sum_sd[:own_hidden]
    shared_in_grad = lax.all_to_all(
        shared_in_grad.reshape(exp_count, own_rows, 2 * padded),
        "exp",
        split_axis=0,
        concat_axis=0,
        tiled=True,
    ).reshape(exp_count, own_rows, 2, ctx_count, padded_own)[..., :own_hidden]
    shared_in_grad = (
        jnp.transpose(shared_in_grad, (2, 1, 3, 0, 4))
        .reshape(2, own_rows, exp_count * ctx_count * own_hidden)
        .astype(jnp.float32)
    )
    return (
        output[None],
        input_grad[None],
        attn_gain_grad,
        sum_in[:, :QUERY_WIDTH],
        sum_in[:, QUERY_WIDTH : QUERY_WIDTH + KEY_WIDTH],
        sum_in[:, QUERY_WIDTH + KEY_WIDTH : edge],
        sum_o.astype(jnp.float32).T,
        sum_in[:, edge],
        shared_in_grad[0],
        shared_in_grad[1],
        sum_sd,
        expert_gate_grad,
        expert_up_grad,
        expert_down_grad,
    )


def solution(mesh):
    return jax.shard_map(
        on_device,
        mesh=mesh,
        in_specs=(
            P("exp", "ctx", None),
            P(),
            P(("ctx", "exp"), None),
            P(("ctx", "exp"), None),
            P(("ctx", "exp"), None),
            P(("ctx", "exp"), None),
            P(),
            P(("ctx", "exp"), None),
            P(("ctx", "exp"), None),
            P(("ctx", "exp"), None),
            P("exp", "ctx", None),
            P("exp", "ctx", None),
            P("exp", None, "ctx"),
            P("exp", "ctx", None),
            P("exp", "ctx", None),
            P("exp", "ctx", None),
        ),
        out_specs=(
            P("exp", "ctx", None),
            P("exp", "ctx", None),
            P(("ctx", "exp")),
            P(("ctx", "exp"), None),
            P(("ctx", "exp"), None),
            P(("ctx", "exp"), None),
            P(None, ("ctx", "exp")),
            P(("ctx", "exp")),
            P(("ctx", "exp"), None),
            P(("ctx", "exp"), None),
            P(("ctx", "exp"), None),
            P("exp", "ctx", None),
            P("exp", "ctx", None),
            P("exp", None, "ctx"),
        ),
        check_vma=False,
    )
```
